32 devices in a mesh: wide: 16 (over z, x, core), narrow: 2 (over y).
Axes of the slice: x: 2, y: 2, z: 4, core: 2. Of those that a mesh axis runs over, the one named last changes fastest.
Arguments:
- raw_ints: float32 [32, 512, 768], P('wide', 'narrow'), may hold values from -1.2 to 1.2
- metric: float32 [768, 768], P('narrow'), may hold values from -0.21875 to 0.21875
- occ_energy: float32 [32], P(('wide', 'narrow')), may hold values from -1.5 to -0.3
- vir_energy: float32 [512], replicated, may hold values from 0.3 to 3
- pair_kept: int32 [32], P(('wide', 'narrow')), may hold values 0 or 1
Outputs:
- density: float32 [512, 512], P('narrow')
- energy: float32 [32], P(('wide', 'narrow'))
The draws below stay inside these ranges and needn't reach their ends.
All inputs are finite; a program needn't handle non-finite values. No bound on the sum of `pair_kept` on one device may be relied on, other than what follows from the above.
Results may differ from the reference program's by a relative error of at most 0.0003.
Values sent between devices are 32-bit elements; how exact they have to be, the bound alone decides.
No kernel may reach another device: no remote copies, remote signals or barrier semaphores. Data moves between devices by JAX's collectives and lax.ppermute only.
A program may use at most 64 MiB of HBM per device.

```python
import jax
import jax.numpy as jnp
from jax import lax

NAUX = 768
VIR = 512
OCC = 32
N_NARROW = 2


def set_ends(array, rng, least, largest):
    longest = array.shape.index(max(array.shape))
    spots = []
    for shift in (0, 1):
        where = [jax.random.randint(jax.random.fold_in(rng, axis), (), 0, length) for axis, length in enumerate(array.shape)]
        where[longest] = (where[longest] + shift) % array.shape[longest]
        spots.append(tuple(where))
    return array.at[spots[0]].set(least).at[spots[1]].set(largest)


def levels(rng, shape, shards, smallest, top_value):
    def one(position, shards_of):
        draws = jax.random.uniform(jax.random.fold_in(jax.random.fold_in(rng, 6), position), (shards_of,), jnp.float32, smallest / len(shards), top_value / len(shards))
        return jnp.repeat(jnp.exp(draws), shape[position] // shards_of).reshape((-1,) + (1,) * (len(shape) - position - 1))

    level = one(*shards[0])
    for cut in shards[1:]:
        level = level * one(*cut)
    return level


def centred(key, dims, spread, reach, pieces=(), held_as=jnp.bfloat16):
    factor_of = levels(key, dims, pieces, -0.22, 0.18) if pieces else 1.0
    drawn = jax.random.normal(key, dims, jnp.float32) * spread * factor_of
    return jnp.minimum(jnp.maximum(drawn, -reach), reach).astype(held_as)


def setup_inputs(seed: int = 0) -> dict:
    splits = jax.random.split(jax.random.key(seed), 6)
    raw_ints = centred(splits[0], (OCC, VIR, NAUX), 0.2, 1.2, ((0, 16), (1, 2)), jnp.float32)
    metric = centred(splits[1], (NAUX, NAUX), NAUX ** -0.5, 0.21875, ((0, 2),), jnp.float32)
    occ_energy = jnp.clip(-1.5 + 1.2 * jax.random.uniform(splits[2], (OCC,), jnp.float32) ** levels(splits[2], (OCC,), ((0, 32),), -0.2, 0.2), -1.5, -0.3)
    vir_energy = jnp.clip(jax.random.uniform(splits[3], (VIR,), jnp.float32, 0.3, 3.0), 0.3, 3.0)
    pair_kept = set_ends((jax.random.randint(splits[4], (OCC,), 0, 4) < 3).astype(jnp.int32), jax.random.fold_in(splits[4], 1), 0, 1)
    return {"raw_ints": raw_ints, "metric": metric, "occ_energy": occ_energy, "vir_energy": vir_energy, "pair_kept": pair_kept}


HIGHEST_PRECISION = lax.Precision.HIGHEST


def pair_pass(left_block, right_block, vir_energy, left_energy, right_energy):
    pair_ints = lax.dot_general(left_block, right_block, (((1,), (1,)), ((), ())), precision=HIGHEST_PRECISION, preferred_element_type=jnp.float32)
    denominator = (vir_energy[:, None] + vir_energy[None, :]) - left_energy - right_energy
    amplitude = pair_ints / denominator
    pair_value = -jnp.sum(pair_ints * (2.0 * amplitude - amplitude.T)) / (pair_ints.shape[0] * pair_ints.shape[1])
    return amplitude, pair_value


def reference(raw_ints, metric, occ_energy, vir_energy, pair_kept):
    fitted = jnp.einsum("iap,qp->iaq", raw_ints, metric, precision=HIGHEST_PRECISION)
    kept_mask = pair_kept.astype(jnp.float32)
    orbitals = fitted.shape[0]

    def accumulate(density, orbital):
        partner = ((orbital - N_NARROW) % orbitals).astype(jnp.int32)
        amplitude, pair_value = pair_pass(fitted[orbital], fitted[partner], vir_energy, occ_energy[orbital], occ_energy[partner])
        pair_term = lax.dot_general(amplitude, amplitude, (((1,), (1,)), ((), ())), precision=HIGHEST_PRECISION, preferred_element_type=jnp.float32)
        pair_term = pair_term + lax.dot_general(amplitude, amplitude, (((0,), (0,)), ((), ())), precision=HIGHEST_PRECISION, preferred_element_type=jnp.float32)
        return density + kept_mask[orbital] * pair_term, kept_mask[orbital] * pair_value

    density, pair_values = lax.scan(accumulate, jnp.zeros((VIR, VIR), jnp.float32), jnp.arange(orbitals, dtype=jnp.int32))
    energy = pair_values + jnp.roll(pair_values, -N_NARROW)
    return density * (0.0625 / orbitals), energy
```

```python
import jax
import jax.numpy as jnp
from jax import lax
from jax.sharding import PartitionSpec as P

PASSES = lax.Precision.HIGH


def contract(left, right, left_dim, right_dim):
    return lax.dot_general(
        left,
        right,
        (((left_dim,), (right_dim,)), ((), ())),
        precision=PASSES,
        preferred_element_type=jnp.float32,
    )


def passed_along(shard, axis, by):
    size = lax.axis_size(axis)
    return lax.ppermute(shard, axis, [(i, (i + by) % size) for i in range(size)])


def swapped(shard, axis, bit):
    size = lax.axis_size(axis)
    return lax.ppermute(shard, axis, [(i, i ^ bit) for i in range(size)])


def whole_metric(metric, wide, narrow, w):
    share = 4 if wide % 4 == 0 else 1
    rows = metric.shape[0] // share
    piece = lax.dynamic_slice_in_dim(metric, (w % share) * rows, rows, 0)
    pieces = [passed_along(piece, "narrow", s) for s in range(1, narrow)]
    far = pieces[0] if narrow == 2 else jnp.concatenate(pieces, 0)
    if share == 4:
        far = jnp.concatenate([far, swapped(far, "wide", 2)], 0)
        far = jnp.concatenate([far, swapped(far, "wide", 1)], 0)
    return jnp.concatenate([metric, far], 0)


def in_order(blocks, n):
    count = len(blocks)
    return jnp.concatenate(
        [lax.select_n(n, *[blocks[(m - b) % count] for m in range(count)]) for b in range(count)], 0
    )


def summed_rows(blocks, table, wide, narrow, w, n):
    pairs, v, _ = blocks.shape
    half, group = v // 2, wide // 2
    rows = half // group
    core = w % 2
    kept = lax.dynamic_slice_in_dim(blocks, core * half, half, 1)
    given = lax.dynamic_slice_in_dim(blocks, (1 - core) * half, half, 1)
    mine = kept + swapped(given, "wide", 1)
    groups = [[2 * k + c for k in range(group)] for c in range(2)]
    mine = mine.reshape(pairs, group, rows, v).transpose(1, 0, 2, 3)
    mine = lax.all_to_all(mine, "wide", 0, 0, axis_index_groups=groups).sum(0)
    total = mine[table[n]]
    for s in range(1, narrow):
        total = total + passed_along(mine[table[(n + s) % narrow]], "narrow", s)
    spread = jnp.broadcast_to(total[None], (group,) + total.shape)
    spread = lax.all_to_all(spread, "wide", 0, 0, axis_index_groups=groups)
    spread = spread.transpose(1, 0, 2, 3).reshape(narrow, half, v)
    other = swapped(spread, "wide", 1)
    first = jnp.where(core == 0, spread, other)
    second = jnp.where(core == 0, other, spread)
    full = jnp.concatenate([first, second], 1)
    return jnp.concatenate(
        [jnp.where(m < n, full[m].T, full[m]) for m in range(narrow)], 1
    )


def on_device(raw_ints, metric, occ_energy, vir_energy, pair_kept):
    wide, narrow = lax.axis_size("wide"), lax.axis_size("narrow")
    w, n = lax.axis_index("wide"), lax.axis_index("narrow")
    v = raw_ints.shape[1]
    virtuals = v * narrow

    lower_energy = passed_along(occ_energy, "wide", 1)
    full_metric = whole_metric(metric, wide, narrow, w)
    raw_own = [lax.dynamic_index_in_dim(raw_ints, n, 0, keepdims=False)]
    raw_low = [passed_along(raw_own[0], "wide", 1)]
    for s in range(1, narrow):
        given = lax.dynamic_index_in_dim(raw_ints, (n + s) % narrow, 0, keepdims=False)
        cuts = jnp.split(given, 2, 0)
        arrived = [passed_along(cut, "narrow", s) for cut in cuts]
        raw_own.append(jnp.concatenate(arrived, 0))
        raw_low.append(jnp.concatenate([passed_along(cut, "wide", 1) for cut in arrived], 0))

    turned = [contract(contract(block, full_metric, 1, 1), full_metric, 1, 0) for block in raw_own]
    pair_ints = contract(in_order(turned, n), in_order(raw_low, n), 1, 1)
    denominator = vir_energy[:, None] + vir_energy[None, :] - occ_energy[0] - lower_energy[0]
    amplitude = pair_ints / denominator
    pair_value = -jnp.sum(pair_ints * (2.0 * amplitude - amplitude.T)) / (virtuals * virtuals)
    kept = pair_kept.astype(jnp.float32)
    own_value = kept * pair_value
    energy = own_value + passed_along(own_value, "wide", -1)

    scale = kept[0] * (0.0625 / (wide * narrow))
    scaled = amplitude * scale
    blocks = []
    for p in range(narrow):
        at = p * v
        row = contract(scaled[at : at + v], amplitude[at:], 1, 1)
        row = row + contract(scaled[:, at : at + v], amplitude[:, at:], 0, 0)
        blocks += jnp.split(row, narrow - p, 1)
    spots = [(p, q) for p in range(narrow) for q in range(p, narrow)]
    table = jnp.array(
        [[spots.index((min(p, q), max(p, q))) for q in range(narrow)] for p in range(narrow)]
    )
    density = summed_rows(jnp.stack(blocks), table, wide, narrow, w, n)
    return density, energy


def solution(mesh):
    placed = (
        P("wide", "narrow", None),
        P("narrow", None),
        P(("wide", "narrow")),
        P(),
        P(("wide", "narrow")),
    )
    return jax.shard_map(
        on_device,
        mesh=mesh,
        in_specs=placed,
        out_specs=(P("narrow", None), P(("wide", "narrow"))),
        check_vma=False,
    )
```

```python
import jax
import jax.numpy as jnp
from jax import lax
from jax.sharding import PartitionSpec as P

PASSES = lax.Precision.HIGH
CHUNKS = 4


def contract(left, right, left_dim, right_dim):
    return lax.dot_general(
        left,
        right,
        (((left_dim,), (right_dim,)), ((), ())),
        precision=PASSES,
        preferred_element_type=jnp.float32,
    )


def passed_along(shard, axis, by):
    size = lax.axis_size(axis)
    return lax.ppermute(shard, axis, [(i, (i + by) % size) for i in range(size)])


def swapped(shard, axis, bit):
    size = lax.axis_size(axis)
    return lax.ppermute(shard, axis, [(i, i ^ bit) for i in range(size)])


def after(value, *gates):
    return lax.optimization_barrier((value,) + gates)[0]


def bits_of(wide):
    return [1 << k for k in range(wide.bit_length() - 1)]


def scattered(blocks, wide, w):
    for bit in bits_of(wide):
        half = blocks.shape[1] // 2
        side = (w // bit) % 2
        kept = lax.dynamic_slice_in_dim(blocks, side * half, half, 1)
        given = lax.dynamic_slice_in_dim(blocks, (1 - side) * half, half, 1)
        blocks = kept + swapped(given, "wide", bit)
    return blocks


def gathered(blocks, wide, w):
    for bit in reversed(bits_of(wide)):
        other = swapped(blocks, "wide", bit)
        low = (w // bit) % 2 == 0
        blocks = jnp.concatenate(
            [jnp.where(low, blocks, other), jnp.where(low, other, blocks)], 1
        )
    return blocks


def on_device(raw_ints, metric, occ_energy, vir_energy, pair_kept):
    wide, narrow = lax.axis_size("wide"), lax.axis_size("narrow")
    w, n = lax.axis_index("wide"), lax.axis_index("narrow")
    v = raw_ints.shape[1]
    virtuals = v * narrow

    share = 4 if wide % 4 == 0 else 1
    count = metric.shape[0] // share
    piece = lax.dynamic_slice_in_dim(metric, (w % share) * count, count, 0)
    far = jnp.concatenate([passed_along(piece, "narrow", s) for s in range(1, narrow)], 0)

    lower_energy = passed_along(occ_energy, "wide", 1)
    own = lax.dynamic_index_in_dim(raw_ints, n, 0, keepdims=False)
    raw_low = [passed_along(own, "wide", 1)]
    arrived = []
    for s in range(1, narrow):
        given = lax.dynamic_index_in_dim(raw_ints, (n + s) % narrow, 0, keepdims=False)
        arrived += [passed_along(cut, "narrow", s) for cut in jnp.split(given, CHUNKS, 0)]

    if share == 4:
        far = jnp.concatenate([far, swapped(far, "wide", 2)], 0)
        raw_low.append(passed_along(arrived[0], "wide", 1))
        raw_low.append(passed_along(after(arrived[1], far), "wide", 1))
        far = jnp.concatenate([far, swapped(far, "wide", 1)], 0)
    full_metric = jnp.concatenate([metric, far], 0)

    def turn(*cuts):
        rows = jnp.concatenate(cuts, 0)
        return contract(contract(rows, full_metric, 1, 1), full_metric, 1, 0)

    turned = [turn(own)]
    for k in range(0, len(arrived), 2):
        for cut in arrived[max(k, len(raw_low) - 1) : k + 2]:
            raw_low.append(passed_along(after(cut, turned[-1]), "wide", 1))
        turned.append(turn(*arrived[k : k + 2]))
    pair_ints = contract(jnp.concatenate(turned, 0), jnp.concatenate(raw_low, 0), 1, 1)

    levels = jnp.concatenate(
        [lax.dynamic_slice_in_dim(vir_energy, ((n - s) % narrow) * v, v, 0) for s in range(narrow)]
    )
    denominator = levels[:, None] + levels[None, :] - occ_energy[0] - lower_energy[0]
    amplitude = pair_ints / denominator
    pair_value = -jnp.sum(pair_ints * (2.0 * amplitude - amplitude.T)) / (virtuals * virtuals)
    kept = pair_kept.astype(jnp.float32)
    own_value = kept * pair_value
    upper_value = passed_along(own_value, "wide", -1)

    scaled = amplitude * (kept[0] * (0.0625 / (wide * narrow)))
    blocks = {}
    for p in range(narrow):
        at = p * v
        row = contract(scaled[at : at + v], amplitude[at:], 1, 1)
        row = row + contract(scaled[:, at : at + v], amplitude[:, at:], 0, 0)
        for q in range(p, narrow):
            block = row[:, (q - p) * v : (q - p + 1) * v]
            turned_round = (n - p) % narrow > (n - q) % narrow
            blocks[p, q] = block if p == q else jnp.where(turned_round, block.T, block)
    spots = {key: k for k, key in enumerate(blocks)}

    def spot(s, t):
        return spots[min(s, t), max(s, t)]

    rows = scattered(jnp.stack(list(blocks.values())), wide, w)
    rows, upper_value = lax.optimization_barrier((rows, upper_value))
    total = jnp.stack([rows[spot(0, t)] for t in range(narrow)])
    for s in range(1, narrow):
        given = jnp.stack([rows[spot(narrow - s, (t - s) % narrow)] for t in range(narrow)])
        total = total + passed_along(given, "narrow", s)
    full = gathered(total, wide, w)
    columns = []
    for b in range(narrow):
        cases = []
        for m in range(narrow):
            block = full[(m - b) % narrow]
            cases.append(block.T if m > b else block)
        columns.append(lax.select_n(n, *cases))
    return jnp.concatenate(columns, 1), own_value + upper_value


def solution(mesh):
    placed = (
        P("wide", "narrow", None),
        P("narrow", None),
        P(("wide", "narrow")),
        P(),
        P(("wide", "narrow")),
    )
    return jax.shard_map(
        on_device,
        mesh=mesh,
        in_specs=placed,
        out_specs=(P("narrow", None), P(("wide", "narrow"))),
        check_vma=False,
    )
```

```python
import functools

import jax
import jax.numpy as jnp
from jax import lax
from jax.experimental import pallas as pl
from jax.experimental.pallas import tpu as pltpu
from jax.sharding import PartitionSpec as P

PASSES = lax.Precision.HIGH
SMEM = pltpu.MemorySpace.SMEM
VMEM = pltpu.MemorySpace.VMEM
NEAR_COST = 15_000_000_000


def contract(left, right, left_dim, right_dim):
    return lax.dot_general(
        left,
        right,
        (((left_dim,), (right_dim,)), ((), ())),
        precision=PASSES,
        preferred_element_type=jnp.float32,
    )


def passed_along(shard, axis, by):
    size = lax.axis_size(axis)
    return lax.ppermute(shard, axis, [(i, (i + by) % size) for i in range(size)])


def swapped(shard, axis, bit):
    size = lax.axis_size(axis)
    return lax.ppermute(shard, axis, [(i, i ^ bit) for i in range(size)])


def far_along(shard, axis, low, by):
    size = lax.axis_size(axis)
    count = size // low
    return lax.ppermute(
        shard, axis, [(i, ((i // low + by) % count) * low + i % low) for i in range(size)]
    )


def after(value, *gates):
    return lax.optimization_barrier((value,) + gates)[0]


def cut_kernel(cuts, place, raw, metric, *refs):
    outs, sems = refs[:-1], refs[-1]
    copies = []
    for k, (which, spot, first, rows) in enumerate(cuts):
        at = place[spot]
        if which == "metric":
            source = metric.at[pl.ds(at * rows, rows)]
        else:
            source = raw.at[at, pl.ds(first, rows)]
        copies.append(pltpu.make_async_copy(source, outs[k], sems.at[k]))
    for copy in copies:
        copy.start()
    for copy in copies:
        copy.wait()


def cut(raw, metric, place, cuts):
    width = raw.shape[2]
    return pl.pallas_call(
        functools.partial(cut_kernel, cuts),
        out_shape=[jax.ShapeDtypeStruct((rows, width), jnp.float32) for *_, rows in cuts],
        in_specs=[
            pl.BlockSpec(memory_space=SMEM),
            pl.BlockSpec(memory_space=pl.ANY),
            pl.BlockSpec(memory_space=pl.ANY),
        ],
        out_specs=[pl.BlockSpec(memory_space=pl.ANY)] * len(cuts),
        scratch_shapes=[pltpu.SemaphoreType.DMA((len(cuts),))],
        name="cut",
    )(place, raw, metric)


def near_fit_kernel(rows_in, metric_in, out, rows, metric, sems):
    copies = [
        pltpu.make_async_copy(rows_in, rows, sems.at[0]),
        pltpu.make_async_copy(metric_in, metric, sems.at[1]),
    ]
    for copy in copies:
        copy.start()
    for copy in copies:
        copy.wait()
    out[...] = dot3(halves(rows[...]), halves(metric[...]), 1)


def near_fit(rows, metric):
    return pl.pallas_call(
        near_fit_kernel,
        out_shape=jax.ShapeDtypeStruct((rows.shape[0], metric.shape[0]), jnp.float32),
        in_specs=[pl.BlockSpec(memory_space=pl.ANY)] * 2,
        out_specs=pl.BlockSpec(memory_space=VMEM),
        scratch_shapes=[
            pltpu.VMEM(rows.shape, jnp.float32),
            pltpu.VMEM(metric.shape, jnp.float32),
            pltpu.SemaphoreType.DMA((2,)),
        ],
        compiler_params=pltpu.CompilerParams(vmem_limit_bytes=20 * 2**20),
        cost_estimate=pl.CostEstimate(flops=NEAR_COST, bytes_accessed=0, transcendentals=0),
        name="near_fit",
    )(rows, metric)


def halves(value):
    high = value.astype(jnp.bfloat16)
    low = (value - high.astype(jnp.float32)).astype(jnp.bfloat16)
    return high, low


def dot3(left, right, right_dim):
    (lh, ll), (rh, rl) = left, right
    dims = (((1,), (right_dim,)), ((), ()))
    total = lax.dot_general(ll, rh, dims, preferred_element_type=jnp.float32)
    total += lax.dot_general(lh, rl, dims, preferred_element_type=jnp.float32)
    return total + lax.dot_general(lh, rh, dims, preferred_element_type=jnp.float32)


def tail_kernel(v, spans, flips, factors, col, row, *refs):
    count = len(spans)
    arrays, (blocks, value), refs = refs[:count], refs[count : count + 2], refs[count + 2 :]
    left, right, amp, amp_t, sems = refs
    virtuals = left.shape[0]
    tiles = virtuals // v
    copies = []
    for k, (side, first, rows) in enumerate(spans):
        target = (left, right)[side].at[pl.ds(first, rows)]
        copies.append(pltpu.make_async_copy(arrays[k], target, sems.at[k]))
    for copy in copies:
        copy.start()
    for copy in copies:
        copy.wait()
    spot = [slice(p * v, (p + 1) * v) for p in range(tiles)]
    lefts = [halves(left[s, :]) for s in spot]
    rights = [halves(right[s, :]) for s in spot]
    total = jnp.float32(0)
    pairs = {}
    for p in range(tiles):
        for q in range(tiles):
            pairs[p, q] = dot3(lefts[p], rights[q], 1)
            gap = col[spot[p], :] + row[:, spot[q]] - factors[0]
            amp[spot[p], spot[q]] = pairs[p, q] / gap
            amp_t[spot[q], spot[p]] = amp[spot[p], spot[q]].T
    for p in range(tiles):
        for q in range(tiles):
            part = 2.0 * amp[spot[p], spot[q]] - amp_t[spot[p], spot[q]]
            total += jnp.sum(pairs[p, q] * part)
    value[0, 0] = total * factors[1]
    k = 0
    for p in range(tiles):
        rows, rows_t = halves(amp[spot[p], :]), halves(amp_t[spot[p], :])
        for q in range(p, tiles):
            block = dot3(rows, halves(amp_t[:, spot[q]]), 0)
            block += dot3(rows_t, halves(amp[:, spot[q]]), 0)
            block *= factors[2]
            if p == q:
                blocks[k] = block
            else:

                @pl.when(flips[k] == 0)
                def _():
                    blocks[k] = block

                @pl.when(flips[k] != 0)
                def _():
                    blocks[k] = block.T

            k += 1


def tail(turned, raw_low, levels, factors, flips, v):
    spans, arrays = [], []
    for side, cuts in ((0, turned), (1, raw_low)):
        first = 0
        for one in cuts:
            spans.append((side, first, one.shape[0]))
            arrays.append(one)
            first += one.shape[0]
    virtuals, width = first, arrays[0].shape[1]
    tiles = virtuals // v
    count = tiles * (tiles + 1) // 2
    square = pltpu.VMEM((virtuals, virtuals), jnp.float32)
    flops = 6 * virtuals * virtuals * width + 12 * count * v * v * virtuals
    return pl.pallas_call(
        functools.partial(tail_kernel, v, spans),
        out_shape=[
            jax.ShapeDtypeStruct((count, v, v), jnp.float32),
            jax.ShapeDtypeStruct((1, 1), jnp.float32),
        ],
        in_specs=[pl.BlockSpec(memory_space=SMEM)] * 2
        + [pl.BlockSpec(memory_space=VMEM)] * 2
        + [pl.BlockSpec(memory_space=pl.ANY)] * len(arrays),
        out_specs=[pl.BlockSpec(memory_space=VMEM), pl.BlockSpec(memory_space=SMEM)],
        scratch_shapes=[
            pltpu.VMEM((virtuals, width), jnp.float32),
            pltpu.VMEM((virtuals, width), jnp.float32),
            square,
            square,
            pltpu.SemaphoreType.DMA((len(arrays),)),
        ],
        compiler_params=pltpu.CompilerParams(vmem_limit_bytes=40 * 2**20),
        cost_estimate=pl.CostEstimate(flops=flops, bytes_accessed=8 * virtuals * width, transcendentals=0),
        name="tail",
    )(flips, factors, levels[:, None], levels[None, :], *arrays)


def tail_plain(turned, raw_low, levels, factors, flips, v):
    virtuals = levels.shape[0]
    pair_ints = contract(jnp.concatenate(turned, 0), jnp.concatenate(raw_low, 0), 1, 1)
    amplitude = pair_ints / (levels[:, None] + levels[None, :] - factors[0])
    value = jnp.sum(pair_ints * (2.0 * amplitude - amplitude.T)) * factors[1]
    blocks = []
    for p in range(virtuals // v):
        at = p * v
        row = contract(amplitude[at : at + v], amplitude[at:], 1, 1)
        row = row + contract(amplitude[:, at : at + v], amplitude[:, at:], 0, 0)
        for first in range(0, virtuals - at, v):
            block = row[:, first : first + v] * factors[2]
            blocks.append(block if first == 0 else jnp.where(flips[len(blocks)] != 0, block.T, block))
    return jnp.stack(blocks), value.reshape(1, 1)


def halved(blocks, w, bit):
    half = blocks.shape[1] // 2
    side = (w // bit) % 2
    kept = lax.dynamic_slice_in_dim(blocks, side * half, half, 1)
    given = lax.dynamic_slice_in_dim(blocks, (1 - side) * half, half, 1)
    return kept + swapped(given, "wide", bit)


def doubled(blocks, w, bit):
    other = swapped(blocks, "wide", bit)
    low = (w // bit) % 2 == 0
    return jnp.concatenate([jnp.where(low, blocks, other), jnp.where(low, other, blocks)], 1)


def spread_out(blocks, far, low, count):
    rows = blocks.shape[1] // count
    total = lax.dynamic_slice_in_dim(blocks, far * rows, rows, 1)
    for by in range(1, count):
        given = lax.dynamic_slice_in_dim(blocks, ((far + by) % count) * rows, rows, 1)
        total = total + far_along(given, "wide", low, by)
    return total


def brought_back(blocks, far, low, count):
    held = [blocks] + [far_along(blocks, "wide", low, by) for by in range(1, count)]
    return jnp.concatenate(
        [lax.select_n(far, *[held[(z - b) % count] for z in range(count)]) for b in range(count)], 1
    )


def on_device(raw_ints, metric, occ_energy, vir_energy, pair_kept):
    wide, narrow = lax.axis_size("wide"), lax.axis_size("narrow")
    w, n = lax.axis_index("wide"), lax.axis_index("narrow")
    v = raw_ints.shape[1]
    virtuals = v * narrow

    near = 4
    count = metric.shape[0] // near
    chunks = [(0, v // 2), (v // 2, v // 4), (3 * v // 4, v // 4)]
    cuts = [("metric", 0, 0, count)]
    for s in range(1, narrow):
        cuts += [("raw", s + 1, first, rows) for first, rows in chunks]
    cuts.append(("raw", 1, 0, v))
    place = jnp.stack([w % near] + [(n + s) % narrow for s in range(narrow)])
    piece, *given, own = cut(raw_ints, metric, place, cuts)

    far = jnp.concatenate([passed_along(piece, "narrow", s) for s in range(1, narrow)], 0)
    raw_low = [passed_along(own, "wide", 1)]
    fit = near_fit(own, metric)
    arrived = []
    for k, one in enumerate(given):
        part = k % len(chunks)
        if part:
            one = after(one, fit if part == 1 else arrived[k - 2])
        arrived.append(passed_along(one, "narrow", 1 + k // len(chunks)))
    lower_energy = passed_along(occ_energy, "wide", 1)
    far = after(far, fit)
    far = jnp.concatenate([far, swapped(far, "wide", 2)], 0)
    raw_low += [passed_along(one, "wide", 1) for one in arrived[:-1]]
    far = after(far, raw_low[0])
    far = jnp.concatenate([far, swapped(far, "wide", 1)], 0)
    full_metric = jnp.concatenate([metric, far], 0)

    def turn(rows):
        return contract(contract(rows, full_metric, 1, 1), full_metric, 1, 0)

    turned = [contract(fit, metric, 1, 0) + contract(contract(own, far, 1, 1), far, 1, 0)]
    raw_low.append(passed_along(after(arrived[-1], turned[0]), "wide", 1))
    turned.append(turn(arrived[0]))
    turned.append(turn(jnp.concatenate(arrived[1:], 0)))

    levels = jnp.concatenate(
        [lax.dynamic_slice_in_dim(vir_energy, ((n - s) % narrow) * v, v, 0) for s in range(narrow)]
    )
    kept = pair_kept[0].astype(jnp.float32)
    factors = jnp.stack(
        [
            occ_energy[0] + lower_energy[0],
            -kept / (virtuals * virtuals),
            kept * (0.0625 / (wide * narrow)),
        ]
    )
    pairs = [(p, q) for p in range(narrow) for q in range(p, narrow)]
    flips = jnp.stack([((n - p) % narrow > (n - q) % narrow).astype(jnp.int32) for p, q in pairs])
    form = tail if v % 128 == 0 else tail_plain
    blocks, own_value = form(turned, raw_low, levels, factors, flips, v)
    own_value = own_value.reshape(1)
    upper_value = passed_along(own_value, "wide", -1)

    def spot(s, t):
        return pairs.index((min(s, t), max(s, t)))

    blocks = halved(blocks, w, 1)
    blocks = halved(blocks, w, 2)
    blocks, upper_value = lax.optimization_barrier((blocks, upper_value))
    rows = spread_out(blocks, w // near, near, wide // near)
    total = jnp.stack([rows[spot(0, t)] for t in range(narrow)])
    for s in range(1, narrow):
        given = jnp.stack([rows[spot(narrow - s, (t - s) % narrow)] for t in range(narrow)])
        total = total + passed_along(given, "narrow", s)
    full = brought_back(total, w // near, near, wide // near)
    full = doubled(doubled(full, w, 2), w, 1)
    columns = []
    for b in range(narrow):
        cases = []
        for m in range(narrow):
            block = full[(m - b) % narrow]
            cases.append(block.T if m > b else block)
        columns.append(lax.select_n(n, *cases))
    return jnp.concatenate(columns, 1), own_value + upper_value


def solution(mesh):
    placed = (
        P("wide", "narrow", None),
        P("narrow", None),
        P(("wide", "narrow")),
        P(),
        P(("wide", "narrow")),
    )
    return jax.shard_map(
        on_device,
        mesh=mesh,
        in_specs=placed,
        out_specs=(P("narrow", None), P(("wide", "narrow"))),
        check_vma=False,
    )
```

```python
import functools

import jax
import jax.numpy as jnp
from jax import lax
from jax.experimental import pallas as pl
from jax.experimental.pallas import tpu as pltpu
from jax.sharding import PartitionSpec as P

PASSES = lax.Precision.HIGH
SMEM = pltpu.MemorySpace.SMEM
VMEM = pltpu.MemorySpace.VMEM
NEAR_COST = 15_000_000_000


def contract(left, right, left_dim, right_dim):
    return lax.dot_general(
        left,
        right,
        (((left_dim,), (right_dim,)), ((), ())),
        precision=PASSES,
        preferred_element_type=jnp.float32,
    )


def passed_along(shard, axis, by):
    size = lax.axis_size(axis)
    return lax.ppermute(shard, axis, [(i, (i + by) % size) for i in range(size)])


def swapped(shard, axis, bit):
    size = lax.axis_size(axis)
    return lax.ppermute(shard, axis, [(i, i ^ bit) for i in range(size)])


def far_along(shard, axis, low, by):
    size = lax.axis_size(axis)
    count = size // low
    return lax.ppermute(
        shard, axis, [(i, ((i // low + by) % count) * low + i % low) for i in range(size)]
    )


def after(value, *gates):
    return lax.optimization_barrier((value,) + gates)[0]


def near_fit_kernel(rows_in, metric_in, out, rows, metric, sems):
    copies = [
        pltpu.make_async_copy(rows_in, rows, sems.at[0]),
        pltpu.make_async_copy(metric_in, metric, sems.at[1]),
    ]
    for copy in copies:
        copy.start()
    for copy in copies:
        copy.wait()
    out[...] = dot3(halves(rows[...]), halves(metric[...]), 1)


def near_fit(rows, metric):
    return pl.pallas_call(
        near_fit_kernel,
        out_shape=jax.ShapeDtypeStruct((rows.shape[0], metric.shape[0]), jnp.float32),
        in_specs=[pl.BlockSpec(memory_space=pl.ANY)] * 2,
        out_specs=pl.BlockSpec(memory_space=VMEM),
        scratch_shapes=[
            pltpu.VMEM(rows.shape, jnp.float32),
            pltpu.VMEM(metric.shape, jnp.float32),
            pltpu.SemaphoreType.DMA((2,)),
        ],
        compiler_params=pltpu.CompilerParams(vmem_limit_bytes=20 * 2**20),
        cost_estimate=pl.CostEstimate(flops=NEAR_COST, bytes_accessed=0, transcendentals=0),
        name="near_fit",
    )(rows, metric)


def halves(value):
    high = value.astype(jnp.bfloat16)
    low = (value - high.astype(jnp.float32)).astype(jnp.bfloat16)
    return high, low


def dot3(left, right, right_dim):
    (lh, ll), (rh, rl) = left, right
    dims = (((1,), (right_dim,)), ((), ()))
    total = lax.dot_general(ll, rh, dims, preferred_element_type=jnp.float32)
    total += lax.dot_general(lh, rl, dims, preferred_element_type=jnp.float32)
    return total + lax.dot_general(lh, rh, dims, preferred_element_type=jnp.float32)


def turn_kernel(spans, *refs):
    count = len(spans)
    arrays, out, sides, sems = refs[:count], refs[count], refs[count + 1 : -1], refs[-1]
    copies = []
    for k, (side, first, length) in enumerate(spans):
        target = sides[side].at[pl.ds(first, length)]
        copies.append(pltpu.make_async_copy(arrays[k], target, sems.at[k]))
    for copy in copies:
        copy.start()
    for copy in copies:
        copy.wait()
    rows, metric, *fits = sides
    done = fits[0].shape[1] if fits else 0
    factor = halves(metric[done:])
    total = dot3(halves(dot3(halves(rows[...]), factor, 1)), factor, 0)
    for fit in fits:
        total += dot3(halves(fit[...]), halves(metric[:done]), 0)
    out[...] = total


def stacked(*sides):
    spans, arrays, lengths = [], [], []
    for side, cuts in enumerate(sides):
        first = 0
        for one in cuts:
            spans.append((side, first, one.shape[0]))
            arrays.append(one)
            first += one.shape[0]
        lengths.append(first)
    return spans, arrays, lengths


def turn(rows, metric, *fits):
    spans, arrays, (count, fitted, *_) = stacked(rows, metric, *[[fit] for fit in fits])
    width = rows[0].shape[1]
    return pl.pallas_call(
        functools.partial(turn_kernel, spans),
        out_shape=jax.ShapeDtypeStruct((count, width), jnp.float32),
        in_specs=[pl.BlockSpec(memory_space=pl.ANY)] * len(arrays),
        out_specs=pl.BlockSpec(memory_space=VMEM),
        scratch_shapes=[
            pltpu.VMEM((count, width), jnp.float32),
            pltpu.VMEM((fitted, width), jnp.float32),
        ]
        + [pltpu.VMEM(fit.shape, jnp.float32) for fit in fits]
        + [pltpu.SemaphoreType.DMA((len(arrays),))],
        compiler_params=pltpu.CompilerParams(vmem_limit_bytes=30 * 2**20),
        cost_estimate=pl.CostEstimate(
            flops=12 * count * fitted * width,
            bytes_accessed=4 * width * (2 * count + fitted),
            transcendentals=0,
        ),
        name="turn",
    )(*arrays)


def tail_kernel(v, spans, flips, factors, col, row, *refs):
    count = len(spans)
    arrays, (blocks, value), refs = refs[:count], refs[count : count + 2], refs[count + 2 :]
    left, right, amp, amp_t, sems = refs
    virtuals = left.shape[0]
    tiles = virtuals // v
    copies = []
    for k, (side, first, rows) in enumerate(spans):
        target = (left, right)[side].at[pl.ds(first, rows)]
        copies.append(pltpu.make_async_copy(arrays[k], target, sems.at[k]))
    for copy in copies:
        copy.start()
    for copy in copies:
        copy.wait()
    spot = [slice(p * v, (p + 1) * v) for p in range(tiles)]
    lefts = [halves(left[s, :]) for s in spot]
    rights = [halves(right[s, :]) for s in spot]
    total = jnp.float32(0)
    pairs = {}
    for p in range(tiles):
        for q in range(tiles):
            pairs[p, q] = dot3(lefts[p], rights[q], 1)
            gap = col[spot[p], :] + row[:, spot[q]] - factors[0]
            amp[spot[p], spot[q]] = pairs[p, q] / gap
            amp_t[spot[q], spot[p]] = amp[spot[p], spot[q]].T
    for p in range(tiles):
        for q in range(tiles):
            part = 2.0 * amp[spot[p], spot[q]] - amp_t[spot[p], spot[q]]
            total += jnp.sum(pairs[p, q] * part)
    value[0, 0] = total * factors[1]
    k = 0
    for p in range(tiles):
        rows, rows_t = halves(amp[spot[p], :]), halves(amp_t[spot[p], :])
        for q in range(p, tiles):
            block = dot3(rows, halves(amp_t[:, spot[q]]), 0)
            block += dot3(rows_t, halves(amp[:, spot[q]]), 0)
            block *= factors[2]
            if p == q:
                blocks[k] = block
            else:

                @pl.when(flips[k] == 0)
                def _():
                    blocks[k] = block

                @pl.when(flips[k] != 0)
                def _():
                    blocks[k] = block.T

            k += 1


def tail(turned, raw_low, levels, factors, flips, v):
    spans, arrays, (virtuals, _) = stacked(turned, raw_low)
    width = arrays[0].shape[1]
    tiles = virtuals // v
    count = tiles * (tiles + 1) // 2
    square = pltpu.VMEM((virtuals, virtuals), jnp.float32)
    flops = 6 * virtuals * virtuals * width + 12 * count * v * v * virtuals
    return pl.pallas_call(
        functools.partial(tail_kernel, v, spans),
        out_shape=[
            jax.ShapeDtypeStruct((count, v, v), jnp.float32),
            jax.ShapeDtypeStruct((1, 1), jnp.float32),
        ],
        in_specs=[pl.BlockSpec(memory_space=SMEM)] * 2
        + [pl.BlockSpec(memory_space=VMEM)] * 2
        + [pl.BlockSpec(memory_space=pl.ANY)] * len(arrays),
        out_specs=[pl.BlockSpec(memory_space=VMEM), pl.BlockSpec(memory_space=SMEM)],
        scratch_shapes=[
            pltpu.VMEM((virtuals, width), jnp.float32),
            pltpu.VMEM((virtuals, width), jnp.float32),
            square,
            square,
            pltpu.SemaphoreType.DMA((len(arrays),)),
        ],
        compiler_params=pltpu.CompilerParams(vmem_limit_bytes=40 * 2**20),
        cost_estimate=pl.CostEstimate(flops=flops, bytes_accessed=8 * virtuals * width, transcendentals=0),
        name="tail",
    )(flips, factors, levels[:, None], levels[None, :], *arrays)


def tail_plain(turned, raw_low, levels, factors, flips, v):
    virtuals = levels.shape[0]
    pair_ints = contract(jnp.concatenate(turned, 0), jnp.concatenate(raw_low, 0), 1, 1)
    amplitude = pair_ints / (levels[:, None] + levels[None, :] - factors[0])
    value = jnp.sum(pair_ints * (2.0 * amplitude - amplitude.T)) * factors[1]
    blocks = []
    for p in range(virtuals // v):
        at = p * v
        row = contract(amplitude[at : at + v], amplitude[at:], 1, 1)
        row = row + contract(amplitude[:, at : at + v], amplitude[:, at:], 0, 0)
        for first in range(0, virtuals - at, v):
            block = row[:, first : first + v] * factors[2]
            blocks.append(block if first == 0 else jnp.where(flips[len(blocks)] != 0, block.T, block))
    return jnp.stack(blocks), value.reshape(1, 1)


def halved(blocks, w, bit):
    half = blocks.shape[1] // 2
    side = (w // bit) % 2
    kept = lax.dynamic_slice_in_dim(blocks, side * half, half, 1)
    given = lax.dynamic_slice_in_dim(blocks, (1 - side) * half, half, 1)
    return kept + swapped(given, "wide", bit)


def doubled(blocks, w, bit):
    other = swapped(blocks, "wide", bit)
    low = (w // bit) % 2 == 0
    return jnp.concatenate([jnp.where(low, blocks, other), jnp.where(low, other, blocks)], 1)


def spread_out(blocks, far, low, count):
    rows = blocks.shape[1] // count
    total = lax.dynamic_slice_in_dim(blocks, far * rows, rows, 1)
    for by in range(1, count):
        given = lax.dynamic_slice_in_dim(blocks, ((far + by) % count) * rows, rows, 1)
        total = total + far_along(given, "wide", low, by)
    return total


def brought_back(blocks, far, low, count):
    held = [blocks] + [far_along(blocks, "wide", low, by) for by in range(1, count)]
    return jnp.concatenate(
        [lax.select_n(far, *[held[(z - b) % count] for z in range(count)]) for b in range(count)], 1
    )


def on_device(raw_ints, metric, occ_energy, vir_energy, pair_kept):
    wide, narrow = lax.axis_size("wide"), lax.axis_size("narrow")
    w, n = lax.axis_index("wide"), lax.axis_index("narrow")
    v = raw_ints.shape[1]
    virtuals = v * narrow

    near = 4
    count = metric.shape[0] // near
    chunks = [(0, v // 2), (v // 2, v // 4), (3 * v // 4, v // 4)]
    piece = lax.dynamic_slice_in_dim(metric, (w % near) * count, count, 0)
    own = lax.dynamic_index_in_dim(raw_ints, n, 0, keepdims=False)

    far = [passed_along(piece, "narrow", s) for s in range(1, narrow)]
    raw_low = [passed_along(own, "wide", 1)]
    arrived, gives = [], []
    for s in range(1, narrow):
        given = lax.dynamic_index_in_dim(raw_ints, (n + s) % narrow, 0, keepdims=False)
        parts = [given[first : first + rows] for first, rows in chunks]
        gives += parts
        arrived += [passed_along(one, "narrow", s) for one in reversed(parts)][::-1]
    lower_energy = passed_along(occ_energy, "wide", 1)
    fit = near_fit(after(own, *gives), metric)
    far = [after(one, fit) for one in far]
    far_x = [swapped(one, "wide", 2) for one in far]
    far_core = [swapped(one, "wide", 1) for one in far]
    raw_low += [passed_along(one, "wide", 1) for one in arrived[:-1]]
    far_x = [after(one, raw_low[0], arrived[0]) for one in far_x]
    far_last = [swapped(one, "wide", 1) for one in far_x]
    pieces = [metric] + far + far_core + far_x + far_last

    turned = [turn([own], pieces, fit)]
    raw_low.append(passed_along(after(arrived[-1], turned[0], raw_low[1]), "wide", 1))
    turned.append(turn(arrived, pieces))

    levels = jnp.concatenate(
        [lax.dynamic_slice_in_dim(vir_energy, ((n - s) % narrow) * v, v, 0) for s in range(narrow)]
    )
    kept = pair_kept[0].astype(jnp.float32)
    factors = jnp.stack(
        [
            occ_energy[0] + lower_energy[0],
            -kept / (virtuals * virtuals),
            kept * (0.0625 / (wide * narrow)),
        ]
    )
    pairs = [(p, q) for p in range(narrow) for q in range(p, narrow)]
    flips = jnp.stack([((n - p) % narrow > (n - q) % narrow).astype(jnp.int32) for p, q in pairs])
    form = tail if v % 128 == 0 else tail_plain
    blocks, own_value = form(turned, raw_low, levels, factors, flips, v)
    own_value = own_value.reshape(1)
    upper_value = passed_along(own_value, "wide", -1)

    def spot(s, t):
        return pairs.index((min(s, t), max(s, t)))

    blocks = halved(blocks, w, 1)
    blocks = halved(blocks, w, 2)
    blocks, upper_value = lax.optimization_barrier((blocks, upper_value))
    rows = spread_out(blocks, w // near, near, wide // near)
    total = jnp.stack([rows[spot(0, t)] for t in range(narrow)])
    for s in range(1, narrow):
        given = jnp.stack([rows[spot(narrow - s, (t - s) % narrow)] for t in range(narrow)])
        total = total + passed_along(given, "narrow", s)
    full = brought_back(total, w // near, near, wide // near)
    full = doubled(doubled(full, w, 2), w, 1)
    columns = []
    for b in range(narrow):
        cases = []
        for m in range(narrow):
            block = full[(m - b) % narrow]
            cases.append(block.T if m > b else block)
        columns.append(lax.select_n(n, *cases))
    return jnp.concatenate(columns, 1), own_value + upper_value


def solution(mesh):
    placed = (
        P("wide", "narrow", None),
        P("narrow", None),
        P(("wide", "narrow")),
        P(),
        P(("wide", "narrow")),
    )
    return jax.shard_map(
        on_device,
        mesh=mesh,
        in_specs=placed,
        out_specs=(P("narrow", None), P(("wide", "narrow"))),
        check_vma=False,
    )
```

```python
import functools

import jax
import jax.numpy as jnp
from jax import lax
from jax.experimental import pallas as pl
from jax.experimental.pallas import tpu as pltpu
from jax.sharding import PartitionSpec as P

PASSES = lax.Precision.HIGH
SMEM = pltpu.MemorySpace.SMEM
VMEM = pltpu.MemorySpace.VMEM
NEAR_COST = 15_000_000_000
PIECE = 8192


def contract(left, right, left_dim, right_dim):
    return lax.dot_general(
        left,
        right,
        (((left_dim,), (right_dim,)), ((), ())),
        precision=PASSES,
        preferred_element_type=jnp.float32,
    )


def passed_along(shard, axis, by):
    size = lax.axis_size(axis)
    return lax.ppermute(shard, axis, [(i, (i + by) % size) for i in range(size)])


def swapped(shard, axis, bit):
    size = lax.axis_size(axis)
    return lax.ppermute(shard, axis, [(i, i ^ bit) for i in range(size)])


def after(value, *gates):
    return lax.optimization_barrier((value,) + gates)[0]


def near_fit_kernel(rows_in, metric_in, out, rows, metric, sems):
    copies = [
        pltpu.make_async_copy(rows_in, rows, sems.at[0]),
        pltpu.make_async_copy(metric_in, metric, sems.at[1]),
    ]
    for copy in copies:
        copy.start()
    for copy in copies:
        copy.wait()
    out[...] = dot3(halves(rows[...]), halves(metric[...]), 1)


def near_fit(rows, metric):
    return pl.pallas_call(
        near_fit_kernel,
        out_shape=jax.ShapeDtypeStruct((rows.shape[0], metric.shape[0]), jnp.float32),
        in_specs=[pl.BlockSpec(memory_space=pl.ANY)] * 2,
        out_specs=pl.BlockSpec(memory_space=VMEM),
        scratch_shapes=[
            pltpu.VMEM(rows.shape, jnp.float32),
            pltpu.VMEM(metric.shape, jnp.float32),
            pltpu.SemaphoreType.DMA((2,)),
        ],
        compiler_params=pltpu.CompilerParams(vmem_limit_bytes=20 * 2**20),
        cost_estimate=pl.CostEstimate(flops=NEAR_COST, bytes_accessed=0, transcendentals=0),
        name="near_fit",
    )(rows, metric)


def halves(value):
    high = value.astype(jnp.bfloat16)
    low = (value - high.astype(jnp.float32)).astype(jnp.bfloat16)
    return high, low


def dot3(left, right, right_dim):
    (lh, ll), (rh, rl) = left, right
    dims = (((1,), (right_dim,)), ((), ()))
    total = lax.dot_general(ll, rh, dims, preferred_element_type=jnp.float32)
    total += lax.dot_general(lh, rl, dims, preferred_element_type=jnp.float32)
    return total + lax.dot_general(lh, rh, dims, preferred_element_type=jnp.float32)


def turn_kernel(spans, *refs):
    count = len(spans)
    arrays, out, sides, sems = refs[:count], refs[count], refs[count + 1 : -1], refs[-1]
    copies = []
    for k, (side, first, length) in enumerate(spans):
        target = sides[side].at[pl.ds(first, length)]
        copies.append(pltpu.make_async_copy(arrays[k], target, sems.at[k]))
    for copy in copies:
        copy.start()
    for copy in copies:
        copy.wait()
    rows, metric, *fits = sides
    done = fits[0].shape[1] if fits else 0
    factor = halves(metric[done:])
    total = dot3(halves(dot3(halves(rows[...]), factor, 1)), factor, 0)
    for fit in fits:
        total += dot3(halves(fit[...]), halves(metric[:done]), 0)
    out[...] = total


def stacked(*sides):
    spans, arrays, lengths = [], [], []
    for side, cuts in enumerate(sides):
        first = 0
        for one in cuts:
            spans.append((side, first, one.shape[0]))
            arrays.append(one)
            first += one.shape[0]
        lengths.append(first)
    return spans, arrays, lengths


def turn(rows, metric, *fits):
    spans, arrays, (count, fitted, *_) = stacked(rows, metric, *[[fit] for fit in fits])
    width = rows[0].shape[1]
    return pl.pallas_call(
        functools.partial(turn_kernel, spans),
        out_shape=jax.ShapeDtypeStruct((count, width), jnp.float32),
        in_specs=[pl.BlockSpec(memory_space=pl.ANY)] * len(arrays),
        out_specs=pl.BlockSpec(memory_space=VMEM),
        scratch_shapes=[
            pltpu.VMEM((count, width), jnp.float32),
            pltpu.VMEM((fitted, width), jnp.float32),
        ]
        + [pltpu.VMEM(fit.shape, jnp.float32) for fit in fits]
        + [pltpu.SemaphoreType.DMA((len(arrays),))],
        compiler_params=pltpu.CompilerParams(vmem_limit_bytes=30 * 2**20),
        cost_estimate=pl.CostEstimate(
            flops=12 * count * fitted * width,
            bytes_accessed=4 * width * (2 * count + fitted),
            transcendentals=0,
        ),
        name="turn",
    )(*arrays)


def count_of(tiles):
    return tiles * (tiles + 1) // 2


def piece_rows(v):
    return min(v, max(8, PIECE // v))


def tail_kernel(v, spans, places, factors, col, row, *refs):
    count = len(spans)
    arrays, outs, (value, left, right, amp, amp_t, sems) = refs[:count], refs[count:-6], refs[-6:]
    virtuals = left.shape[0]
    tiles = virtuals // v
    copies = []
    for k, (side, first, rows) in enumerate(spans):
        target = (left, right)[side].at[pl.ds(first, rows)]
        copies.append(pltpu.make_async_copy(arrays[k], target, sems.at[k]))
    for copy in copies:
        copy.start()
    for copy in copies:
        copy.wait()
    spot = [slice(p * v, (p + 1) * v) for p in range(tiles)]
    lefts = [halves(left[s, :]) for s in spot]
    rights = [halves(right[s, :]) for s in spot]
    total = jnp.float32(0)
    pairs = {}
    for p in range(tiles):
        for q in range(tiles):
            pairs[p, q] = dot3(lefts[p], rights[q], 1)
            gap = col[spot[p], :] + row[:, spot[q]] - factors[0]
            amp[spot[p], spot[q]] = pairs[p, q] / gap
            amp_t[spot[q], spot[p]] = amp[spot[p], spot[q]].T
    for p in range(tiles):
        for q in range(tiles):
            part = 2.0 * amp[spot[p], spot[q]] - amp_t[spot[p], spot[q]]
            total += jnp.sum(pairs[p, q] * part)
    value[0, 0] = total * factors[1]
    k = 0
    for a in range(tiles):
        at = pl.ds(pl.multiple_of(places[a], v), v)
        rows, rows_t = halves(amp[at, :]), halves(amp_t[at, :])
        for b in range(a, tiles):
            at = pl.ds(pl.multiple_of(places[b], v), v)
            block = dot3(rows, halves(amp_t[:, at]), 0)
            block += dot3(rows_t, halves(amp[:, at]), 0)
            block *= factors[2]
            for first in range(0, v, outs[k].shape[0]):
                outs[k][...] = block[first : first + outs[k].shape[0]]
                k += 1


def tail(turned, raw_low, levels, factors, places, v):
    spans, arrays, (virtuals, _) = stacked(turned, raw_low)
    width = arrays[0].shape[1]
    tiles = virtuals // v
    count, rows = count_of(tiles), piece_rows(v)
    square = pltpu.VMEM((virtuals, virtuals), jnp.float32)
    flops = 6 * virtuals * virtuals * width + 12 * count * v * v * virtuals
    pieces = [jax.ShapeDtypeStruct((rows, v), jnp.float32)] * (count * v // rows)
    *blocks, value = pl.pallas_call(
        functools.partial(tail_kernel, v, spans),
        out_shape=pieces + [jax.ShapeDtypeStruct((1, 1), jnp.float32)],
        in_specs=[pl.BlockSpec(memory_space=SMEM)] * 2
        + [pl.BlockSpec(memory_space=VMEM)] * 2
        + [pl.BlockSpec(memory_space=pl.ANY)] * len(arrays),
        out_specs=[pl.BlockSpec(memory_space=VMEM)] * len(pieces) + [pl.BlockSpec(memory_space=SMEM)],
        scratch_shapes=[
            pltpu.VMEM((virtuals, width), jnp.float32),
            pltpu.VMEM((virtuals, width), jnp.float32),
            square,
            square,
            pltpu.SemaphoreType.DMA((len(arrays),)),
        ],
        compiler_params=pltpu.CompilerParams(vmem_limit_bytes=40 * 2**20),
        cost_estimate=pl.CostEstimate(flops=flops, bytes_accessed=8 * virtuals * width, transcendentals=0),
        name="tail",
    )(places, factors, levels[:, None], levels[None, :], *arrays)
    return blocks, value


def tail_plain(turned, raw_low, levels, factors, places, v):
    virtuals = levels.shape[0]
    pair_ints = contract(jnp.concatenate(turned, 0), jnp.concatenate(raw_low, 0), 1, 1)
    amplitude = pair_ints / (levels[:, None] + levels[None, :] - factors[0])
    value = jnp.sum(pair_ints * (2.0 * amplitude - amplitude.T)) * factors[1]
    order = (places[:, None] + jnp.arange(v)[None, :]).reshape(virtuals)
    amplitude = amplitude[order][:, order]
    blocks = []
    for at in range(0, virtuals, v):
        row = contract(amplitude[at : at + v], amplitude[at:], 1, 1)
        row = row + contract(amplitude[:, at : at + v], amplitude[:, at:], 0, 0)
        blocks += jnp.split(row * factors[2], (virtuals - at) // v, 1)
    return [piece for block in blocks for piece in jnp.split(block, v // piece_rows(v), 0)], value


def assembled_kernel(v, pairs, index, *refs):
    pieces, out = refs[:-1], refs[-1]
    each = len(pieces) // len(pairs)
    tiles = out.shape[1] // v
    for m in range(tiles):

        @pl.when(index[0] == m)
        def _():
            for b in range(tiles):
                k = pairs.index((min(m, b), max(m, b))) * each
                block = jnp.concatenate([one[...] for one in pieces[k : k + each]], 0)
                out[:, b * v : (b + 1) * v] = block.T if m > b else block


def assembled(pieces, pairs, n, v, narrow):
    return pl.pallas_call(
        functools.partial(assembled_kernel, v, pairs),
        out_shape=jax.ShapeDtypeStruct((v, v * narrow), jnp.float32),
        in_specs=[pl.BlockSpec(memory_space=SMEM)] + [pl.BlockSpec(memory_space=VMEM)] * len(pieces),
        out_specs=pl.BlockSpec(memory_space=VMEM),
        name="assembled",
    )(n.reshape(1), *pieces)


def assembled_plain(pieces, pairs, n, v, narrow):
    each = len(pieces) // len(pairs)
    full = [jnp.concatenate(pieces[k * each : (k + 1) * each], 0) for k in range(len(pairs))]
    columns = []
    for b in range(narrow):
        cases = []
        for m in range(narrow):
            block = full[pairs.index((min(m, b), max(m, b)))]
            cases.append(block.T if m > b else block)
        columns.append(lax.select_n(n, *cases))
    return jnp.concatenate(columns, 1)


def on_device(raw_ints, metric, occ_energy, vir_energy, pair_kept):
    wide, narrow = lax.axis_size("wide"), lax.axis_size("narrow")
    w, n = lax.axis_index("wide"), lax.axis_index("narrow")
    v = raw_ints.shape[1]
    virtuals = v * narrow

    near = 4
    count = metric.shape[0] // near
    chunks = [(0, v // 2), (v // 2, v // 4), (3 * v // 4, v // 4)]
    piece = lax.dynamic_slice_in_dim(metric, (w % near) * count, count, 0)
    own = lax.dynamic_index_in_dim(raw_ints, n, 0, keepdims=False)

    far = [passed_along(piece, "narrow", s) for s in range(1, narrow)]
    raw_low = [passed_along(own, "wide", 1)]
    arrived, gives = [], []
    for s in range(1, narrow):
        given = lax.dynamic_index_in_dim(raw_ints, (n + s) % narrow, 0, keepdims=False)
        parts = [given[first : first + rows] for first, rows in chunks]
        gives += parts
        arrived += [passed_along(one, "narrow", s) for one in reversed(parts)][::-1]
    lower_energy = passed_along(occ_energy, "wide", 1)
    fit = near_fit(after(own, *gives), metric)
    far = [after(one, fit) for one in far]
    far_x = [swapped(one, "wide", 2) for one in far]
    far_core = [swapped(one, "wide", 1) for one in far]
    raw_low += [passed_along(one, "wide", 1) for one in arrived[:-1]]
    far_x = [after(one, raw_low[0], arrived[0]) for one in far_x]
    far_last = [swapped(one, "wide", 1) for one in far_x]
    pieces = [metric] + far + far_core + far_x + far_last

    turned = [turn([own], pieces, fit)]
    raw_low.append(passed_along(after(arrived[-1], turned[0], raw_low[1]), "wide", 1))
    turned.append(turn(arrived, pieces))

    levels = jnp.concatenate(
        [lax.dynamic_slice_in_dim(vir_energy, ((n - s) % narrow) * v, v, 0) for s in range(narrow)]
    )
    kept = pair_kept[0].astype(jnp.float32)
    factors = jnp.stack(
        [
            occ_energy[0] + lower_energy[0],
            -kept / (virtuals * virtuals),
            kept * (0.0625 / (wide * narrow)),
        ]
    )
    pairs = [(a, b) for a in range(narrow) for b in range(a, narrow)]
    places = jnp.stack([(n - a) % narrow * v for a in range(narrow)])
    form, joined = (tail, assembled) if v % 128 == 0 else (tail_plain, assembled_plain)
    blocks, own_value = form(turned, raw_low, levels, factors, places, v)

    place = w * narrow + n
    values = jnp.where(jnp.arange(wide * narrow) == place, own_value.reshape(()), 0.0)
    *blocks, values = lax.psum((*blocks, values), ("wide", "narrow"))
    partner = lax.dynamic_index_in_dim(values, (place + narrow) % (wide * narrow), 0)
    energy = lax.dynamic_index_in_dim(values, place, 0) + partner

    return joined(blocks, pairs, n, v, narrow), energy


def solution(mesh):
    placed = (
        P("wide", "narrow", None),
        P("narrow", None),
        P(("wide", "narrow")),
        P(),
        P(("wide", "narrow")),
    )
    return jax.shard_map(
        on_device,
        mesh=mesh,
        in_specs=placed,
        out_specs=(P("narrow", None), P(("wide", "narrow"))),
        check_vma=False,
    )
```

```python
import functools

import jax
import jax.numpy as jnp
from jax import lax
from jax.experimental import pallas as pl
from jax.experimental.pallas import tpu as pltpu
from jax.sharding import PartitionSpec as P

PASSES = lax.Precision.HIGH
SMEM = pltpu.MemorySpace.SMEM
VMEM = pltpu.MemorySpace.VMEM
NEAR_COST = 15_000_000_000
PIECE = 2048


def contract(left, right, left_dim, right_dim):
    return lax.dot_general(
        left,
        right,
        (((left_dim,), (right_dim,)), ((), ())),
        precision=PASSES,
        preferred_element_type=jnp.float32,
    )


def passed_along(shard, axis, by):
    size = lax.axis_size(axis)
    return lax.ppermute(shard, axis, [(i, (i + by) % size) for i in range(size)])


def swapped(shard, axis, bit):
    size = lax.axis_size(axis)
    return lax.ppermute(shard, axis, [(i, i ^ bit) for i in range(size)])


def after(value, *gates):
    return lax.optimization_barrier((value,) + gates)[0]


def near_fit_kernel(rows_in, metric_in, out, rows, metric, sems):
    copies = [
        pltpu.make_async_copy(rows_in, rows, sems.at[0]),
        pltpu.make_async_copy(metric_in, metric, sems.at[1]),
    ]
    for copy in copies:
        copy.start()
    for copy in copies:
        copy.wait()
    out[...] = dot3(halves(rows[...]), halves(metric[...]), 1)


def near_fit(rows, metric):
    return pl.pallas_call(
        near_fit_kernel,
        out_shape=jax.ShapeDtypeStruct((rows.shape[0], metric.shape[0]), jnp.float32),
        in_specs=[pl.BlockSpec(memory_space=pl.ANY)] * 2,
        out_specs=pl.BlockSpec(memory_space=VMEM),
        scratch_shapes=[
            pltpu.VMEM(rows.shape, jnp.float32),
            pltpu.VMEM(metric.shape, jnp.float32),
            pltpu.SemaphoreType.DMA((2,)),
        ],
        compiler_params=pltpu.CompilerParams(vmem_limit_bytes=20 * 2**20),
        cost_estimate=pl.CostEstimate(flops=NEAR_COST, bytes_accessed=0, transcendentals=0),
        name="near_fit",
    )(rows, metric)


def halves(value):
    high = value.astype(jnp.bfloat16)
    low = (value - high.astype(jnp.float32)).astype(jnp.bfloat16)
    return high, low


def dot3(left, right, right_dim):
    (lh, ll), (rh, rl) = left, right
    dims = (((1,), (right_dim,)), ((), ()))
    total = lax.dot_general(ll, rh, dims, preferred_element_type=jnp.float32)
    total += lax.dot_general(lh, rl, dims, preferred_element_type=jnp.float32)
    return total + lax.dot_general(lh, rh, dims, preferred_element_type=jnp.float32)


def turn_kernel(spans, *refs):
    count = len(spans)
    arrays, out, sides, sems = refs[:count], refs[count], refs[count + 1 : -1], refs[-1]
    copies = []
    for k, (side, first, length) in enumerate(spans):
        target = sides[side].at[pl.ds(first, length)]
        copies.append(pltpu.make_async_copy(arrays[k], target, sems.at[k]))
    for copy in copies:
        copy.start()
    for copy in copies:
        copy.wait()
    rows, metric, *fits = sides
    done = fits[0].shape[1] if fits else 0
    factor = halves(metric[done:])
    total = dot3(halves(dot3(halves(rows[...]), factor, 1)), factor, 0)
    for fit in fits:
        total += dot3(halves(fit[...]), halves(metric[:done]), 0)
    out[...] = total


def stacked(*sides):
    spans, arrays, lengths = [], [], []
    for side, cuts in enumerate(sides):
        first = 0
        for one in cuts:
            spans.append((side, first, one.shape[0]))
            arrays.append(one)
            first += one.shape[0]
        lengths.append(first)
    return spans, arrays, lengths


def turn(rows, metric, *fits):
    spans, arrays, (count, fitted, *_) = stacked(rows, metric, *[[fit] for fit in fits])
    width = rows[0].shape[1]
    return pl.pallas_call(
        functools.partial(turn_kernel, spans),
        out_shape=jax.ShapeDtypeStruct((count, width), jnp.float32),
        in_specs=[pl.BlockSpec(memory_space=pl.ANY)] * len(arrays),
        out_specs=pl.BlockSpec(memory_space=VMEM),
        scratch_shapes=[
            pltpu.VMEM((count, width), jnp.float32),
            pltpu.VMEM((fitted, width), jnp.float32),
        ]
        + [pltpu.VMEM(fit.shape, jnp.float32) for fit in fits]
        + [pltpu.SemaphoreType.DMA((len(arrays),))],
        compiler_params=pltpu.CompilerParams(vmem_limit_bytes=30 * 2**20),
        cost_estimate=pl.CostEstimate(
            flops=12 * count * fitted * width,
            bytes_accessed=4 * width * (2 * count + fitted),
            transcendentals=0,
        ),
        name="turn",
    )(*arrays)


def count_of(tiles):
    return tiles * (tiles + 1) // 2


def piece_rows(v):
    return min(v, max(8, PIECE // v))


def tail_kernel(v, spans, places, factors, col, row, *refs):
    count = len(spans)
    arrays, outs, (value, left, right, amp, amp_t, sems) = refs[:count], refs[count:-6], refs[-6:]
    virtuals = left.shape[0]
    tiles = virtuals // v
    copies = []
    for k, (side, first, rows) in enumerate(spans):
        target = (left, right)[side].at[pl.ds(first, rows)]
        copies.append(pltpu.make_async_copy(arrays[k], target, sems.at[k]))
    for copy in copies:
        copy.start()
    for copy in copies:
        copy.wait()
    spot = [slice(p * v, (p + 1) * v) for p in range(tiles)]
    lefts = [halves(left[s, :]) for s in spot]
    rights = [halves(right[s, :]) for s in spot]
    total = jnp.float32(0)
    pairs = {}
    for p in range(tiles):
        for q in range(tiles):
            pairs[p, q] = dot3(lefts[p], rights[q], 1)
            gap = col[spot[p], :] + row[:, spot[q]] - factors[0]
            amp[spot[p], spot[q]] = pairs[p, q] / gap
            amp_t[spot[q], spot[p]] = amp[spot[p], spot[q]].T
    for p in range(tiles):
        for q in range(tiles):
            part = 2.0 * amp[spot[p], spot[q]] - amp_t[spot[p], spot[q]]
            total += jnp.sum(pairs[p, q] * part)
    value[0, 0] = total * factors[1]
    k = 0
    for a in range(tiles):
        at = pl.ds(pl.multiple_of(places[a], v), v)
        rows, rows_t = halves(amp[at, :]), halves(amp_t[at, :])
        for b in range(a, tiles):
            at = pl.ds(pl.multiple_of(places[b], v), v)
            block = dot3(rows, halves(amp_t[:, at]), 0)
            block += dot3(rows_t, halves(amp[:, at]), 0)
            block *= factors[2]
            for first in range(0, v, outs[k].shape[0]):
                outs[k][...] = block[first : first + outs[k].shape[0]]
                k += 1


def tail(turned, raw_low, levels, factors, places, v):
    spans, arrays, (virtuals, _) = stacked(turned, raw_low)
    width = arrays[0].shape[1]
    tiles = virtuals // v
    count, rows = count_of(tiles), piece_rows(v)
    square = pltpu.VMEM((virtuals, virtuals), jnp.float32)
    flops = 6 * virtuals * virtuals * width + 12 * count * v * v * virtuals
    pieces = [jax.ShapeDtypeStruct((rows, v), jnp.float32)] * (count * v // rows)
    *blocks, value = pl.pallas_call(
        functools.partial(tail_kernel, v, spans),
        out_shape=pieces + [jax.ShapeDtypeStruct((1, 1), jnp.float32)],
        in_specs=[pl.BlockSpec(memory_space=SMEM)] * 2
        + [pl.BlockSpec(memory_space=VMEM)] * 2
        + [pl.BlockSpec(memory_space=pl.ANY)] * len(arrays),
        out_specs=[pl.BlockSpec(memory_space=VMEM)] * len(pieces) + [pl.BlockSpec(memory_space=SMEM)],
        scratch_shapes=[
            pltpu.VMEM((virtuals, width), jnp.float32),
            pltpu.VMEM((virtuals, width), jnp.float32),
            square,
            square,
            pltpu.SemaphoreType.DMA((len(arrays),)),
        ],
        compiler_params=pltpu.CompilerParams(vmem_limit_bytes=40 * 2**20),
        cost_estimate=pl.CostEstimate(flops=flops, bytes_accessed=8 * virtuals * width, transcendentals=0),
        name="tail",
    )(places, factors, levels[:, None], levels[None, :], *arrays)
    return blocks, value


def tail_plain(turned, raw_low, levels, factors, places, v):
    virtuals = levels.shape[0]
    pair_ints = contract(jnp.concatenate(turned, 0), jnp.concatenate(raw_low, 0), 1, 1)
    amplitude = pair_ints / (levels[:, None] + levels[None, :] - factors[0])
    value = jnp.sum(pair_ints * (2.0 * amplitude - amplitude.T)) * factors[1]
    order = (places[:, None] + jnp.arange(v)[None, :]).reshape(virtuals)
    amplitude = amplitude[order][:, order]
    blocks = []
    for at in range(0, virtuals, v):
        row = contract(amplitude[at : at + v], amplitude[at:], 1, 1)
        row = row + contract(amplitude[:, at : at + v], amplitude[:, at:], 0, 0)
        blocks += jnp.split(row * factors[2], (virtuals - at) // v, 1)
    return [piece for block in blocks for piece in jnp.split(block, v // piece_rows(v), 0)], value


def assembled_kernel(v, pairs, index, *refs):
    pieces, out = refs[:-1], refs[-1]
    each = len(pieces) // len(pairs)
    tiles = out.shape[1] // v
    for m in range(tiles):

        @pl.when(index[0] == m)
        def _():
            for b in range(tiles):
                k = pairs.index((min(m, b), max(m, b))) * each
                block = jnp.concatenate([one[...] for one in pieces[k : k + each]], 0)
                out[:, b * v : (b + 1) * v] = block.T if m > b else block


def assembled(pieces, pairs, n, v, narrow):
    return pl.pallas_call(
        functools.partial(assembled_kernel, v, pairs),
        out_shape=jax.ShapeDtypeStruct((v, v * narrow), jnp.float32),
        in_specs=[pl.BlockSpec(memory_space=SMEM)] + [pl.BlockSpec(memory_space=VMEM)] * len(pieces),
        out_specs=pl.BlockSpec(memory_space=VMEM),
        name="assembled",
    )(n.reshape(1), *pieces)


def assembled_plain(pieces, pairs, n, v, narrow):
    each = len(pieces) // len(pairs)
    full = [jnp.concatenate(pieces[k * each : (k + 1) * each], 0) for k in range(len(pairs))]
    columns = []
    for b in range(narrow):
        cases = []
        for m in range(narrow):
            block = full[pairs.index((min(m, b), max(m, b)))]
            cases.append(block.T if m > b else block)
        columns.append(lax.select_n(n, *cases))
    return jnp.concatenate(columns, 1)


def on_device(raw_ints, metric, occ_energy, vir_energy, pair_kept):
    wide, narrow = lax.axis_size("wide"), lax.axis_size("narrow")
    w, n = lax.axis_index("wide"), lax.axis_index("narrow")
    v = raw_ints.shape[1]
    virtuals = v * narrow

    near = 4
    count = metric.shape[0] // near
    chunks = [(0, v // 2), (v // 2, v // 4), (3 * v // 4, v // 4)]
    piece = lax.dynamic_slice_in_dim(metric, (w % near) * count, count, 0)
    own = lax.dynamic_index_in_dim(raw_ints, n, 0, keepdims=False)

    far = [passed_along(piece, "narrow", s) for s in range(1, narrow)]
    raw_low = [passed_along(own, "wide", 1)]
    arrived, gives = [], []
    for s in range(1, narrow):
        given = lax.dynamic_index_in_dim(raw_ints, (n + s) % narrow, 0, keepdims=False)
        parts = [given[first : first + rows] for first, rows in chunks]
        gives += parts
        arrived += [passed_along(one, "narrow", s) for one in reversed(parts)][::-1]
    lower_energy = passed_along(occ_energy, "wide", 1)
    fit = near_fit(after(own, *gives), metric)
    far = [after(one, fit) for one in far]
    far_x = [swapped(one, "wide", 2) for one in far]
    far_core = [swapped(one, "wide", 1) for one in far]
    raw_low += [passed_along(one, "wide", 1) for one in arrived[:-1]]
    far_x = [after(one, raw_low[0], arrived[0]) for one in far_x]
    far_last = [swapped(one, "wide", 1) for one in far_x]
    pieces = [metric] + far + far_core + far_x + far_last

    turned = [turn([own], pieces, fit)]
    raw_low.append(passed_along(after(arrived[-1], turned[0], raw_low[1]), "wide", 1))
    turned.append(turn(arrived, pieces))

    levels = jnp.concatenate(
        [lax.dynamic_slice_in_dim(vir_energy, ((n - s) % narrow) * v, v, 0) for s in range(narrow)]
    )
    kept = pair_kept[0].astype(jnp.float32)
    factors = jnp.stack(
        [
            occ_energy[0] + lower_energy[0],
            -kept / (virtuals * virtuals),
            kept * (0.0625 / (wide * narrow)),
        ]
    )
    pairs = [(a, b) for a in range(narrow) for b in range(a, narrow)]
    places = jnp.stack([(n - a) % narrow * v for a in range(narrow)])
    form, joined = (tail, assembled) if v % 128 == 0 else (tail_plain, assembled_plain)
    blocks, own_value = form(turned, raw_low, levels, factors, places, v)

    place = w * narrow + n
    values = jnp.where(jnp.arange(wide * narrow) == place, own_value.reshape(()), 0.0)
    *blocks, values = lax.psum((*blocks, values), ("wide", "narrow"))
    partner = lax.dynamic_index_in_dim(values, (place + narrow) % (wide * narrow), 0)
    energy = lax.dynamic_index_in_dim(values, place, 0) + partner

    return joined(blocks, pairs, n, v, narrow), energy


def solution(mesh):
    placed = (
        P("wide", "narrow", None),
        P("narrow", None),
        P(("wide", "narrow")),
        P(),
        P(("wide", "narrow")),
    )
    return jax.shard_map(
        on_device,
        mesh=mesh,
        in_specs=placed,
        out_specs=(P("narrow", None), P(("wide", "narrow"))),
        check_vma=False,
    )
```

```python
import functools

import jax
import jax.numpy as jnp
from jax import lax
from jax.experimental import pallas as pl
from jax.experimental.pallas import tpu as pltpu
from jax.sharding import PartitionSpec as P

PASSES = lax.Precision.HIGH
SMEM = pltpu.MemorySpace.SMEM
VMEM = pltpu.MemorySpace.VMEM
NEAR_COST = 15_000_000_000


def contract(left, right, left_dim, right_dim):
    return lax.dot_general(
        left,
        right,
        (((left_dim,), (right_dim,)), ((), ())),
        precision=PASSES,
        preferred_element_type=jnp.float32,
    )


def passed_along(shard, axis, by):
    size = lax.axis_size(axis)
    return lax.ppermute(shard, axis, [(i, (i + by) % size) for i in range(size)])


def swapped(shard, axis, bit):
    size = lax.axis_size(axis)
    return lax.ppermute(shard, axis, [(i, i ^ bit) for i in range(size)])


def after(value, *gates):
    return lax.optimization_barrier((value,) + gates)[0]


def in_vmem(count):
    return [pl.BlockSpec(memory_space=VMEM)] * count


def limit(mib):
    return pltpu.CompilerParams(vmem_limit_bytes=mib * 2**20)


def cost(flops):
    return pl.CostEstimate(flops=flops, bytes_accessed=0, transcendentals=0)


def cut_kernel(cuts, near, narrow, raw, metric, *outs):
    part = lax.rem(lax.axis_index("wide"), near)
    n = lax.axis_index("narrow")
    for out, (shift, first, rows) in zip(outs, cuts):
        if shift is None:
            out[...] = metric[pl.ds(pl.multiple_of(part * rows, rows), rows), :]
        else:
            out[...] = raw[lax.rem(n + shift, narrow), first : first + rows, :]


def cut(raw, metric, cuts, near, narrow):
    width = raw.shape[2]
    return pl.pallas_call(
        functools.partial(cut_kernel, cuts, near, narrow),
        out_shape=[like(rows, width, jnp.float32) for *_, rows in cuts],
        in_specs=in_vmem(2),
        out_specs=in_vmem(len(cuts)),
        compiler_params=limit(8),
        name="cut",
    )(raw, metric)


def halves(value):
    high = value.astype(jnp.bfloat16)
    low = (value - high.astype(jnp.float32)).astype(jnp.bfloat16)
    return high, low


def dot3(left, right, right_dim):
    (lh, ll), (rh, rl) = left, right
    dims = (((1,), (right_dim,)), ((), ()))
    total = lax.dot_general(ll, rh, dims, preferred_element_type=jnp.float32)
    total += lax.dot_general(lh, rl, dims, preferred_element_type=jnp.float32)
    return total + lax.dot_general(lh, rh, dims, preferred_element_type=jnp.float32)


def stacked(refs):
    return jnp.concatenate([one[...] for one in refs], 0)


def like(rows, width, dtype):
    return jax.ShapeDtypeStruct((rows, width), dtype)


def near_fit_kernel(rows, metric, fit_high, fit_low, high, low):
    parts = halves(metric[...])
    high[...], low[...] = parts
    fit_high[...], fit_low[...] = halves(dot3(halves(rows[...]), parts, 1))


def near_fit(rows, metric):
    (count, width), near = rows.shape, metric.shape[0]
    return pl.pallas_call(
        near_fit_kernel,
        out_shape=[like(count, near, jnp.bfloat16)] * 2 + [like(near, width, jnp.bfloat16)] * 2,
        in_specs=in_vmem(2),
        out_specs=in_vmem(4),
        compiler_params=limit(16),
        cost_estimate=cost(NEAR_COST),
        name="near_fit",
    )(rows, metric)


def turn_own_kernel(rows, fit_high, fit_low, near_high, near_low, *refs):
    pieces, (out_high, out_low, high, low) = refs[:-4], refs[-4:]
    parts = halves(stacked(pieces))
    high[...], low[...] = parts
    fit = halves(dot3(halves(rows[...]), parts, 1))
    total = dot3(fit, parts, 0)
    total += dot3((fit_high[...], fit_low[...]), (near_high[...], near_low[...]), 0)
    out_high[...], out_low[...] = halves(total)


def turn_own(rows, near, pieces):
    (count, width), far = rows.shape, sum(piece.shape[0] for piece in pieces)
    return pl.pallas_call(
        turn_own_kernel,
        out_shape=[like(count, width, jnp.bfloat16)] * 2 + [like(far, width, jnp.bfloat16)] * 2,
        in_specs=in_vmem(5 + len(pieces)),
        out_specs=in_vmem(4),
        compiler_params=limit(20),
        cost_estimate=cost(12 * count * far * width),
        name="turn_own",
    )(rows, *near, *pieces)


def turn_kernel(near_high, near_low, far_high, far_low, *refs):
    cuts, (out_high, out_low) = refs[:-2], refs[-2:]
    rows = halves(stacked(cuts))
    total = 0
    for parts in ((near_high[...], near_low[...]), (far_high[...], far_low[...])):
        total += dot3(halves(dot3(rows, parts, 1)), parts, 0)
    out_high[...], out_low[...] = halves(total)


def turn(cuts, near, far):
    count, width = sum(one.shape[0] for one in cuts), cuts[0].shape[1]
    return pl.pallas_call(
        turn_kernel,
        out_shape=[like(count, width, jnp.bfloat16)] * 2,
        in_specs=in_vmem(4 + len(cuts)),
        out_specs=in_vmem(2),
        compiler_params=limit(20),
        cost_estimate=cost(12 * count * width * (near[0].shape[0] + far[0].shape[0])),
        name="turn",
    )(*near, *far, *cuts)


def tail_kernel(v, tiles, factors, col, row, own_high, own_low, far_high, far_low, *refs):
    lows, (first, second, value), scratch = refs[:-9], refs[-9:-6], refs[-6:]
    amp, amp_t, high, low, high_t, low_t = scratch
    n = lax.axis_index("narrow")
    virtuals = v * tiles
    spot = [slice(p * v, (p + 1) * v) for p in range(tiles)]
    right = halves(stacked(lows))
    total = jnp.float32(0)
    left = (own_high[...], own_low[...]), (far_high[...], far_low[...])
    pairs = [dot3(left[0], right, 1), dot3(left[1], right, 1)]
    for pair, at in zip(pairs, (slice(0, v), slice(v, virtuals))):
        amp[at, :] = pair / (col[at, :] + row[...] - factors[0])
    amp_t[...] = amp[...].T
    for pair, at in zip(pairs, (slice(0, v), slice(v, virtuals))):
        total += jnp.sum(pair * (2.0 * amp[at, :] - amp_t[at, :]))
    value[0, 0] = total * factors[1]
    high[...], low[...] = halves(amp[...])
    high_t[...], low_t[...] = halves(amp_t[...])
    at = [pl.ds(pl.multiple_of(lax.rem(n - a + tiles, tiles) * v, v), v) for a in range(tiles)]
    k = 0
    for a in range(tiles):
        for b in range(a, tiles):
            block = dot3((high[at[a], :], low[at[a], :]), (high_t[:, at[b]], low_t[:, at[b]]), 0)
            block += dot3((high_t[at[a], :], low_t[at[a], :]), (high[:, at[b]], low[:, at[b]]), 0)
            block *= factors[2]
            first[k], second[k] = block[:, : v // 2], block[:, v // 2 :]
            k += 1


def tail(turned, raw_low, levels, factors, v):
    virtuals, width = levels.shape[0], raw_low[0].shape[1]
    tiles = virtuals // v
    count = tiles * (tiles + 1) // 2
    half = jax.ShapeDtypeStruct((count, v, v // 2), jnp.float32)
    square = [pltpu.VMEM((virtuals, virtuals), kind) for kind in (jnp.float32, jnp.bfloat16)]
    return pl.pallas_call(
        functools.partial(tail_kernel, v, tiles),
        out_shape=[half, half, jax.ShapeDtypeStruct((1, 1), jnp.float32)],
        in_specs=[pl.BlockSpec(memory_space=SMEM)] + in_vmem(6 + len(raw_low)),
        out_specs=in_vmem(2) + [pl.BlockSpec(memory_space=SMEM)],
        scratch_shapes=[square[0]] * 2 + [square[1]] * 4,
        compiler_params=limit(24),
        cost_estimate=cost(6 * virtuals * virtuals * width + 12 * count * v * v * virtuals),
        name="tail",
    )(factors, levels[:, None], levels[None, :], *turned, *raw_low)


def tail_plain(turned, raw_low, levels, factors, v):
    virtuals = levels.shape[0]
    narrow = virtuals // v
    n = lax.axis_index("narrow")
    own_high, own_low, far_high, far_low = [one.astype(jnp.float32) for one in turned]
    left = jnp.concatenate([own_high + own_low, far_high + far_low], 0)
    pair_ints = contract(left, jnp.concatenate(raw_low, 0), 1, 1)
    amplitude = pair_ints / (levels[:, None] + levels[None, :] - factors[0])
    value = jnp.sum(pair_ints * (2.0 * amplitude - amplitude.T)) * factors[1]
    order = ((n - jnp.arange(narrow)) % narrow * v)[:, None] + jnp.arange(v)[None, :]
    order = order.reshape(virtuals)
    amplitude = amplitude[order][:, order]
    blocks = []
    for at in range(0, virtuals, v):
        row = contract(amplitude[at : at + v], amplitude[at:], 1, 1)
        row = row + contract(amplitude[:, at : at + v], amplitude[:, at:], 0, 0)
        blocks += jnp.split(row * factors[2], (virtuals - at) // v, 1)
    whole = jnp.stack(blocks)
    return whole[:, :, : v // 2], whole[:, :, v // 2 :], value.reshape(1, 1)


def halved(blocks, w, bit):
    half = blocks.shape[1] // 2
    side = (w // bit) % 2
    kept = lax.dynamic_slice_in_dim(blocks, side * half, half, 1)
    given = lax.dynamic_slice_in_dim(blocks, (1 - side) * half, half, 1)
    return kept + swapped(given, "wide", bit)


def doubled(blocks, w, bit):
    other = swapped(blocks, "wide", bit)
    low = (w // bit) % 2 == 0
    return jnp.concatenate([jnp.where(low, blocks, other), jnp.where(low, other, blocks)], 1)


def own_rows(blocks, pairs, n, narrow):
    def of(m):
        picked = []
        for b in range(narrow):
            spots = [pairs.index((min(a, b), max(a, b))) for a in range(narrow)]
            picked.append(lax.select_n(m, *[blocks[k] for k in spots]))
        return jnp.stack(picked)

    total = of(n)
    for s in range(1, narrow):
        total = total + passed_along(of((n + s) % narrow), "narrow", s)
    return total


def on_device(raw_ints, metric, occ_energy, vir_energy, pair_kept):
    wide, narrow = lax.axis_size("wide"), lax.axis_size("narrow")
    w, n = lax.axis_index("wide"), lax.axis_index("narrow")
    v = raw_ints.shape[1]
    virtuals = v * narrow

    near = 4
    chunks = [(0, 5 * v // 8), (5 * v // 8, 3 * v // 8)]
    cuts = [(None, 0, metric.shape[0] // near), (0, 0, v)]
    cuts += [(s, first, rows) for s in range(1, narrow) for first, rows in chunks]
    piece, own, *given = cut(raw_ints, metric, cuts, near, narrow)

    far = [passed_along(piece, "narrow", s) for s in range(1, narrow)]
    raw_low = [passed_along(own, "wide", 1)]
    arrived = []
    for k in range(0, len(given), len(chunks)):
        parts = given[k : k + len(chunks)]
        arrived += [passed_along(one, "narrow", 1 + k // len(chunks)) for one in reversed(parts)][::-1]
    lower_energy = passed_along(occ_energy, "wide", 1)
    fit_near = near_fit(own, metric)
    far = [after(one, fit_near[0]) for one in far]
    far_x = [swapped(one, "wide", 2) for one in far]
    far_core = [swapped(one, "wide", 1) for one in far]
    raw_low += [passed_along(one, "wide", 1) for one in arrived[:-1]]
    far_x = [after(one, raw_low[0]) for one in far_x]
    far_last = [swapped(one, "wide", 1) for one in far_x]

    *own_turned, far_high, far_low = turn_own(own, fit_near, far + far_core + far_x + far_last)
    raw_low.append(passed_along(after(arrived[-1], own_turned[0]), "wide", 1))
    turned = [*own_turned, *turn(arrived, fit_near[2:], (far_high, far_low))]

    levels = jnp.concatenate(
        [lax.dynamic_slice_in_dim(vir_energy, ((n - s) % narrow) * v, v, 0) for s in range(narrow)]
    )
    kept = pair_kept[0].astype(jnp.float32)
    factors = jnp.stack(
        [
            occ_energy[0] + lower_energy[0],
            -kept / (virtuals * virtuals),
            kept * (0.0625 / (wide * narrow)),
        ]
    )
    pairs = [(a, b) for a in range(narrow) for b in range(a, narrow)]
    form = tail if v % 256 == 0 else tail_plain
    *parts, own_value = form(turned, raw_low, levels, factors, v)
    own_value = own_value.reshape(1)
    upper_value = passed_along(own_value, "wide", -1)

    bits = [1 << k for k in range(wide.bit_length() - 1)]
    orders = [bits, bits[:1] + bits[2:] + bits[1:2]]
    for step in range(len(bits)):
        parts = [halved(part, w, order[step]) for part, order in zip(parts, orders)]
        if step == 1:
            parts[0], upper_value = lax.optimization_barrier((parts[0], upper_value))
    parts = [own_rows(part, pairs, n, narrow) for part in parts]
    for step in reversed(range(len(bits))):
        parts = [doubled(part, w, order[step]) for part, order in zip(parts, orders)]
    full = jnp.concatenate(parts, 2)
    columns = []
    for b in range(narrow):
        cases = [full[b].T if m > b else full[b] for m in range(narrow)]
        columns.append(lax.select_n(n, *cases))
    return jnp.concatenate(columns, 1), own_value + upper_value


def solution(mesh):
    placed = (
        P("wide", "narrow", None),
        P("narrow", None),
        P(("wide", "narrow")),
        P(),
        P(("wide", "narrow")),
    )
    return jax.shard_map(
        on_device,
        mesh=mesh,
        in_specs=placed,
        out_specs=(P("narrow", None), P(("wide", "narrow"))),
        check_vma=False,
    )
```

```python
import functools

import jax
import jax.numpy as jnp
from jax import lax
from jax.experimental import pallas as pl
from jax.experimental.pallas import tpu as pltpu
from jax.sharding import PartitionSpec as P

PASSES = lax.Precision.HIGH
VMEM = pltpu.MemorySpace.VMEM
NEAR_COST = 15_000_000_000


def contract(left, right, left_dim, right_dim):
    return lax.dot_general(
        left,
        right,
        (((left_dim,), (right_dim,)), ((), ())),
        precision=PASSES,
        preferred_element_type=jnp.float32,
    )


def passed_along(shard, axis, by):
    size = lax.axis_size(axis)
    return lax.ppermute(shard, axis, [(i, (i + by) % size) for i in range(size)])


def swapped(shard, axis, bit):
    size = lax.axis_size(axis)
    return lax.ppermute(shard, axis, [(i, i ^ bit) for i in range(size)])


def after(value, *gates):
    return lax.optimization_barrier((value,) + gates)[0]


def in_vmem(count):
    return [pl.BlockSpec(memory_space=VMEM)] * count


def limit(mib):
    return pltpu.CompilerParams(vmem_limit_bytes=mib * 2**20)


def cost(flops):
    return pl.CostEstimate(flops=flops, bytes_accessed=0, transcendentals=0)


def halves(value):
    high = value.astype(jnp.bfloat16)
    low = (value - high.astype(jnp.float32)).astype(jnp.bfloat16)
    return high, low


def dot3(left, right, right_dim):
    (lh, ll), (rh, rl) = left, right
    dims = (((1,), (right_dim,)), ((), ()))
    total = lax.dot_general(ll, rh, dims, preferred_element_type=jnp.float32)
    total += lax.dot_general(lh, rl, dims, preferred_element_type=jnp.float32)
    return total + lax.dot_general(lh, rh, dims, preferred_element_type=jnp.float32)


def stacked(refs):
    return jnp.concatenate([one[...] for one in refs], 0)


def like(rows, width, dtype):
    return jax.ShapeDtypeStruct((rows, width), dtype)


def near_fit_kernel(rows, metric, occ, kept, fit_high, fit_low, high, low, occ_tile, kept_tile):
    parts = halves(metric[...])
    high[...], low[...] = parts
    fit_high[...], fit_low[...] = halves(dot3(halves(rows[...]), parts, 1))
    occ_tile[...] = jnp.broadcast_to(occ[...], occ_tile.shape)
    kept_tile[...] = jnp.broadcast_to(kept[...].astype(jnp.float32), kept_tile.shape)


def near_fit(rows, metric, occ, kept):
    (count, width), near = rows.shape, metric.shape[0]
    return pl.pallas_call(
        near_fit_kernel,
        out_shape=[like(count, near, jnp.bfloat16)] * 2
        + [like(near, width, jnp.bfloat16)] * 2
        + [like(8, 128, jnp.float32)] * 2,
        in_specs=in_vmem(4),
        out_specs=in_vmem(6),
        compiler_params=limit(16),
        cost_estimate=cost(NEAR_COST),
        name="near_fit",
    )(rows, metric, occ[None, :], kept[None, :])


def turn_own_kernel(rows, fit_high, fit_low, near_high, near_low, *refs):
    pieces, (out_high, out_low, high, low) = refs[:-4], refs[-4:]
    parts = halves(stacked(pieces))
    high[...], low[...] = parts
    fit = halves(dot3(halves(rows[...]), parts, 1))
    total = dot3(fit, parts, 0)
    total += dot3((fit_high[...], fit_low[...]), (near_high[...], near_low[...]), 0)
    out_high[...], out_low[...] = halves(total)


def turn_own(rows, near, pieces):
    (count, width), far = rows.shape, sum(piece.shape[0] for piece in pieces)
    return pl.pallas_call(
        turn_own_kernel,
        out_shape=[like(count, width, jnp.bfloat16)] * 2 + [like(far, width, jnp.bfloat16)] * 2,
        in_specs=in_vmem(5 + len(pieces)),
        out_specs=in_vmem(4),
        compiler_params=limit(20),
        cost_estimate=cost(12 * count * far * width),
        name="turn_own",
    )(rows, *near, *pieces)


def turn_kernel(near_high, near_low, far_high, far_low, *refs):
    cuts, (out_high, out_low) = refs[:-2], refs[-2:]
    rows = halves(stacked(cuts))
    total = 0
    for parts in ((near_high[...], near_low[...]), (far_high[...], far_low[...])):
        total += dot3(halves(dot3(rows, parts, 1)), parts, 0)
    out_high[...], out_low[...] = halves(total)


def turn(cuts, near, far):
    count, width = sum(one.shape[0] for one in cuts), cuts[0].shape[1]
    return pl.pallas_call(
        turn_kernel,
        out_shape=[like(count, width, jnp.bfloat16)] * 2,
        in_specs=in_vmem(4 + len(cuts)),
        out_specs=in_vmem(2),
        compiler_params=limit(20),
        cost_estimate=cost(12 * count * width * (near[0].shape[0] + far[0].shape[0])),
        name="turn",
    )(*near, *far, *cuts)


def tail_kernel(v, tiles, scale, occ, low_occ, kept, vir, own_high, own_low, far_high, far_low, *refs):
    lows, (blocks, value), scratch = refs[:-8], refs[-8:-6], refs[-6:]
    amp, amp_t, high, low, high_t, low_t = scratch
    n = lax.axis_index("narrow")
    virtuals = v * tiles
    at = [pl.ds(pl.multiple_of(lax.rem(n - a + tiles, tiles) * v, v), v) for a in range(tiles)]
    row = jnp.concatenate([vir[:, one] for one in at], 1)
    col = jnp.broadcast_to(row, (128, virtuals)).T[:, :1]
    gap = occ[:1, :1] + low_occ[:1, :1]
    weight = kept[:1, :1]
    right = halves(stacked(lows))
    left = (own_high[...], own_low[...]), (far_high[...], far_low[...])
    pairs = [dot3(one, right, 1) for one in left]
    spans = slice(0, v), slice(v, virtuals)
    for pair, span in zip(pairs, spans):
        amp[span, :] = pair / (col[span, :] + row - gap)
    amp_t[...] = amp[...].T
    total = jnp.float32(0)
    for pair, span in zip(pairs, spans):
        total += jnp.sum(pair * (2.0 * amp[span, :] - amp_t[span, :]))
    value[...] = -weight * total / (virtuals * virtuals)
    high[...], low[...] = halves(amp[...])
    high_t[...], low_t[...] = halves(amp_t[...])
    k = 0
    for a in range(tiles):
        for b in range(a, tiles):
            block = dot3((high[at[a], :], low[at[a], :]), (high_t[:, at[b]], low_t[:, at[b]]), 0)
            block += dot3((high_t[at[a], :], low_t[at[a], :]), (high[:, at[b]], low[:, at[b]]), 0)
            blocks[k] = block * (weight * scale)
            k += 1


def tail(turned, raw_low, energies, v, scale):
    virtuals, width = energies[-1].shape[0], raw_low[0].shape[1]
    tiles = virtuals // v
    count = tiles * (tiles + 1) // 2
    square = [pltpu.VMEM((virtuals, virtuals), kind) for kind in (jnp.float32, jnp.bfloat16)]
    return pl.pallas_call(
        functools.partial(tail_kernel, v, tiles, scale),
        out_shape=[
            jax.ShapeDtypeStruct((count, v, v), jnp.float32),
            jax.ShapeDtypeStruct((1, 1), jnp.float32),
        ],
        in_specs=in_vmem(8 + len(raw_low)),
        out_specs=in_vmem(2),
        scratch_shapes=[square[0]] * 2 + [square[1]] * 4,
        compiler_params=limit(24),
        cost_estimate=cost(6 * virtuals * virtuals * width + 12 * count * v * v * virtuals),
        name="tail",
    )(*energies[:-1], energies[-1][None, :], *turned, *raw_low)


def tail_plain(turned, raw_low, energies, v, scale):
    occ, low_occ, kept, vir = energies
    virtuals = vir.shape[0]
    narrow = virtuals // v
    order = ((lax.axis_index("narrow") - jnp.arange(narrow)) % narrow * v)[:, None] + jnp.arange(v)[None, :]
    order = order.reshape(virtuals)
    weight = kept[0, 0]
    levels = vir[order]
    own_high, own_low, far_high, far_low = [one.astype(jnp.float32) for one in turned]
    left = jnp.concatenate([own_high + own_low, far_high + far_low], 0)
    pair_ints = contract(left, jnp.concatenate(raw_low, 0), 1, 1)
    amplitude = pair_ints / (levels[:, None] + levels[None, :] - occ[0, 0] - low_occ[0, 0])
    value = jnp.sum(pair_ints * (2.0 * amplitude - amplitude.T)) * -weight / (virtuals * virtuals)
    amplitude = amplitude[order][:, order]
    blocks = []
    for at in range(0, virtuals, v):
        row = contract(amplitude[at : at + v], amplitude[at:], 1, 1)
        row = row + contract(amplitude[:, at : at + v], amplitude[:, at:], 0, 0)
        blocks += jnp.split(row * (weight * scale), (virtuals - at) // v, 1)
    return jnp.stack(blocks), value.reshape(1, 1)


def halved(blocks, w, bit):
    half = blocks.shape[1] // 2
    side = (w // bit) % 2
    kept = lax.dynamic_slice_in_dim(blocks, side * half, half, 1)
    given = lax.dynamic_slice_in_dim(blocks, (1 - side) * half, half, 1)
    return kept + swapped(given, "wide", bit)


def doubled(blocks, w, bit):
    other = swapped(blocks, "wide", bit)
    low = (w // bit) % 2 == 0
    return jnp.concatenate([jnp.where(low, blocks, other), jnp.where(low, other, blocks)], 1)


def own_rows(blocks, pairs, n, bit):
    wide, narrow = lax.axis_size("wide"), lax.axis_size("narrow")

    def of(m):
        picked = []
        for b in range(narrow):
            spots = [pairs.index((min(a, b), max(a, b))) for a in range(narrow)]
            picked.append(lax.select_n(m, *[blocks[k] for k in spots]))
        return jnp.stack(picked)

    total = of(n)
    for s in range(narrow):
        given = of((n + s) % narrow)
        for flip in (0, bit):
            if s or flip:
                steps = [
                    (w * narrow + m, (w ^ flip) * narrow + (m + s) % narrow)
                    for w in range(wide)
                    for m in range(narrow)
                ]
                total = total + lax.ppermute(given, ("wide", "narrow"), steps)
    return total


def on_device(raw_ints, metric, occ_energy, vir_energy, pair_kept):
    wide, narrow = lax.axis_size("wide"), lax.axis_size("narrow")
    w, n = lax.axis_index("wide"), lax.axis_index("narrow")
    v = raw_ints.shape[1]
    virtuals = v * narrow

    near = 4
    chunks = [(0, 5 * v // 8), (5 * v // 8, 3 * v // 8)]
    rows = metric.shape[0] // near
    piece = lax.dynamic_slice_in_dim(metric, (w % near) * rows, rows, 0)
    far = [passed_along(piece, "narrow", s) for s in range(1, narrow)]
    own = lax.dynamic_index_in_dim(raw_ints, n, 0, keepdims=False)
    raw_low = [passed_along(own, "wide", 1)]
    arrived, given = [], []
    for s in range(1, narrow):
        block = lax.dynamic_index_in_dim(raw_ints, (n + s) % narrow, 0, keepdims=False)
        parts = [block[first : first + rows] for first, rows in chunks]
        arrived += [passed_along(one, "narrow", s) for one in reversed(parts)][::-1]
        given += parts
    *fit_near, occ, kept = near_fit(after(own, *given), metric, occ_energy, pair_kept)
    low_occ = passed_along(occ, "wide", 1)
    far = [after(one, fit_near[0]) for one in far]
    far_x = [swapped(one, "wide", 2) for one in far]
    far_core = [swapped(one, "wide", 1) for one in far]
    raw_low += [passed_along(one, "wide", 1) for one in arrived[:-1]]
    far_x = [after(one, raw_low[0]) for one in far_x]
    far_last = [swapped(one, "wide", 1) for one in far_x]

    *own_turned, far_high, far_low = turn_own(own, fit_near, far + far_core + far_x + far_last)
    raw_low.append(passed_along(after(arrived[-1], own_turned[0]), "wide", 1))
    turned = [*own_turned, *turn(arrived, fit_near[2:], (far_high, far_low))]

    pairs = [(a, b) for a in range(narrow) for b in range(a, narrow)]
    form = tail if v % 128 == 0 else tail_plain
    energies = occ, low_occ, kept, vir_energy
    blocks, own_value = form(turned, raw_low, energies, v, 0.0625 / (wide * narrow))
    blocks, own_value, w, n = lax.optimization_barrier((blocks, own_value, w, n))
    own_value = own_value.reshape(1)
    upper_value = passed_along(own_value, "wide", -1)

    *bits, last = [1 << k for k in range(wide.bit_length() - 1)]
    for bit in bits:
        blocks = halved(blocks, w, bit)
        if bit == 2:
            blocks, upper_value = lax.optimization_barrier((blocks, upper_value))
    full = own_rows(blocks, pairs, n, last)
    for bit in reversed(bits):
        full = doubled(full, w, bit)
    columns = []
    for b in range(narrow):
        cases = [full[b].T if m > b else full[b] for m in range(narrow)]
        columns.append(lax.select_n(n, *cases))
    return jnp.concatenate(columns, 1), own_value + upper_value


def solution(mesh):
    placed = (
        P("wide", "narrow", None),
        P("narrow", None),
        P(("wide", "narrow")),
        P(),
        P(("wide", "narrow")),
    )
    return jax.shard_map(
        on_device,
        mesh=mesh,
        in_specs=placed,
        out_specs=(P("narrow", None), P(("wide", "narrow"))),
        check_vma=False,
    )
```

```python
import functools

import jax
import jax.numpy as jnp
from jax import lax
from jax.experimental import pallas as pl
from jax.experimental.pallas import tpu as pltpu
from jax.sharding import PartitionSpec as P

PASSES = lax.Precision.HIGH
VMEM = pltpu.MemorySpace.VMEM
NEAR_COST = 15_000_000_000


def contract(left, right, left_dim, right_dim):
    return lax.dot_general(
        left,
        right,
        (((left_dim,), (right_dim,)), ((), ())),
        precision=PASSES,
        preferred_element_type=jnp.float32,
    )


def passed_along(shard, axis, by):
    size = lax.axis_size(axis)
    return lax.ppermute(shard, axis, [(i, (i + by) % size) for i in range(size)])


def swapped(shard, axis, bit):
    size = lax.axis_size(axis)
    return lax.ppermute(shard, axis, [(i, i ^ bit) for i in range(size)])


def after(value, *gates):
    return lax.optimization_barrier((value,) + gates)[0]


def in_vmem(count):
    return [pl.BlockSpec(memory_space=VMEM)] * count


def limit(mib):
    return pltpu.CompilerParams(vmem_limit_bytes=mib * 2**20)


def cost(flops):
    return pl.CostEstimate(flops=flops, bytes_accessed=0, transcendentals=0)


def halves(value):
    high = value.astype(jnp.bfloat16)
    low = (value - high.astype(jnp.float32)).astype(jnp.bfloat16)
    return high, low


def dot3(left, right, right_dim):
    (lh, ll), (rh, rl) = left, right
    dims = (((1,), (right_dim,)), ((), ()))
    total = lax.dot_general(ll, rh, dims, preferred_element_type=jnp.float32)
    total += lax.dot_general(lh, rl, dims, preferred_element_type=jnp.float32)
    return total + lax.dot_general(lh, rh, dims, preferred_element_type=jnp.float32)


def stacked(refs):
    return jnp.concatenate([one[...] for one in refs], 0)


def like(rows, width, dtype):
    return jax.ShapeDtypeStruct((rows, width), dtype)


def near_fit_kernel(rows, metric, occ, kept, fit_high, fit_low, high, low, occ_tile, kept_tile):
    parts = halves(metric[...])
    high[...], low[...] = parts
    fit_high[...], fit_low[...] = halves(dot3(halves(rows[...]), parts, 1))
    occ_tile[...] = jnp.broadcast_to(occ[...], occ_tile.shape)
    kept_tile[...] = jnp.broadcast_to(kept[...].astype(jnp.float32), kept_tile.shape)


def near_fit(rows, metric, occ, kept):
    (count, width), near = rows.shape, metric.shape[0]
    return pl.pallas_call(
        near_fit_kernel,
        out_shape=[like(count, near, jnp.bfloat16)] * 2
        + [like(near, width, jnp.bfloat16)] * 2
        + [like(8, 128, jnp.float32)] * 2,
        in_specs=in_vmem(4),
        out_specs=in_vmem(6),
        compiler_params=limit(16),
        cost_estimate=cost(NEAR_COST),
        name="near_fit",
    )(rows, metric, occ[None, :], kept[None, :])


def turn_own_kernel(rows, fit_high, fit_low, near_high, near_low, *refs):
    pieces, (out_high, out_low, high, low) = refs[:-4], refs[-4:]
    parts = halves(stacked(pieces))
    high[...], low[...] = parts
    fit = halves(dot3(halves(rows[...]), parts, 1))
    total = dot3(fit, parts, 0)
    total += dot3((fit_high[...], fit_low[...]), (near_high[...], near_low[...]), 0)
    out_high[...], out_low[...] = halves(total)


def turn_own(rows, near, pieces):
    (count, width), far = rows.shape, sum(piece.shape[0] for piece in pieces)
    return pl.pallas_call(
        turn_own_kernel,
        out_shape=[like(count, width, jnp.bfloat16)] * 2 + [like(far, width, jnp.bfloat16)] * 2,
        in_specs=in_vmem(5 + len(pieces)),
        out_specs=in_vmem(4),
        compiler_params=limit(20),
        cost_estimate=cost(12 * count * far * width),
        name="turn_own",
    )(rows, *near, *pieces)


def turn_kernel(near_high, near_low, far_high, far_low, *refs):
    cuts, (out_high, out_low) = refs[:-2], refs[-2:]
    rows = halves(stacked(cuts))
    total = 0
    for parts in ((near_high[...], near_low[...]), (far_high[...], far_low[...])):
        total += dot3(halves(dot3(rows, parts, 1)), parts, 0)
    out_high[...], out_low[...] = halves(total)


def turn(cuts, near, far):
    count, width = sum(one.shape[0] for one in cuts), cuts[0].shape[1]
    return pl.pallas_call(
        turn_kernel,
        out_shape=[like(count, width, jnp.bfloat16)] * 2,
        in_specs=in_vmem(4 + len(cuts)),
        out_specs=in_vmem(2),
        compiler_params=limit(20),
        cost_estimate=cost(12 * count * width * (near[0].shape[0] + far[0].shape[0])),
        name="turn",
    )(*near, *far, *cuts)


def spots_of(tiles):
    pairs = []
    for a in range(tiles):
        for b in range(a, tiles):
            halves_of = [(2 * a + r, 2 * b + c) for r in (0, 1) for c in (0, 1)]
            pairs += [pair for pair in halves_of if pair[0] <= pair[1]]
    return {pair: k for k, pair in enumerate(pairs)}


def row_spots(n, tiles):
    spots = spots_of(tiles)
    return {pair: k for pair, k in spots.items() if pair[0] // 2 == n or pair[1] // 2 == n}


def tail_kernel(v, tiles, scale, occ, low_occ, kept, vir, own_high, own_low, far_high, far_low, *refs):
    lows, (blocks, value), scratch = refs[:-8], refs[-8:-6], refs[-6:]
    amp, amp_t, high, low, high_t, low_t = scratch
    n = lax.axis_index("narrow")
    virtuals = v * tiles
    at = [pl.ds(pl.multiple_of(lax.rem(n - a + tiles, tiles) * v, v), v) for a in range(tiles)]
    row = jnp.concatenate([vir[:, one] for one in at], 1)
    col = jnp.broadcast_to(row, (128, virtuals)).T[:, :1]
    gap = occ[:1, :1] + low_occ[:1, :1]
    weight = kept[:1, :1]
    right = halves(stacked(lows))
    left = (own_high[...], own_low[...]), (far_high[...], far_low[...])
    pairs = [dot3(one, right, 1) for one in left]
    spans = slice(0, v), slice(v, virtuals)
    for pair, span in zip(pairs, spans):
        amp[span, :] = pair / (col[span, :] + row - gap)
    amp_t[...] = amp[...].T
    total = jnp.float32(0)
    for pair, span in zip(pairs, spans):
        total += jnp.sum(pair * (2.0 * amp[span, :] - amp_t[span, :]))
    value[...] = -weight * total / (virtuals * virtuals)
    high[...], low[...] = halves(amp[...])
    high_t[...], low_t[...] = halves(amp_t[...])
    spots, half = spots_of(tiles), v // 2
    for a in range(tiles):
        for b in range(a, tiles):
            block = dot3((high[at[a], :], low[at[a], :]), (high_t[:, at[b]], low_t[:, at[b]]), 0)
            block += dot3((high_t[at[a], :], low_t[at[a], :]), (high[:, at[b]], low[:, at[b]]), 0)
            block *= weight * scale
            for r in (0, 1):
                for c in (0, 1):
                    k = spots.get((2 * a + r, 2 * b + c))
                    if k is not None:
                        blocks[k] = block[r * half : (r + 1) * half, c * half : (c + 1) * half]


def tail(turned, raw_low, energies, v, scale):
    virtuals, width = energies[-1].shape[0], raw_low[0].shape[1]
    tiles = virtuals // v
    count = len(spots_of(tiles))
    square = [pltpu.VMEM((virtuals, virtuals), kind) for kind in (jnp.float32, jnp.bfloat16)]
    return pl.pallas_call(
        functools.partial(tail_kernel, v, tiles, scale),
        out_shape=[
            jax.ShapeDtypeStruct((count, v // 2, v // 2), jnp.float32),
            jax.ShapeDtypeStruct((1, 1), jnp.float32),
        ],
        in_specs=in_vmem(8 + len(raw_low)),
        out_specs=in_vmem(2),
        scratch_shapes=[square[0]] * 2 + [square[1]] * 4,
        compiler_params=limit(24),
        cost_estimate=cost(6 * virtuals * virtuals * width + 3 * count * v * v * virtuals),
        name="tail",
    )(*energies[:-1], energies[-1][None, :], *turned, *raw_low)


def tail_plain(turned, raw_low, energies, v, scale):
    occ, low_occ, kept, vir = energies
    virtuals = vir.shape[0]
    narrow = virtuals // v
    order = ((lax.axis_index("narrow") - jnp.arange(narrow)) % narrow * v)[:, None] + jnp.arange(v)[None, :]
    order = order.reshape(virtuals)
    weight = kept[0, 0]
    levels = vir[order]
    own_high, own_low, far_high, far_low = [one.astype(jnp.float32) for one in turned]
    left = jnp.concatenate([own_high + own_low, far_high + far_low], 0)
    pair_ints = contract(left, jnp.concatenate(raw_low, 0), 1, 1)
    amplitude = pair_ints / (levels[:, None] + levels[None, :] - occ[0, 0] - low_occ[0, 0])
    value = jnp.sum(pair_ints * (2.0 * amplitude - amplitude.T)) * -weight / (virtuals * virtuals)
    amplitude = amplitude[order][:, order]
    blocks, half = [], v // 2
    for at in range(0, virtuals, half):
        row = contract(amplitude[at : at + half], amplitude[at:], 1, 1)
        row = row + contract(amplitude[:, at : at + half], amplitude[:, at:], 0, 0)
        blocks += jnp.split(row * (weight * scale), (virtuals - at) // half, 1)
    return jnp.stack(blocks), value.reshape(1, 1)


def halved(blocks, w, bit):
    half = blocks.shape[1] // 2
    side = (w // bit) % 2
    kept = lax.dynamic_slice_in_dim(blocks, side * half, half, 1)
    given = lax.dynamic_slice_in_dim(blocks, (1 - side) * half, half, 1)
    return kept + swapped(given, "wide", bit)


def doubled(blocks, w, bit):
    other = swapped(blocks, "wide", bit)
    low = (w // bit) % 2 == 0
    return jnp.concatenate([jnp.where(low, blocks, other), jnp.where(low, other, blocks)], 1)


def own_rows(blocks, n, bit):
    wide, narrow = lax.axis_size("wide"), lax.axis_size("narrow")
    spots = [list(row_spots(m, narrow).values()) for m in range(narrow)]

    def of(m):
        picked = [jnp.concatenate([blocks[k : k + 1] for k in row]) for row in spots]
        return lax.select_n(m, *picked)

    total = of(n)
    for s in range(narrow):
        given = of((n + s) % narrow)
        for flip in (0, bit):
            if s or flip:
                steps = [
                    (w * narrow + m, (w ^ flip) * narrow + (m + s) % narrow)
                    for w in range(wide)
                    for m in range(narrow)
                ]
                total = total + lax.ppermute(given, ("wide", "narrow"), steps)
    return total


def row_of(full, m, narrow):
    held = {pair: k for k, pair in enumerate(row_spots(m, narrow))}
    for r in (0, 1):
        for c in range(2 * narrow):
            pair = (2 * m + r, c)
            yield r, c, full[held[pair]] if pair in held else full[held[c, 2 * m + r]].T


def assembled_kernel(narrow, mine, other, out):
    first = lax.rem(lax.axis_index("wide"), 2) == 0
    half = 2 * mine.shape[1]
    whole = jnp.concatenate(
        [jnp.where(first, mine[...], other[...]), jnp.where(first, other[...], mine[...])], 1
    )
    for m in range(narrow):

        @pl.when(lax.axis_index("narrow") == m)
        def _():
            for r, c, block in row_of(whole, m, narrow):
                out[r * half : (r + 1) * half, c * half : (c + 1) * half] = block


def assembled(mine, w, n, narrow):
    other = swapped(mine, "wide", 1)
    half = 2 * mine.shape[1]
    if half % 128 == 0:
        return pl.pallas_call(
            functools.partial(assembled_kernel, narrow),
            out_shape=like(2 * half, 2 * half * narrow, jnp.float32),
            in_specs=in_vmem(2),
            out_specs=in_vmem(1)[0],
            compiler_params=limit(8),
            name="assembled",
        )(mine, other)
    first = w % 2 == 0
    whole = jnp.concatenate([jnp.where(first, mine, other), jnp.where(first, other, mine)], 1)
    rows = []
    for m in range(narrow):
        blocks = [block for *_, block in row_of(whole, m, narrow)]
        spans = blocks[: 2 * narrow], blocks[2 * narrow :]
        rows.append(jnp.concatenate([jnp.concatenate(span, 1) for span in spans], 0))
    return lax.select_n(n, *rows)


def on_device(raw_ints, metric, occ_energy, vir_energy, pair_kept):
    wide, narrow = lax.axis_size("wide"), lax.axis_size("narrow")
    w, n = lax.axis_index("wide"), lax.axis_index("narrow")
    v = raw_ints.shape[1]
    virtuals = v * narrow

    near = 4
    chunks = [(0, v // 2), (v // 2, v // 2)]
    rows = metric.shape[0] // near
    piece = lax.dynamic_slice_in_dim(metric, (w % near) * rows, rows, 0)
    far = [passed_along(piece, "narrow", s) for s in range(1, narrow)]
    own = lax.dynamic_index_in_dim(raw_ints, n, 0, keepdims=False)
    raw_low = [passed_along(own, "wide", 1)]
    arrived, given = [], []
    for s in range(1, narrow):
        block = lax.dynamic_index_in_dim(raw_ints, (n + s) % narrow, 0, keepdims=False)
        parts = [block[first : first + rows] for first, rows in chunks]
        arrived += [passed_along(one, "narrow", s) for one in reversed(parts)][::-1]
        given += parts
    *fit_near, occ, kept = near_fit(after(own, *given), metric, occ_energy, pair_kept)
    low_occ = passed_along(occ, "wide", 1)
    far = [after(one, fit_near[0]) for one in far]
    far_x = [swapped(one, "wide", 2) for one in far]
    far_core = [swapped(one, "wide", 1) for one in far]
    raw_low += [passed_along(one, "wide", 1) for one in arrived[:-1]]
    far_x = [after(one, raw_low[0], low_occ, arrived[0]) for one in far_x]
    far_last = [swapped(one, "wide", 1) for one in far_x]

    *own_turned, far_high, far_low = turn_own(own, fit_near, far + far_core + far_x + far_last)
    raw_low.append(passed_along(after(arrived[-1], own_turned[0]), "wide", 1))
    turned = [*own_turned, *turn(arrived, fit_near[2:], (far_high, far_low))]

    form = tail if v % 128 == 0 else tail_plain
    energies = occ, low_occ, kept, vir_energy
    blocks, own_value = form(turned, raw_low, energies, v, 0.0625 / (wide * narrow))
    blocks, own_value, w, n = lax.optimization_barrier((blocks, own_value, w, n))
    own_value = own_value.reshape(1)
    upper_value = passed_along(own_value, "wide", -1)

    *bits, last = [1 << k for k in range(wide.bit_length() - 1)]
    for bit in bits:
        blocks = halved(blocks, w, bit)
        if bit == 2:
            blocks, upper_value = lax.optimization_barrier((blocks, upper_value))
    full = own_rows(blocks, n, last)
    for bit in reversed(bits[1:]):
        full = doubled(full, w, bit)
    return assembled(full, w, n, narrow), own_value + upper_value


def solution(mesh):
    placed = (
        P("wide", "narrow", None),
        P("narrow", None),
        P(("wide", "narrow")),
        P(),
        P(("wide", "narrow")),
    )
    return jax.shard_map(
        on_device,
        mesh=mesh,
        in_specs=placed,
        out_specs=(P("narrow", None), P(("wide", "narrow"))),
        check_vma=False,
    )
```

```python
import functools

import jax
import jax.numpy as jnp
from jax import lax
from jax.experimental import pallas as pl
from jax.experimental.pallas import tpu as pltpu
from jax.sharding import PartitionSpec as P

PASSES = lax.Precision.HIGH
VMEM = pltpu.MemorySpace.VMEM
NEAR_COST = 15_000_000_000


def contract(left, right, left_dim, right_dim):
    return lax.dot_general(
        left,
        right,
        (((left_dim,), (right_dim,)), ((), ())),
        precision=PASSES,
        preferred_element_type=jnp.float32,
    )


def passed_along(shard, axis, by):
    size = lax.axis_size(axis)
    return lax.ppermute(shard, axis, [(i, (i + by) % size) for i in range(size)])


def swapped(shard, axis, bit):
    size = lax.axis_size(axis)
    return lax.ppermute(shard, axis, [(i, i ^ bit) for i in range(size)])


def after(value, *gates):
    return lax.optimization_barrier((value,) + gates)[0]


def in_vmem(count):
    return [pl.BlockSpec(memory_space=VMEM)] * count


def limit(mib):
    return pltpu.CompilerParams(vmem_limit_bytes=mib * 2**20)


def cost(flops):
    return pl.CostEstimate(flops=flops, bytes_accessed=0, transcendentals=0)


def joined_kernel(*refs):
    *parts, out = refs
    out[...] = stacked(parts)


def joined(parts):
    rows, width = sum(part.shape[0] for part in parts), parts[0].shape[1]
    return pl.pallas_call(
        joined_kernel,
        out_shape=like(rows, width, jnp.float32),
        in_specs=in_vmem(len(parts)),
        out_specs=in_vmem(1)[0],
        compiler_params=limit(8),
        name="joined",
    )(*parts)


def halves(value):
    high = value.astype(jnp.bfloat16)
    low = (value - high.astype(jnp.float32)).astype(jnp.bfloat16)
    return high, low


def dot3(left, right, right_dim):
    (lh, ll), (rh, rl) = left, right
    dims = (((1,), (right_dim,)), ((), ()))
    total = lax.dot_general(ll, rh, dims, preferred_element_type=jnp.float32)
    total += lax.dot_general(lh, rl, dims, preferred_element_type=jnp.float32)
    return total + lax.dot_general(lh, rh, dims, preferred_element_type=jnp.float32)


def stacked(refs):
    return jnp.concatenate([one[...] for one in refs], 0)


def like(rows, width, dtype):
    return jax.ShapeDtypeStruct((rows, width), dtype)


def near_fit_kernel(rows, metric, occ, kept, fit_high, fit_low, high, low, occ_tile, kept_tile):
    parts = halves(metric[...])
    high[...], low[...] = parts
    fit_high[...], fit_low[...] = halves(dot3(halves(rows[...]), parts, 1))
    occ_tile[...] = jnp.broadcast_to(occ[...], occ_tile.shape)
    kept_tile[...] = jnp.broadcast_to(kept[...].astype(jnp.float32), kept_tile.shape)


def near_fit(rows, metric, occ, kept):
    (count, width), near = rows.shape, metric.shape[0]
    return pl.pallas_call(
        near_fit_kernel,
        out_shape=[like(count, near, jnp.bfloat16)] * 2
        + [like(near, width, jnp.bfloat16)] * 2
        + [like(8, 128, jnp.float32)] * 2,
        in_specs=in_vmem(4),
        out_specs=in_vmem(6),
        compiler_params=limit(16),
        cost_estimate=cost(NEAR_COST),
        name="near_fit",
    )(rows, metric, occ[None, :], kept[None, :])


def turn_own_kernel(rows, fit_high, fit_low, near_high, near_low, *refs):
    pieces, (out_high, out_low, high, low) = refs[:-4], refs[-4:]
    parts = halves(stacked(pieces))
    high[...], low[...] = parts
    fit = halves(dot3(halves(rows[...]), parts, 1))
    total = dot3(fit, parts, 0)
    total += dot3((fit_high[...], fit_low[...]), (near_high[...], near_low[...]), 0)
    out_high[...], out_low[...] = halves(total)


def turn_own(rows, near, pieces):
    (count, width), far = rows.shape, sum(piece.shape[0] for piece in pieces)
    return pl.pallas_call(
        turn_own_kernel,
        out_shape=[like(count, width, jnp.bfloat16)] * 2 + [like(far, width, jnp.bfloat16)] * 2,
        in_specs=in_vmem(5 + len(pieces)),
        out_specs=in_vmem(4),
        compiler_params=limit(20),
        cost_estimate=cost(12 * count * far * width),
        name="turn_own",
    )(rows, *near, *pieces)


def turn_kernel(near_high, near_low, far_high, far_low, *refs):
    cuts, (out_high, out_low) = refs[:-2], refs[-2:]
    rows = halves(stacked(cuts))
    total = 0
    for parts in ((near_high[...], near_low[...]), (far_high[...], far_low[...])):
        total += dot3(halves(dot3(rows, parts, 1)), parts, 0)
    out_high[...], out_low[...] = halves(total)


def turn(cuts, near, far):
    count, width = sum(one.shape[0] for one in cuts), cuts[0].shape[1]
    return pl.pallas_call(
        turn_kernel,
        out_shape=[like(count, width, jnp.bfloat16)] * 2,
        in_specs=in_vmem(4 + len(cuts)),
        out_specs=in_vmem(2),
        compiler_params=limit(20),
        cost_estimate=cost(12 * count * width * (near[0].shape[0] + far[0].shape[0])),
        name="turn",
    )(*near, *far, *cuts)


def spots_of(tiles):
    pairs = []
    for a in range(tiles):
        for b in range(a, tiles):
            halves_of = [(2 * a + r, 2 * b + c) for r in (0, 1) for c in (0, 1)]
            pairs += [pair for pair in halves_of if pair[0] <= pair[1]]
    return {pair: k for k, pair in enumerate(pairs)}


def row_spots(n, tiles):
    spots = spots_of(tiles)
    return {pair: k for pair, k in spots.items() if pair[0] // 2 == n or pair[1] // 2 == n}


def tail_kernel(v, tiles, scale, occ, low_occ, kept, vir, own_high, own_low, far_high, far_low, *refs):
    lows, (blocks, value), scratch = refs[:-8], refs[-8:-6], refs[-6:]
    amp, amp_t, high, low, high_t, low_t = scratch
    n = lax.axis_index("narrow")
    virtuals = v * tiles
    at = [pl.ds(pl.multiple_of(lax.rem(n - a + tiles, tiles) * v, v), v) for a in range(tiles)]
    row = jnp.concatenate([vir[:, one] for one in at], 1)
    col = jnp.broadcast_to(row, (128, virtuals)).T[:, :1]
    gap = occ[:1, :1] + low_occ[:1, :1]
    weight = kept[:1, :1]
    right = halves(stacked(lows))
    left = (own_high[...], own_low[...]), (far_high[...], far_low[...])
    pairs = [dot3(one, right, 1) for one in left]
    spans = slice(0, v), slice(v, virtuals)
    for pair, span in zip(pairs, spans):
        amp[span, :] = pair / (col[span, :] + row - gap)
    amp_t[...] = amp[...].T
    total = jnp.float32(0)
    for pair, span in zip(pairs, spans):
        total += jnp.sum(pair * (2.0 * amp[span, :] - amp_t[span, :]))
    value[...] = -weight * total / (virtuals * virtuals)
    high[...], low[...] = halves(amp[...])
    high_t[...], low_t[...] = halves(amp_t[...])
    spots, half = spots_of(tiles), v // 2
    for a in range(tiles):
        for b in range(a, tiles):
            block = dot3((high[at[a], :], low[at[a], :]), (high_t[:, at[b]], low_t[:, at[b]]), 0)
            block += dot3((high_t[at[a], :], low_t[at[a], :]), (high[:, at[b]], low[:, at[b]]), 0)
            block *= weight * scale
            for r in (0, 1):
                for c in (0, 1):
                    k = spots.get((2 * a + r, 2 * b + c))
                    if k is not None:
                        blocks[k] = block[r * half : (r + 1) * half, c * half : (c + 1) * half]


def tail(turned, raw_low, energies, v, scale):
    virtuals, width = energies[-1].shape[0], raw_low[0].shape[1]
    tiles = virtuals // v
    count = len(spots_of(tiles))
    square = [pltpu.VMEM((virtuals, virtuals), kind) for kind in (jnp.float32, jnp.bfloat16)]
    return pl.pallas_call(
        functools.partial(tail_kernel, v, tiles, scale),
        out_shape=[
            jax.ShapeDtypeStruct((count, v // 2, v // 2), jnp.float32),
            jax.ShapeDtypeStruct((1, 1), jnp.float32),
        ],
        in_specs=in_vmem(8 + len(raw_low)),
        out_specs=in_vmem(2),
        scratch_shapes=[square[0]] * 2 + [square[1]] * 4,
        compiler_params=limit(24),
        cost_estimate=cost(6 * virtuals * virtuals * width + 3 * count * v * v * virtuals),
        name="tail",
    )(*energies[:-1], energies[-1][None, :], *turned, *raw_low)


def tail_plain(turned, raw_low, energies, v, scale):
    occ, low_occ, kept, vir = energies
    virtuals = vir.shape[0]
    narrow = virtuals // v
    order = ((lax.axis_index("narrow") - jnp.arange(narrow)) % narrow * v)[:, None] + jnp.arange(v)[None, :]
    order = order.reshape(virtuals)
    weight = kept[0, 0]
    levels = vir[order]
    own_high, own_low, far_high, far_low = [one.astype(jnp.float32) for one in turned]
    left = jnp.concatenate([own_high + own_low, far_high + far_low], 0)
    pair_ints = contract(left, jnp.concatenate(raw_low, 0), 1, 1)
    amplitude = pair_ints / (levels[:, None] + levels[None, :] - occ[0, 0] - low_occ[0, 0])
    value = jnp.sum(pair_ints * (2.0 * amplitude - amplitude.T)) * -weight / (virtuals * virtuals)
    amplitude = amplitude[order][:, order]
    blocks, half = [], v // 2
    for at in range(0, virtuals, half):
        row = contract(amplitude[at : at + half], amplitude[at:], 1, 1)
        row = row + contract(amplitude[:, at : at + half], amplitude[:, at:], 0, 0)
        blocks += jnp.split(row * (weight * scale), (virtuals - at) // half, 1)
    return jnp.stack(blocks), value.reshape(1, 1)


def halved(blocks, w, bit):
    half = blocks.shape[1] // 2
    side = (w // bit) % 2
    kept = lax.dynamic_slice_in_dim(blocks, side * half, half, 1)
    given = lax.dynamic_slice_in_dim(blocks, (1 - side) * half, half, 1)
    return kept + swapped(given, "wide", bit)


def doubled(blocks, w, bit):
    other = swapped(blocks, "wide", bit)
    low = (w // bit) % 2 == 0
    return jnp.concatenate([jnp.where(low, blocks, other), jnp.where(low, other, blocks)], 1)


def own_rows(blocks, n, bit):
    wide, narrow = lax.axis_size("wide"), lax.axis_size("narrow")
    spots = [list(row_spots(m, narrow).values()) for m in range(narrow)]

    def of(m):
        picked = [jnp.concatenate([blocks[k : k + 1] for k in row]) for row in spots]
        return lax.select_n(m, *picked)

    total = of(n)
    for s in range(narrow):
        given = of((n + s) % narrow)
        for flip in (0, bit):
            if s or flip:
                steps = [
                    (w * narrow + m, (w ^ flip) * narrow + (m + s) % narrow)
                    for w in range(wide)
                    for m in range(narrow)
                ]
                total = total + lax.ppermute(given, ("wide", "narrow"), steps)
    return total


def row_of(full, m, narrow):
    held = {pair: k for k, pair in enumerate(row_spots(m, narrow))}
    for r in (0, 1):
        for c in range(2 * narrow):
            pair = (2 * m + r, c)
            yield r, c, full[held[pair]] if pair in held else full[held[c, 2 * m + r]].T


def assembled_kernel(narrow, mine, other, out):
    first = lax.rem(lax.axis_index("wide"), 2) == 0
    half = 2 * mine.shape[1]
    whole = jnp.concatenate(
        [jnp.where(first, mine[...], other[...]), jnp.where(first, other[...], mine[...])], 1
    )
    for m in range(narrow):

        @pl.when(lax.axis_index("narrow") == m)
        def _():
            for r, c, block in row_of(whole, m, narrow):
                out[r * half : (r + 1) * half, c * half : (c + 1) * half] = block


def assembled(mine, w, n, narrow):
    other = swapped(mine, "wide", 1)
    half = 2 * mine.shape[1]
    if half % 128 == 0:
        return pl.pallas_call(
            functools.partial(assembled_kernel, narrow),
            out_shape=like(2 * half, 2 * half * narrow, jnp.float32),
            in_specs=in_vmem(2),
            out_specs=in_vmem(1)[0],
            compiler_params=limit(8),
            name="assembled",
        )(mine, other)
    first = w % 2 == 0
    whole = jnp.concatenate([jnp.where(first, mine, other), jnp.where(first, other, mine)], 1)
    rows = []
    for m in range(narrow):
        blocks = [block for *_, block in row_of(whole, m, narrow)]
        spans = blocks[: 2 * narrow], blocks[2 * narrow :]
        rows.append(jnp.concatenate([jnp.concatenate(span, 1) for span in spans], 0))
    return lax.select_n(n, *rows)


def on_device(raw_ints, metric, occ_energy, vir_energy, pair_kept):
    wide, narrow = lax.axis_size("wide"), lax.axis_size("narrow")
    w, n = lax.axis_index("wide"), lax.axis_index("narrow")
    v = raw_ints.shape[1]
    virtuals = v * narrow

    near = 8 if wide % 8 == 0 and metric.shape[0] % 64 == 0 else 4
    chunks = [(0, v // 4), (v // 4, v // 2), (3 * v // 4, v // 4)]
    rows = metric.shape[0] // near
    piece = lax.dynamic_slice_in_dim(metric, (w % near) * rows, rows, 0)
    far = [passed_along(piece, "narrow", s) for s in range(1, narrow)]
    own = lax.dynamic_index_in_dim(raw_ints, n, 0, keepdims=False)
    raw_low = [passed_along(own, "wide", 1)]
    arrived, given = [], []
    for s in range(1, narrow):
        block = lax.dynamic_index_in_dim(raw_ints, (n + s) % narrow, 0, keepdims=False)
        parts = [block[first : first + rows] for first, rows in chunks]
        arrived += [passed_along(one, "narrow", s) for one in reversed(parts)][::-1]
        given += parts
    *fit_near, occ, kept = near_fit(after(own, *given), metric, occ_energy, pair_kept)
    low_occ = passed_along(occ, "wide", 1)
    far = [after(one, fit_near[0]) for one in far]
    if near == 8:
        far += [swapped(one, "wide", 4) for one in far]
    far = joined(far)
    far_x = swapped(after(far, arrived[0]), "wide", 2)
    far_core = swapped(far, "wide", 1)
    raw_low += [passed_along(one, "wide", 1) for one in arrived[:-1]]
    far_x = after(far_x, raw_low[0], arrived[1])
    far_last = swapped(far_x, "wide", 1)

    *own_turned, far_high, far_low = turn_own(own, fit_near, [far, far_core, far_x, far_last])
    raw_low.append(passed_along(after(arrived[-1], low_occ, own_turned[0]), "wide", 1))
    turned = [*own_turned, *turn(arrived, fit_near[2:], (far_high, far_low))]

    form = tail if v % 128 == 0 else tail_plain
    energies = occ, low_occ, kept, vir_energy
    blocks, own_value = form(turned, raw_low, energies, v, 0.0625 / (wide * narrow))
    blocks, own_value, w, n = lax.optimization_barrier((blocks, own_value, w, n))
    own_value = own_value.reshape(1)
    upper_value = passed_along(own_value, "wide", -1)

    *bits, last = [1 << k for k in range(wide.bit_length() - 1)]
    for bit in bits:
        blocks = halved(blocks, w, bit)
        if bit == 2:
            blocks, upper_value = lax.optimization_barrier((blocks, upper_value))
    full = own_rows(blocks, n, last)
    for bit in reversed(bits[1:]):
        full = doubled(full, w, bit)
    return assembled(full, w, n, narrow), own_value + upper_value


def solution(mesh):
    placed = (
        P("wide", "narrow", None),
        P("narrow", None),
        P(("wide", "narrow")),
        P(),
        P(("wide", "narrow")),
    )
    return jax.shard_map(
        on_device,
        mesh=mesh,
        in_specs=placed,
        out_specs=(P("narrow", None), P(("wide", "narrow"))),
        check_vma=False,
    )
```

```python
import functools

import jax
import jax.numpy as jnp
from jax import lax
from jax.experimental import pallas as pl
from jax.experimental.pallas import tpu as pltpu
from jax.sharding import PartitionSpec as P

PASSES = lax.Precision.HIGH
VMEM = pltpu.MemorySpace.VMEM
NEAR_COST = 15_000_000_000


def contract(left, right, left_dim, right_dim):
    return lax.dot_general(
        left,
        right,
        (((left_dim,), (right_dim,)), ((), ())),
        precision=PASSES,
        preferred_element_type=jnp.float32,
    )


def passed_along(shard, axis, by):
    size = lax.axis_size(axis)
    return lax.ppermute(shard, axis, [(i, (i + by) % size) for i in range(size)])


def swapped(shard, axis, bit):
    size = lax.axis_size(axis)
    return lax.ppermute(shard, axis, [(i, i ^ bit) for i in range(size)])


def after(value, *gates):
    return lax.optimization_barrier((value,) + gates)[0]


def in_vmem(count):
    return [pl.BlockSpec(memory_space=VMEM)] * count


def limit(mib):
    return pltpu.CompilerParams(vmem_limit_bytes=mib * 2**20)


def cost(flops):
    return pl.CostEstimate(flops=flops, bytes_accessed=0, transcendentals=0)


def halves(value):
    high = value.astype(jnp.bfloat16)
    low = (value - high.astype(jnp.float32)).astype(jnp.bfloat16)
    return high, low


def dot3(left, right, right_dim):
    (lh, ll), (rh, rl) = left, right
    dims = (((1,), (right_dim,)), ((), ()))
    total = lax.dot_general(ll, rh, dims, preferred_element_type=jnp.float32)
    total += lax.dot_general(lh, rl, dims, preferred_element_type=jnp.float32)
    return total + lax.dot_general(lh, rh, dims, preferred_element_type=jnp.float32)


def stacked(refs):
    return jnp.concatenate([one[...] for one in refs], 0)


def like(rows, width, dtype):
    return jax.ShapeDtypeStruct((rows, width), dtype)


def near_fit_kernel(rows, metric, occ, kept, fit_high, fit_low, high, low, occ_tile, kept_tile):
    parts = halves(metric[...])
    high[...], low[...] = parts
    fit_high[...], fit_low[...] = halves(dot3(halves(rows[...]), parts, 1))
    occ_tile[...] = jnp.broadcast_to(occ[...], occ_tile.shape)
    kept_tile[...] = jnp.broadcast_to(kept[...].astype(jnp.float32), kept_tile.shape)


def near_fit(rows, metric, occ, kept):
    (count, width), near = rows.shape, metric.shape[0]
    return pl.pallas_call(
        near_fit_kernel,
        out_shape=[like(count, near, jnp.bfloat16)] * 2
        + [like(near, width, jnp.bfloat16)] * 2
        + [like(8, 128, jnp.float32)] * 2,
        in_specs=in_vmem(4),
        out_specs=in_vmem(6),
        compiler_params=limit(16),
        cost_estimate=cost(NEAR_COST),
        name="near_fit",
    )(rows, metric, occ[None, :], kept[None, :])


def turn_own_kernel(rows, fit_high, fit_low, near_high, near_low, *refs):
    pieces, (out_high, out_low, high, low) = refs[:-4], refs[-4:]
    parts = halves(stacked(pieces))
    high[...], low[...] = parts
    fit = halves(dot3(halves(rows[...]), parts, 1))
    total = dot3(fit, parts, 0)
    total += dot3((fit_high[...], fit_low[...]), (near_high[...], near_low[...]), 0)
    out_high[...], out_low[...] = halves(total)


def turn_own(rows, near, pieces):
    (count, width), far = rows.shape, sum(piece.shape[0] for piece in pieces)
    return pl.pallas_call(
        turn_own_kernel,
        out_shape=[like(count, width, jnp.bfloat16)] * 2 + [like(far, width, jnp.bfloat16)] * 2,
        in_specs=in_vmem(5 + len(pieces)),
        out_specs=in_vmem(4),
        compiler_params=limit(20),
        cost_estimate=cost(12 * count * far * width),
        name="turn_own",
    )(rows, *near, *pieces)


def turn_kernel(near_high, near_low, far_high, far_low, *refs):
    cuts, (out_high, out_low) = refs[:-2], refs[-2:]
    rows = halves(stacked(cuts))
    total = 0
    for parts in ((near_high[...], near_low[...]), (far_high[...], far_low[...])):
        total += dot3(halves(dot3(rows, parts, 1)), parts, 0)
    out_high[...], out_low[...] = halves(total)


def turn(cuts, near, far):
    count, width = sum(one.shape[0] for one in cuts), cuts[0].shape[1]
    return pl.pallas_call(
        turn_kernel,
        out_shape=[like(count, width, jnp.bfloat16)] * 2,
        in_specs=in_vmem(4 + len(cuts)),
        out_specs=in_vmem(2),
        compiler_params=limit(20),
        cost_estimate=cost(12 * count * width * (near[0].shape[0] + far[0].shape[0])),
        name="turn",
    )(*near, *far, *cuts)


def spots_of(tiles):
    pairs = []
    for a in range(tiles):
        for b in range(a, tiles):
            halves_of = [(2 * a + r, 2 * b + c) for r in (0, 1) for c in (0, 1)]
            pairs += [pair for pair in halves_of if pair[0] <= pair[1]]
    return {pair: k for k, pair in enumerate(pairs)}


def row_spots(n, tiles):
    spots = spots_of(tiles)
    return {pair: k for pair, k in spots.items() if pair[0] // 2 == n or pair[1] // 2 == n}


def tail_kernel(v, tiles, scale, occ, low_occ, kept, vir, own_high, own_low, far_high, far_low, *refs):
    lows, (blocks, value), scratch = refs[:-8], refs[-8:-6], refs[-6:]
    amp, amp_t, high, low, high_t, low_t = scratch
    n = lax.axis_index("narrow")
    virtuals = v * tiles
    at = [pl.ds(pl.multiple_of(lax.rem(n - a + tiles, tiles) * v, v), v) for a in range(tiles)]
    row = jnp.concatenate([vir[:, one] for one in at], 1)
    col = jnp.broadcast_to(row, (128, virtuals)).T[:, :1]
    gap = occ[:1, :1] + low_occ[:1, :1]
    weight = kept[:1, :1]
    right = halves(stacked(lows))
    left = (own_high[...], own_low[...]), (far_high[...], far_low[...])
    pairs = [dot3(one, right, 1) for one in left]
    spans = slice(0, v), slice(v, virtuals)
    for pair, span in zip(pairs, spans):
        amp[span, :] = pair / (col[span, :] + row - gap)
    amp_t[...] = amp[...].T
    total = jnp.float32(0)
    for pair, span in zip(pairs, spans):
        total += jnp.sum(pair * (2.0 * amp[span, :] - amp_t[span, :]))
    value[...] = -weight * total / (virtuals * virtuals)
    high[...], low[...] = halves(amp[...])
    high_t[...], low_t[...] = halves(amp_t[...])
    spots, half = spots_of(tiles), v // 2
    for a in range(tiles):
        for b in range(a, tiles):
            block = dot3((high[at[a], :], low[at[a], :]), (high_t[:, at[b]], low_t[:, at[b]]), 0)
            block += dot3((high_t[at[a], :], low_t[at[a], :]), (high[:, at[b]], low[:, at[b]]), 0)
            block *= weight * scale
            for r in (0, 1):
                for c in (0, 1):
                    k = spots.get((2 * a + r, 2 * b + c))
                    if k is not None:
                        blocks[k] = block[r * half : (r + 1) * half, c * half : (c + 1) * half]


def tail(turned, raw_low, energies, v, scale):
    virtuals, width = energies[-1].shape[0], raw_low[0].shape[1]
    tiles = virtuals // v
    count = len(spots_of(tiles))
    square = [pltpu.VMEM((virtuals, virtuals), kind) for kind in (jnp.float32, jnp.bfloat16)]
    return pl.pallas_call(
        functools.partial(tail_kernel, v, tiles, scale),
        out_shape=[
            jax.ShapeDtypeStruct((count, v // 2, v // 2), jnp.float32),
            jax.ShapeDtypeStruct((1, 1), jnp.float32),
        ],
        in_specs=in_vmem(8 + len(raw_low)),
        out_specs=in_vmem(2),
        scratch_shapes=[square[0]] * 2 + [square[1]] * 4,
        compiler_params=limit(24),
        cost_estimate=cost(6 * virtuals * virtuals * width + 3 * count * v * v * virtuals),
        name="tail",
    )(*energies[:-1], energies[-1][None, :], *turned, *raw_low)


def tail_plain(turned, raw_low, energies, v, scale):
    occ, low_occ, kept, vir = energies
    virtuals = vir.shape[0]
    narrow = virtuals // v
    order = ((lax.axis_index("narrow") - jnp.arange(narrow)) % narrow * v)[:, None] + jnp.arange(v)[None, :]
    order = order.reshape(virtuals)
    weight = kept[0, 0]
    levels = vir[order]
    own_high, own_low, far_high, far_low = [one.astype(jnp.float32) for one in turned]
    left = jnp.concatenate([own_high + own_low, far_high + far_low], 0)
    pair_ints = contract(left, jnp.concatenate(raw_low, 0), 1, 1)
    amplitude = pair_ints / (levels[:, None] + levels[None, :] - occ[0, 0] - low_occ[0, 0])
    value = jnp.sum(pair_ints * (2.0 * amplitude - amplitude.T)) * -weight / (virtuals * virtuals)
    amplitude = amplitude[order][:, order]
    blocks, half = [], v // 2
    for at in range(0, virtuals, half):
        row = contract(amplitude[at : at + half], amplitude[at:], 1, 1)
        row = row + contract(amplitude[:, at : at + half], amplitude[:, at:], 0, 0)
        blocks += jnp.split(row * (weight * scale), (virtuals - at) // half, 1)
    return jnp.stack(blocks), value.reshape(1, 1)


def halved(blocks, w, bit):
    half = blocks.shape[1] // 2
    side = (w // bit) % 2
    kept = lax.dynamic_slice_in_dim(blocks, side * half, half, 1)
    given = lax.dynamic_slice_in_dim(blocks, (1 - side) * half, half, 1)
    return kept + swapped(given, "wide", bit)


def doubled(blocks, w, bit):
    other = swapped(blocks, "wide", bit)
    low = (w // bit) % 2 == 0
    return jnp.concatenate([jnp.where(low, blocks, other), jnp.where(low, other, blocks)], 1)


def quartered(blocks, w, low):
    rows, spot = blocks.shape[1] // 4, (w // low) % 4
    total = lax.dynamic_slice_in_dim(blocks, spot * rows, rows, 1)
    for flip in (3, 1, 2):
        given = lax.dynamic_slice_in_dim(blocks, (spot ^ flip) * rows, rows, 1)
        total = total + swapped(given, "wide", flip * low)
    return total


def quadrupled(blocks, w, low):
    held = [blocks] + [swapped(blocks, "wide", flip * low) for flip in (1, 2, 3)]
    spot = (w // low) % 4
    return jnp.concatenate(
        [lax.select_n(spot, *[held[at ^ mine] for mine in range(4)]) for at in range(4)], 1
    )


def own_rows(blocks, n, bit):
    wide, narrow = lax.axis_size("wide"), lax.axis_size("narrow")
    spots = [list(row_spots(m, narrow).values()) for m in range(narrow)]

    def of(m):
        picked = [jnp.concatenate([blocks[k : k + 1] for k in row]) for row in spots]
        return lax.select_n(m, *picked)

    total = of(n)
    for s in range(narrow):
        given = of((n + s) % narrow)
        for flip in (0, bit):
            if s or flip:
                steps = [
                    (w * narrow + m, (w ^ flip) * narrow + (m + s) % narrow)
                    for w in range(wide)
                    for m in range(narrow)
                ]
                total = total + lax.ppermute(given, ("wide", "narrow"), steps)
    return total


def row_of(full, m, narrow):
    held = {pair: k for k, pair in enumerate(row_spots(m, narrow))}
    for r in (0, 1):
        for c in range(2 * narrow):
            pair = (2 * m + r, c)
            yield r, c, full[held[pair]] if pair in held else full[held[c, 2 * m + r]].T


def assembled_kernel(narrow, mine, other, out):
    first = lax.rem(lax.axis_index("wide"), 2) == 0
    half = 2 * mine.shape[1]
    whole = jnp.concatenate(
        [jnp.where(first, mine[...], other[...]), jnp.where(first, other[...], mine[...])], 1
    )
    for m in range(narrow):

        @pl.when(lax.axis_index("narrow") == m)
        def _():
            for r, c, block in row_of(whole, m, narrow):
                out[r * half : (r + 1) * half, c * half : (c + 1) * half] = block


def assembled(mine, w, n, narrow):
    other = swapped(mine, "wide", 1)
    half = 2 * mine.shape[1]
    if half % 128 == 0:
        return pl.pallas_call(
            functools.partial(assembled_kernel, narrow),
            out_shape=like(2 * half, 2 * half * narrow, jnp.float32),
            in_specs=in_vmem(2),
            out_specs=in_vmem(1)[0],
            compiler_params=limit(8),
            name="assembled",
        )(mine, other)
    first = w % 2 == 0
    whole = jnp.concatenate([jnp.where(first, mine, other), jnp.where(first, other, mine)], 1)
    rows = []
    for m in range(narrow):
        blocks = [block for *_, block in row_of(whole, m, narrow)]
        spans = blocks[: 2 * narrow], blocks[2 * narrow :]
        rows.append(jnp.concatenate([jnp.concatenate(span, 1) for span in spans], 0))
    return lax.select_n(n, *rows)


def on_device(raw_ints, metric, occ_energy, vir_energy, pair_kept):
    wide, narrow = lax.axis_size("wide"), lax.axis_size("narrow")
    w, n = lax.axis_index("wide"), lax.axis_index("narrow")
    v = raw_ints.shape[1]
    virtuals = v * narrow

    near = 4
    chunks = [(0, v // 2), (v // 2, v // 2)]
    rows = metric.shape[0] // near
    piece = lax.dynamic_slice_in_dim(metric, (w % near) * rows, rows, 0)
    far = [passed_along(piece, "narrow", s) for s in range(1, narrow)]
    own = lax.dynamic_index_in_dim(raw_ints, n, 0, keepdims=False)
    raw_low = [passed_along(own, "wide", 1)]
    arrived, given = [], []
    for s in range(1, narrow):
        block = lax.dynamic_index_in_dim(raw_ints, (n + s) % narrow, 0, keepdims=False)
        parts = [block[first : first + rows] for first, rows in chunks]
        arrived += [passed_along(one, "narrow", s) for one in reversed(parts)][::-1]
        given += parts
    *fit_near, occ, kept = near_fit(after(own, *given), metric, occ_energy, pair_kept)
    low_occ = passed_along(occ, "wide", 1)
    far = [after(one, fit_near[0]) for one in far]
    far_x = [swapped(one, "wide", 2) for one in far]
    far_core = [swapped(one, "wide", 1) for one in far]
    raw_low += [passed_along(one, "wide", 1) for one in arrived[:-1]]
    far_x = [after(one, raw_low[0], low_occ, arrived[0]) for one in far_x]
    far_last = [swapped(one, "wide", 1) for one in far_x]

    *own_turned, far_high, far_low = turn_own(own, fit_near, far + far_core + far_x + far_last)
    raw_low.append(passed_along(after(arrived[-1], *far_last), "wide", 1))
    turned = [*own_turned, *turn(arrived, fit_near[2:], (far_high, far_low))]

    form = tail if v % 128 == 0 else tail_plain
    energies = occ, low_occ, kept, vir_energy
    blocks, own_value = form(turned, raw_low, energies, v, 0.0625 / (wide * narrow))
    blocks, own_value, w, n = lax.optimization_barrier((blocks, own_value, w, n))
    own_value = own_value.reshape(1)
    upper_value = passed_along(own_value, "wide", -1)

    first, *bits, last = [1 << k for k in range(wide.bit_length() - 1)]
    low, bits = bits[0], bits[2:]
    blocks = halved(blocks, w, first)
    blocks = quartered(blocks, w, low)
    blocks, upper_value = lax.optimization_barrier((blocks, upper_value))
    for bit in bits:
        blocks = halved(blocks, w, bit)
    full = own_rows(blocks, n, last)
    for bit in reversed(bits):
        full = doubled(full, w, bit)
    full = quadrupled(full, w, low)
    return assembled(full, w, n, narrow), own_value + upper_value


def solution(mesh):
    placed = (
        P("wide", "narrow", None),
        P("narrow", None),
        P(("wide", "narrow")),
        P(),
        P(("wide", "narrow")),
    )
    return jax.shard_map(
        on_device,
        mesh=mesh,
        in_specs=placed,
        out_specs=(P("narrow", None), P(("wide", "narrow"))),
        check_vma=False,
    )
```

```python
import functools

import jax
import jax.numpy as jnp
from jax import lax
from jax.experimental import pallas as pl
from jax.experimental.pallas import tpu as pltpu
from jax.sharding import PartitionSpec as P

PASSES = lax.Precision.HIGH
VMEM = pltpu.MemorySpace.VMEM
NEAR_COST = 15_000_000_000


def contract(left, right, left_dim, right_dim):
    return lax.dot_general(
        left,
        right,
        (((left_dim,), (right_dim,)), ((), ())),
        precision=PASSES,
        preferred_element_type=jnp.float32,
    )


def passed_along(shard, axis, by):
    size = lax.axis_size(axis)
    return lax.ppermute(shard, axis, [(i, (i + by) % size) for i in range(size)])


def swapped(shard, axis, bit):
    size = lax.axis_size(axis)
    return lax.ppermute(shard, axis, [(i, i ^ bit) for i in range(size)])


def after(value, *gates):
    return lax.optimization_barrier((value,) + gates)[0]


def in_vmem(count):
    return [pl.BlockSpec(memory_space=VMEM)] * count


def limit(mib):
    return pltpu.CompilerParams(vmem_limit_bytes=mib * 2**20)


def cost(flops):
    return pl.CostEstimate(flops=flops, bytes_accessed=0, transcendentals=0)


def halves(value):
    high = value.astype(jnp.bfloat16)
    low = (value - high.astype(jnp.float32)).astype(jnp.bfloat16)
    return high, low


def dot3(left, right, right_dim):
    (lh, ll), (rh, rl) = left, right
    dims = (((1,), (right_dim,)), ((), ()))
    total = lax.dot_general(ll, rh, dims, preferred_element_type=jnp.float32)
    total += lax.dot_general(lh, rl, dims, preferred_element_type=jnp.float32)
    return total + lax.dot_general(lh, rh, dims, preferred_element_type=jnp.float32)


def stacked(refs):
    return jnp.concatenate([one[...] for one in refs], 0)


def like(rows, width, dtype):
    return jax.ShapeDtypeStruct((rows, width), dtype)


def near_fit_kernel(rows, metric, occ, kept, fit_high, fit_low, high, low, occ_tile, kept_tile):
    parts = halves(metric[...])
    high[...], low[...] = parts
    fit_high[...], fit_low[...] = halves(dot3(halves(rows[...]), parts, 1))
    occ_tile[...] = jnp.broadcast_to(occ[...], occ_tile.shape)
    kept_tile[...] = jnp.broadcast_to(kept[...].astype(jnp.float32), kept_tile.shape)


def near_fit(rows, metric, occ, kept):
    (count, width), near = rows.shape, metric.shape[0]
    return pl.pallas_call(
        near_fit_kernel,
        out_shape=[like(count, near, jnp.bfloat16)] * 2
        + [like(near, width, jnp.bfloat16)] * 2
        + [like(8, 128, jnp.float32)] * 2,
        in_specs=in_vmem(4),
        out_specs=in_vmem(6),
        compiler_params=limit(16),
        cost_estimate=cost(NEAR_COST),
        name="near_fit",
    )(rows, metric, occ[None, :], kept[None, :])


def turn_own_kernel(rows, fit_high, fit_low, near_high, near_low, *refs):
    pieces, (out_high, out_low, high, low) = refs[:-4], refs[-4:]
    parts = halves(stacked(pieces))
    high[...], low[...] = parts
    fit = halves(dot3(halves(rows[...]), parts, 1))
    total = dot3(fit, parts, 0)
    total += dot3((fit_high[...], fit_low[...]), (near_high[...], near_low[...]), 0)
    out_high[...], out_low[...] = halves(total)


def turn_own(rows, near, pieces):
    (count, width), far = rows.shape, sum(piece.shape[0] for piece in pieces)
    return pl.pallas_call(
        turn_own_kernel,
        out_shape=[like(count, width, jnp.bfloat16)] * 2 + [like(far, width, jnp.bfloat16)] * 2,
        in_specs=in_vmem(5 + len(pieces)),
        out_specs=in_vmem(4),
        compiler_params=limit(20),
        cost_estimate=cost(12 * count * far * width),
        name="turn_own",
    )(rows, *near, *pieces)


def turn_kernel(near_high, near_low, far_high, far_low, *refs):
    cuts, (out_high, out_low) = refs[:-2], refs[-2:]
    rows = halves(stacked(cuts))
    total = 0
    for parts in ((near_high[...], near_low[...]), (far_high[...], far_low[...])):
        total += dot3(halves(dot3(rows, parts, 1)), parts, 0)
    out_high[...], out_low[...] = halves(total)


def turn(cuts, near, far):
    count, width = sum(one.shape[0] for one in cuts), cuts[0].shape[1]
    return pl.pallas_call(
        turn_kernel,
        out_shape=[like(count, width, jnp.bfloat16)] * 2,
        in_specs=in_vmem(4 + len(cuts)),
        out_specs=in_vmem(2),
        compiler_params=limit(20),
        cost_estimate=cost(12 * count * width * (near[0].shape[0] + far[0].shape[0])),
        name="turn",
    )(*near, *far, *cuts)


def spots_of(tiles):
    pairs = []
    for a in range(tiles):
        for b in range(a, tiles):
            halves_of = [(2 * a + r, 2 * b + c) for r in (0, 1) for c in (0, 1)]
            pairs += [pair for pair in halves_of if pair[0] <= pair[1]]
    return {pair: k for k, pair in enumerate(pairs)}


def row_spots(n, tiles):
    spots = spots_of(tiles)
    return {pair: k for pair, k in spots.items() if pair[0] // 2 == n or pair[1] // 2 == n}


def tail_kernel(v, tiles, scale, occ, low_occ, kept, vir, own_high, own_low, far_high, far_low, *refs):
    lows, (blocks, value), scratch = refs[:-8], refs[-8:-6], refs[-6:]
    amp, amp_t, high, low, high_t, low_t = scratch
    n = lax.axis_index("narrow")
    virtuals = v * tiles
    at = [pl.ds(pl.multiple_of(lax.rem(n - a + tiles, tiles) * v, v), v) for a in range(tiles)]
    row = jnp.concatenate([vir[:, one] for one in at], 1)
    col = jnp.broadcast_to(row, (128, virtuals)).T[:, :1]
    gap = occ[:1, :1] + low_occ[:1, :1]
    weight = kept[:1, :1]
    right = halves(stacked(lows))
    left = (own_high[...], own_low[...]), (far_high[...], far_low[...])
    pairs = [dot3(one, right, 1) for one in left]
    spans = slice(0, v), slice(v, virtuals)
    for pair, span in zip(pairs, spans):
        amp[span, :] = pair / (col[span, :] + row - gap)
    amp_t[...] = amp[...].T
    total = jnp.float32(0)
    for pair, span in zip(pairs, spans):
        total += jnp.sum(pair * (2.0 * amp[span, :] - amp_t[span, :]))
    value[...] = -weight * total / (virtuals * virtuals)
    high[...], low[...] = halves(amp[...])
    high_t[...], low_t[...] = halves(amp_t[...])
    spots, half = spots_of(tiles), v // 2
    for a in range(tiles):
        for b in range(a, tiles):
            block = dot3((high[at[a], :], low[at[a], :]), (high_t[:, at[b]], low_t[:, at[b]]), 0)
            block += dot3((high_t[at[a], :], low_t[at[a], :]), (high[:, at[b]], low[:, at[b]]), 0)
            block *= weight * scale
            for r in (0, 1):
                for c in (0, 1):
                    k = spots.get((2 * a + r, 2 * b + c))
                    if k is not None:
                        blocks[k] = block[r * half : (r + 1) * half, c * half : (c + 1) * half]


def tail(turned, raw_low, energies, v, scale):
    virtuals, width = energies[-1].shape[0], raw_low[0].shape[1]
    tiles = virtuals // v
    count = len(spots_of(tiles))
    square = [pltpu.VMEM((virtuals, virtuals), kind) for kind in (jnp.float32, jnp.bfloat16)]
    return pl.pallas_call(
        functools.partial(tail_kernel, v, tiles, scale),
        out_shape=[
            jax.ShapeDtypeStruct((count, v // 2, v // 2), jnp.float32),
            jax.ShapeDtypeStruct((1, 1), jnp.float32),
        ],
        in_specs=in_vmem(8 + len(raw_low)),
        out_specs=in_vmem(2),
        scratch_shapes=[square[0]] * 2 + [square[1]] * 4,
        compiler_params=limit(24),
        cost_estimate=cost(6 * virtuals * virtuals * width + 3 * count * v * v * virtuals),
        name="tail",
    )(*energies[:-1], energies[-1][None, :], *turned, *raw_low)


def tail_plain(turned, raw_low, energies, v, scale):
    occ, low_occ, kept, vir = energies
    virtuals = vir.shape[0]
    narrow = virtuals // v
    order = ((lax.axis_index("narrow") - jnp.arange(narrow)) % narrow * v)[:, None] + jnp.arange(v)[None, :]
    order = order.reshape(virtuals)
    weight = kept[0, 0]
    levels = vir[order]
    own_high, own_low, far_high, far_low = [one.astype(jnp.float32) for one in turned]
    left = jnp.concatenate([own_high + own_low, far_high + far_low], 0)
    pair_ints = contract(left, jnp.concatenate(raw_low, 0), 1, 1)
    amplitude = pair_ints / (levels[:, None] + levels[None, :] - occ[0, 0] - low_occ[0, 0])
    value = jnp.sum(pair_ints * (2.0 * amplitude - amplitude.T)) * -weight / (virtuals * virtuals)
    amplitude = amplitude[order][:, order]
    blocks, half = [], v // 2
    for at in range(0, virtuals, half):
        row = contract(amplitude[at : at + half], amplitude[at:], 1, 1)
        row = row + contract(amplitude[:, at : at + half], amplitude[:, at:], 0, 0)
        blocks += jnp.split(row * (weight * scale), (virtuals - at) // half, 1)
    return jnp.stack(blocks), value.reshape(1, 1)


def halved(blocks, w, bit):
    half = blocks.shape[1] // 2
    side = (w // bit) % 2
    kept = lax.dynamic_slice_in_dim(blocks, side * half, half, 1)
    given = lax.dynamic_slice_in_dim(blocks, (1 - side) * half, half, 1)
    return kept + swapped(given, "wide", bit)


def doubled(blocks, w, bit):
    other = swapped(blocks, "wide", bit)
    low = (w // bit) % 2 == 0
    return jnp.concatenate([jnp.where(low, blocks, other), jnp.where(low, other, blocks)], 1)


def quartered(blocks, w, low):
    rows, spot = blocks.shape[1] // 4, (w // low) % 4
    total = lax.dynamic_slice_in_dim(blocks, spot * rows, rows, 1)
    for flip in (3, 1, 2):
        given = lax.dynamic_slice_in_dim(blocks, (spot ^ flip) * rows, rows, 1)
        total = total + swapped(given, "wide", flip * low)
    return total


def quadrupled(blocks, w, low):
    held = [blocks] + [swapped(blocks, "wide", flip * low) for flip in (1, 2, 3)]
    spot = (w // low) % 4
    return jnp.concatenate(
        [lax.select_n(spot, *[held[at ^ mine] for mine in range(4)]) for at in range(4)], 1
    )


def own_rows(blocks, n, bit):
    wide, narrow = lax.axis_size("wide"), lax.axis_size("narrow")
    spots = [list(row_spots(m, narrow).values()) for m in range(narrow)]

    def of(m):
        picked = [jnp.concatenate([blocks[k : k + 1] for k in row]) for row in spots]
        return lax.select_n(m, *picked)

    total = of(n)
    for s in range(narrow):
        given = of((n + s) % narrow)
        for flip in (0, bit):
            if s or flip:
                steps = [
                    (w * narrow + m, (w ^ flip) * narrow + (m + s) % narrow)
                    for w in range(wide)
                    for m in range(narrow)
                ]
                total = total + lax.ppermute(given, ("wide", "narrow"), steps)
    return total


def row_of(full, m, narrow):
    held = {pair: k for k, pair in enumerate(row_spots(m, narrow))}
    for r in (0, 1):
        for c in range(2 * narrow):
            pair = (2 * m + r, c)
            yield r, c, full[held[pair]] if pair in held else full[held[c, 2 * m + r]].T


def assembled_kernel(narrow, mine, other, out):
    first = lax.rem(lax.axis_index("wide"), 2) == 0
    half = 2 * mine.shape[1]
    whole = jnp.concatenate(
        [jnp.where(first, mine[...], other[...]), jnp.where(first, other[...], mine[...])], 1
    )
    for m in range(narrow):

        @pl.when(lax.axis_index("narrow") == m)
        def _():
            for r, c, block in row_of(whole, m, narrow):
                out[r * half : (r + 1) * half, c * half : (c + 1) * half] = block


def assembled(mine, w, n, narrow):
    other = swapped(mine, "wide", 1)
    half = 2 * mine.shape[1]
    if half % 128 == 0:
        return pl.pallas_call(
            functools.partial(assembled_kernel, narrow),
            out_shape=like(2 * half, 2 * half * narrow, jnp.float32),
            in_specs=in_vmem(2),
            out_specs=in_vmem(1)[0],
            compiler_params=limit(8),
            name="assembled",
        )(mine, other)
    first = w % 2 == 0
    whole = jnp.concatenate([jnp.where(first, mine, other), jnp.where(first, other, mine)], 1)
    rows = []
    for m in range(narrow):
        blocks = [block for *_, block in row_of(whole, m, narrow)]
        spans = blocks[: 2 * narrow], blocks[2 * narrow :]
        rows.append(jnp.concatenate([jnp.concatenate(span, 1) for span in spans], 0))
    return lax.select_n(n, *rows)


def on_device(raw_ints, metric, occ_energy, vir_energy, pair_kept):
    wide, narrow = lax.axis_size("wide"), lax.axis_size("narrow")
    w, n = lax.axis_index("wide"), lax.axis_index("narrow")
    v = raw_ints.shape[1]
    virtuals = v * narrow

    near = 4
    chunks = [(0, v // 2), (v // 2, v // 2)]
    rows = metric.shape[0] // near
    piece = lax.dynamic_slice_in_dim(metric, (w % near) * rows, rows, 0)
    far = [passed_along(piece, "narrow", s) for s in range(1, narrow)]
    own = lax.dynamic_index_in_dim(raw_ints, n, 0, keepdims=False)
    raw_low = [passed_along(own, "wide", 1)]
    arrived, given = [], []
    for s in range(1, narrow):
        block = lax.dynamic_index_in_dim(after(raw_ints, own), (n + s) % narrow, 0, keepdims=False)
        parts = [block[first : first + rows] for first, rows in chunks]
        arrived += [passed_along(one, "narrow", s) for one in reversed(parts)][::-1]
        given += parts
    *fit_near, occ, kept = near_fit(after(own, *given), metric, occ_energy, pair_kept)
    low_occ = passed_along(occ, "wide", 1)
    far = [after(one, fit_near[0]) for one in far]
    far_x = [swapped(one, "wide", 2) for one in far]
    far_core = [swapped(one, "wide", 1) for one in far]
    raw_low += [passed_along(one, "wide", 1) for one in arrived[:-1]]
    far_x = [after(one, raw_low[0], arrived[0]) for one in far_x]
    far_last = [swapped(one, "wide", 1) for one in far_x]

    *own_turned, far_high, far_low = turn_own(own, fit_near, far + far_core + far_x + far_last)
    raw_low.append(passed_along(after(arrived[-1], own_turned[0], raw_low[1], low_occ), "wide", 1))
    turned = [*own_turned, *turn(arrived, fit_near[2:], (far_high, far_low))]

    form = tail if v % 128 == 0 else tail_plain
    energies = occ, low_occ, kept, vir_energy
    blocks, own_value = form(turned, raw_low, energies, v, 0.0625 / (wide * narrow))
    blocks, own_value, w, n = lax.optimization_barrier((blocks, own_value, w, n))
    own_value = own_value.reshape(1)
    upper_value = passed_along(own_value, "wide", -1)

    first, *bits, last = [1 << k for k in range(wide.bit_length() - 1)]
    low, bits = bits[0], bits[2:]
    blocks = halved(blocks, w, first)
    blocks = quartered(blocks, w, low)
    blocks, upper_value = lax.optimization_barrier((blocks, upper_value))
    for bit in bits:
        blocks = halved(blocks, w, bit)
    full = own_rows(blocks, n, last)
    for bit in reversed(bits):
        full = doubled(full, w, bit)
    full = quadrupled(full, w, low)
    return assembled(full, w, n, narrow), own_value + upper_value


def solution(mesh):
    placed = (
        P("wide", "narrow", None),
        P("narrow", None),
        P(("wide", "narrow")),
        P(),
        P(("wide", "narrow")),
    )
    return jax.shard_map(
        on_device,
        mesh=mesh,
        in_specs=placed,
        out_specs=(P("narrow", None), P(("wide", "narrow"))),
        check_vma=False,
    )
```

```python
import functools

import jax
import jax.numpy as jnp
from jax import lax
from jax.experimental import pallas as pl
from jax.experimental.pallas import tpu as pltpu
from jax.sharding import PartitionSpec as P

PASSES = lax.Precision.HIGH
VMEM = pltpu.MemorySpace.VMEM
NEAR_COST = 15_000_000_000
EXTRA = 8


def contract(left, right, left_dim, right_dim):
    return lax.dot_general(
        left,
        right,
        (((left_dim,), (right_dim,)), ((), ())),
        precision=PASSES,
        preferred_element_type=jnp.float32,
    )


def passed_along(shard, axis, by):
    size = lax.axis_size(axis)
    return lax.ppermute(shard, axis, [(i, (i + by) % size) for i in range(size)])


def swapped(shard, axis, bit):
    size = lax.axis_size(axis)
    return lax.ppermute(shard, axis, [(i, i ^ bit) for i in range(size)])


def after(value, *gates):
    return lax.optimization_barrier((value,) + gates)[0]


def in_vmem(count):
    return [pl.BlockSpec(memory_space=VMEM)] * count


def limit(mib):
    return pltpu.CompilerParams(vmem_limit_bytes=mib * 2**20)


def cost(flops):
    return pl.CostEstimate(flops=flops, bytes_accessed=0, transcendentals=0)


def halves(value):
    high = value.astype(jnp.bfloat16)
    low = (value - high.astype(jnp.float32)).astype(jnp.bfloat16)
    return high, low


def dot3(left, right, right_dim):
    (lh, ll), (rh, rl) = left, right
    dims = (((1,), (right_dim,)), ((), ()))
    total = lax.dot_general(ll, rh, dims, preferred_element_type=jnp.float32)
    total += lax.dot_general(lh, rl, dims, preferred_element_type=jnp.float32)
    return total + lax.dot_general(lh, rh, dims, preferred_element_type=jnp.float32)


def stacked(refs):
    return jnp.concatenate([one[...] for one in refs], 0)


def like(rows, width, dtype):
    return jax.ShapeDtypeStruct((rows, width), dtype)


def near_fit_kernel(rows, metric, kept, fit_high, fit_low, high, low, kept_tile):
    parts = halves(metric[...])
    high[...], low[...] = parts
    fit_high[...], fit_low[...] = halves(dot3(halves(rows[: fit_high.shape[0]]), parts, 1))
    kept_tile[...] = jnp.broadcast_to(kept[...].astype(jnp.float32), kept_tile.shape)


def near_fit(rows, metric, kept):
    (count, width), near = rows.shape, metric.shape[0]
    count -= EXTRA
    return pl.pallas_call(
        near_fit_kernel,
        out_shape=[like(count, near, jnp.bfloat16)] * 2
        + [like(near, width, jnp.bfloat16)] * 2
        + [like(8, 128, jnp.float32)],
        in_specs=in_vmem(3),
        out_specs=in_vmem(5),
        compiler_params=limit(16),
        cost_estimate=cost(NEAR_COST),
        name="near_fit",
    )(rows, metric, kept[None, :])


def turn_own_kernel(rows, fit_high, fit_low, near_high, near_low, *refs):
    pieces, (out_high, out_low, high, low) = refs[:-4], refs[-4:]
    parts = halves(stacked(pieces))
    high[...], low[...] = parts
    fit = halves(dot3(halves(rows[: out_high.shape[0]]), parts, 1))
    total = dot3(fit, parts, 0)
    total += dot3((fit_high[...], fit_low[...]), (near_high[...], near_low[...]), 0)
    out_high[...], out_low[...] = halves(total)


def turn_own(rows, near, pieces):
    (count, width), far = rows.shape, sum(piece.shape[0] for piece in pieces)
    count -= EXTRA
    return pl.pallas_call(
        turn_own_kernel,
        out_shape=[like(count, width, jnp.bfloat16)] * 2 + [like(far, width, jnp.bfloat16)] * 2,
        in_specs=in_vmem(5 + len(pieces)),
        out_specs=in_vmem(4),
        compiler_params=limit(20),
        cost_estimate=cost(12 * count * far * width),
        name="turn_own",
    )(rows, *near, *pieces)


def turn_kernel(near_high, near_low, far_high, far_low, *refs):
    cuts, (out_high, out_low) = refs[:-2], refs[-2:]
    rows = halves(stacked(cuts))
    total = 0
    for parts in ((near_high[...], near_low[...]), (far_high[...], far_low[...])):
        total += dot3(halves(dot3(rows, parts, 1)), parts, 0)
    out_high[...], out_low[...] = halves(total)


def turn(cuts, near, far):
    count, width = sum(one.shape[0] for one in cuts), cuts[0].shape[1]
    return pl.pallas_call(
        turn_kernel,
        out_shape=[like(count, width, jnp.bfloat16)] * 2,
        in_specs=in_vmem(4 + len(cuts)),
        out_specs=in_vmem(2),
        compiler_params=limit(20),
        cost_estimate=cost(12 * count * width * (near[0].shape[0] + far[0].shape[0])),
        name="turn",
    )(*near, *far, *cuts)


def spots_of(tiles):
    pairs = []
    for a in range(tiles):
        for b in range(a, tiles):
            halves_of = [(2 * a + r, 2 * b + c) for r in (0, 1) for c in (0, 1)]
            pairs += [pair for pair in halves_of if pair[0] <= pair[1]]
    return {pair: k for k, pair in enumerate(pairs)}


def row_spots(n, tiles):
    spots = spots_of(tiles)
    return {pair: k for pair, k in spots.items() if pair[0] // 2 == n or pair[1] // 2 == n}


def tail_kernel(v, tiles, scale, own, kept, vir, own_high, own_low, far_high, far_low, *refs):
    lows, (blocks, value), scratch = refs[:-8], refs[-8:-6], refs[-6:]
    amp, amp_t, high, low, high_t, low_t = scratch
    n = lax.axis_index("narrow")
    virtuals = v * tiles
    at = [pl.ds(pl.multiple_of(lax.rem(n - a + tiles, tiles) * v, v), v) for a in range(tiles)]
    row = jnp.concatenate([vir[:, one] for one in at], 1)
    col = jnp.broadcast_to(row, (128, virtuals)).T[:, :1]
    gap = own[v : v + 1, :1] + lows[0][v : v + 1, :1]
    weight = kept[:1, :1]
    right = halves(jnp.concatenate([lows[0][:v]] + [one[...] for one in lows[1:]], 0))
    left = (own_high[...], own_low[...]), (far_high[...], far_low[...])
    pairs = [dot3(one, right, 1) for one in left]
    spans = slice(0, v), slice(v, virtuals)
    for pair, span in zip(pairs, spans):
        amp[span, :] = pair / (col[span, :] + row - gap)
    amp_t[...] = amp[...].T
    total = jnp.float32(0)
    for pair, span in zip(pairs, spans):
        total += jnp.sum(pair * (2.0 * amp[span, :] - amp_t[span, :]))
    value[...] = -weight * total / (virtuals * virtuals)
    high[...], low[...] = halves(amp[...])
    high_t[...], low_t[...] = halves(amp_t[...])
    spots, half = spots_of(tiles), v // 2
    for a in range(tiles):
        for b in range(a, tiles):
            block = dot3((high[at[a], :], low[at[a], :]), (high_t[:, at[b]], low_t[:, at[b]]), 0)
            block += dot3((high_t[at[a], :], low_t[at[a], :]), (high[:, at[b]], low[:, at[b]]), 0)
            block *= weight * scale
            for r in (0, 1):
                for c in (0, 1):
                    k = spots.get((2 * a + r, 2 * b + c))
                    if k is not None:
                        blocks[k] = block[r * half : (r + 1) * half, c * half : (c + 1) * half]


def tail(turned, raw_low, energies, v, scale):
    virtuals, width = energies[-1].shape[0], raw_low[0].shape[1]
    tiles = virtuals // v
    count = len(spots_of(tiles))
    square = [pltpu.VMEM((virtuals, virtuals), kind) for kind in (jnp.float32, jnp.bfloat16)]
    return pl.pallas_call(
        functools.partial(tail_kernel, v, tiles, scale),
        out_shape=[
            jax.ShapeDtypeStruct((count, v // 2, v // 2), jnp.float32),
            jax.ShapeDtypeStruct((1, 1), jnp.float32),
        ],
        in_specs=in_vmem(7 + len(raw_low)),
        out_specs=in_vmem(2),
        scratch_shapes=[square[0]] * 2 + [square[1]] * 4,
        compiler_params=limit(24),
        cost_estimate=cost(6 * virtuals * virtuals * width + 3 * count * v * v * virtuals),
        name="tail",
    )(*energies[:-1], energies[-1][None, :], *turned, *raw_low)


def tail_plain(turned, raw_low, energies, v, scale):
    own, kept, vir = energies
    virtuals = vir.shape[0]
    narrow = virtuals // v
    order = ((lax.axis_index("narrow") - jnp.arange(narrow)) % narrow * v)[:, None] + jnp.arange(v)[None, :]
    order = order.reshape(virtuals)
    weight = kept[0, 0]
    levels = vir[order]
    own_high, own_low, far_high, far_low = [one.astype(jnp.float32) for one in turned]
    left = jnp.concatenate([own_high + own_low, far_high + far_low], 0)
    pair_ints = contract(left, jnp.concatenate([raw_low[0][:v]] + raw_low[1:], 0), 1, 1)
    amplitude = pair_ints / (levels[:, None] + levels[None, :] - own[v, 0] - raw_low[0][v, 0])
    value = jnp.sum(pair_ints * (2.0 * amplitude - amplitude.T)) * -weight / (virtuals * virtuals)
    amplitude = amplitude[order][:, order]
    blocks, half = [], v // 2
    for at in range(0, virtuals, half):
        row = contract(amplitude[at : at + half], amplitude[at:], 1, 1)
        row = row + contract(amplitude[:, at : at + half], amplitude[:, at:], 0, 0)
        blocks += jnp.split(row * (weight * scale), (virtuals - at) // half, 1)
    return jnp.stack(blocks), value.reshape(1, 1)


def halved(blocks, w, bit):
    half = blocks.shape[1] // 2
    side = (w // bit) % 2
    kept = lax.dynamic_slice_in_dim(blocks, side * half, half, 1)
    given = lax.dynamic_slice_in_dim(blocks, (1 - side) * half, half, 1)
    return kept + swapped(given, "wide", bit)


def doubled(blocks, w, bit):
    other = swapped(blocks, "wide", bit)
    low = (w // bit) % 2 == 0
    return jnp.concatenate([jnp.where(low, blocks, other), jnp.where(low, other, blocks)], 1)


def quartered(blocks, w, low):
    rows, spot = blocks.shape[1] // 4, (w // low) % 4
    total = lax.dynamic_slice_in_dim(blocks, spot * rows, rows, 1)
    for flip in (3, 1, 2):
        given = lax.dynamic_slice_in_dim(blocks, (spot ^ flip) * rows, rows, 1)
        total = total + swapped(given, "wide", flip * low)
    return total


def quadrupled(blocks, w, low):
    held = [blocks] + [swapped(blocks, "wide", flip * low) for flip in (1, 2, 3)]
    spot = (w // low) % 4
    return jnp.concatenate(
        [lax.select_n(spot, *[held[at ^ mine] for mine in range(4)]) for at in range(4)], 1
    )


def own_rows(blocks, n, bit):
    wide, narrow = lax.axis_size("wide"), lax.axis_size("narrow")
    spots = [list(row_spots(m, narrow).values()) for m in range(narrow)]

    def of(m):
        picked = [jnp.concatenate([blocks[k : k + 1] for k in row]) for row in spots]
        return lax.select_n(m, *picked)

    total = of(n)
    for s in range(narrow):
        given = of((n + s) % narrow)
        for flip in (0, bit):
            if s or flip:
                steps = [
                    (w * narrow + m, (w ^ flip) * narrow + (m + s) % narrow)
                    for w in range(wide)
                    for m in range(narrow)
                ]
                total = total + lax.ppermute(given, ("wide", "narrow"), steps)
    return total


def row_of(full, m, narrow):
    held = {pair: k for k, pair in enumerate(row_spots(m, narrow))}
    for r in (0, 1):
        for c in range(2 * narrow):
            pair = (2 * m + r, c)
            yield r, c, full[held[pair]] if pair in held else full[held[c, 2 * m + r]].T


def assembled_kernel(narrow, mine, other, out):
    first = lax.rem(lax.axis_index("wide"), 2) == 0
    half = 2 * mine.shape[1]
    whole = jnp.concatenate(
        [jnp.where(first, mine[...], other[...]), jnp.where(first, other[...], mine[...])], 1
    )
    for m in range(narrow):

        @pl.when(lax.axis_index("narrow") == m)
        def _():
            for r, c, block in row_of(whole, m, narrow):
                out[r * half : (r + 1) * half, c * half : (c + 1) * half] = block


def assembled(mine, w, n, narrow):
    other = swapped(mine, "wide", 1)
    half = 2 * mine.shape[1]
    if half % 128 == 0:
        return pl.pallas_call(
            functools.partial(assembled_kernel, narrow),
            out_shape=like(2 * half, 2 * half * narrow, jnp.float32),
            in_specs=in_vmem(2),
            out_specs=in_vmem(1)[0],
            compiler_params=limit(8),
            name="assembled",
        )(mine, other)
    first = w % 2 == 0
    whole = jnp.concatenate([jnp.where(first, mine, other), jnp.where(first, other, mine)], 1)
    rows = []
    for m in range(narrow):
        blocks = [block for *_, block in row_of(whole, m, narrow)]
        spans = blocks[: 2 * narrow], blocks[2 * narrow :]
        rows.append(jnp.concatenate([jnp.concatenate(span, 1) for span in spans], 0))
    return lax.select_n(n, *rows)


def on_device(raw_ints, metric, occ_energy, vir_energy, pair_kept):
    wide, narrow = lax.axis_size("wide"), lax.axis_size("narrow")
    w, n = lax.axis_index("wide"), lax.axis_index("narrow")
    v = raw_ints.shape[1]
    virtuals = v * narrow

    near = 4
    chunks = [(0, 6 * v // 8), (6 * v // 8, 2 * v // 8)]
    rows = metric.shape[0] // near
    piece = lax.dynamic_slice_in_dim(metric, (w % near) * rows, rows, 0)
    far = [passed_along(piece, "narrow", s) for s in range(1, narrow)]
    own = lax.dynamic_index_in_dim(raw_ints, n, 0, keepdims=False)
    own = jnp.concatenate([own, jnp.broadcast_to(occ_energy, (EXTRA, own.shape[1]))], 0)
    raw_low = [passed_along(own, "wide", 1)]
    arrived, given = [], []
    for s in range(1, narrow):
        block = lax.dynamic_index_in_dim(after(raw_ints, own), (n + s) % narrow, 0, keepdims=False)
        parts = [block[first : first + rows] for first, rows in chunks]
        arrived += [passed_along(one, "narrow", s) for one in reversed(parts)][::-1]
        given += parts
    *fit_near, kept = near_fit(after(own, *given), metric, pair_kept)
    far = [after(one, fit_near[0]) for one in far]
    far_x = [swapped(one, "wide", 2) for one in far]
    far_core = [swapped(one, "wide", 1) for one in far]
    raw_low += [passed_along(one, "wide", 1) for one in arrived[:-1]]
    far_x = [after(one, raw_low[0], arrived[0]) for one in far_x]
    far_last = [swapped(one, "wide", 1) for one in far_x]

    *own_turned, far_high, far_low = turn_own(own, fit_near, far + far_core + far_x + far_last)
    raw_low.append(passed_along(after(arrived[-1], own_turned[0]), "wide", 1))
    turned = [*own_turned, *turn(arrived, fit_near[2:], (far_high, far_low))]

    form = tail if v % 128 == 0 else tail_plain
    energies = own, kept, vir_energy
    blocks, own_value = form(turned, raw_low, energies, v, 0.0625 / (wide * narrow))
    blocks, own_value, w, n = lax.optimization_barrier((blocks, own_value, w, n))
    own_value = own_value.reshape(1)
    upper_value = passed_along(own_value, "wide", -1)

    first, *bits, last = [1 << k for k in range(wide.bit_length() - 1)]
    low, bits = bits[0], bits[2:]
    blocks = halved(blocks, w, first)
    blocks = quartered(blocks, w, low)
    blocks, upper_value = lax.optimization_barrier((blocks, upper_value))
    for bit in bits:
        blocks = halved(blocks, w, bit)
    full = own_rows(blocks, n, last)
    for bit in reversed(bits):
        full = doubled(full, w, bit)
    full = quadrupled(full, w, low)
    return assembled(full, w, n, narrow), own_value + upper_value


def solution(mesh):
    placed = (
        P("wide", "narrow", None),
        P("narrow", None),
        P(("wide", "narrow")),
        P(),
        P(("wide", "narrow")),
    )
    return jax.shard_map(
        on_device,
        mesh=mesh,
        in_specs=placed,
        out_specs=(P("narrow", None), P(("wide", "narrow"))),
        check_vma=False,
    )
```

```python
import functools

import jax
import jax.numpy as jnp
from jax import lax
from jax.experimental import pallas as pl
from jax.experimental.pallas import tpu as pltpu
from jax.sharding import PartitionSpec as P

PASSES = lax.Precision.HIGH
VMEM = pltpu.MemorySpace.VMEM
NEAR_COST = 15_000_000_000
EXTRA = 8


def contract(left, right, left_dim, right_dim):
    return lax.dot_general(
        left,
        right,
        (((left_dim,), (right_dim,)), ((), ())),
        precision=PASSES,
        preferred_element_type=jnp.float32,
    )


def passed_along(shard, axis, by):
    size = lax.axis_size(axis)
    return lax.ppermute(shard, axis, [(i, (i + by) % size) for i in range(size)])


def swapped(shard, axis, bit):
    size = lax.axis_size(axis)
    return lax.ppermute(shard, axis, [(i, i ^ bit) for i in range(size)])


def after(value, *gates):
    return lax.optimization_barrier((value,) + gates)[0]


def in_vmem(count):
    return [pl.BlockSpec(memory_space=VMEM)] * count


def limit(mib):
    return pltpu.CompilerParams(vmem_limit_bytes=mib * 2**20)


def cost(flops):
    return pl.CostEstimate(flops=flops, bytes_accessed=0, transcendentals=0)


def halves(value):
    high = value.astype(jnp.bfloat16)
    low = (value - high.astype(jnp.float32)).astype(jnp.bfloat16)
    return high, low


def dot3(left, right, right_dim):
    (lh, ll), (rh, rl) = left, right
    dims = (((1,), (right_dim,)), ((), ()))
    total = lax.dot_general(ll, rh, dims, preferred_element_type=jnp.float32)
    total += lax.dot_general(lh, rl, dims, preferred_element_type=jnp.float32)
    return total + lax.dot_general(lh, rh, dims, preferred_element_type=jnp.float32)


def stacked(refs):
    return jnp.concatenate([one[...] for one in refs], 0)


def like(rows, width, dtype):
    return jax.ShapeDtypeStruct((rows, width), dtype)


def near_fit_kernel(rows, metric, kept, fit_high, fit_low, high, low, kept_tile):
    parts = halves(metric[...])
    high[...], low[...] = parts
    fit_high[...], fit_low[...] = halves(dot3(halves(rows[: fit_high.shape[0]]), parts, 1))
    kept_tile[...] = jnp.broadcast_to(kept[...].astype(jnp.float32), kept_tile.shape)


def near_fit(rows, metric, kept):
    (count, width), near = rows.shape, metric.shape[0]
    count -= EXTRA
    return pl.pallas_call(
        near_fit_kernel,
        out_shape=[like(count, near, jnp.bfloat16)] * 2
        + [like(near, width, jnp.bfloat16)] * 2
        + [like(8, 128, jnp.float32)],
        in_specs=in_vmem(3),
        out_specs=in_vmem(5),
        compiler_params=limit(16),
        cost_estimate=cost(NEAR_COST),
        name="near_fit",
    )(rows, metric, kept[None, :])


def turn_own_kernel(rows, fit_high, fit_low, near_high, near_low, *refs):
    pieces, (out_high, out_low, high, low) = refs[:-4], refs[-4:]
    parts = halves(stacked(pieces))
    high[...], low[...] = parts
    fit = halves(dot3(halves(rows[: out_high.shape[0]]), parts, 1))
    total = dot3(fit, parts, 0)
    total += dot3((fit_high[...], fit_low[...]), (near_high[...], near_low[...]), 0)
    out_high[...], out_low[...] = halves(total)


def turn_own(rows, near, pieces):
    (count, width), far = rows.shape, sum(piece.shape[0] for piece in pieces)
    count -= EXTRA
    return pl.pallas_call(
        turn_own_kernel,
        out_shape=[like(count, width, jnp.bfloat16)] * 2 + [like(far, width, jnp.bfloat16)] * 2,
        in_specs=in_vmem(5 + len(pieces)),
        out_specs=in_vmem(4),
        compiler_params=limit(20),
        cost_estimate=cost(12 * count * far * width),
        name="turn_own",
    )(rows, *near, *pieces)


def turn_kernel(near_high, near_low, far_high, far_low, *refs):
    cuts, (out_high, out_low) = refs[:-2], refs[-2:]
    rows = halves(stacked(cuts))
    total = 0
    for parts in ((near_high[...], near_low[...]), (far_high[...], far_low[...])):
        total += dot3(halves(dot3(rows, parts, 1)), parts, 0)
    out_high[...], out_low[...] = halves(total)


def turn(cuts, near, far):
    count, width = sum(one.shape[0] for one in cuts), cuts[0].shape[1]
    return pl.pallas_call(
        turn_kernel,
        out_shape=[like(count, width, jnp.bfloat16)] * 2,
        in_specs=in_vmem(4 + len(cuts)),
        out_specs=in_vmem(2),
        compiler_params=limit(20),
        cost_estimate=cost(12 * count * width * (near[0].shape[0] + far[0].shape[0])),
        name="turn",
    )(*near, *far, *cuts)


def spots_of(tiles):
    pairs = []
    for a in range(tiles):
        for b in range(a, tiles):
            halves_of = [(2 * a + r, 2 * b + c) for r in (0, 1) for c in (0, 1)]
            pairs += [pair for pair in halves_of if pair[0] <= pair[1]]
    return {pair: k for k, pair in enumerate(pairs)}


def row_spots(n, tiles):
    spots = spots_of(tiles)
    return {pair: k for pair, k in spots.items() if pair[0] // 2 == n or pair[1] // 2 == n}


def tail_kernel(v, tiles, scale, own, kept, vir, own_high, own_low, far_high, far_low, *refs):
    lows, (blocks, value), scratch = refs[:-8], refs[-8:-6], refs[-6:]
    amp, amp_t, high, low, high_t, low_t = scratch
    n = lax.axis_index("narrow")
    virtuals = v * tiles
    at = [pl.ds(pl.multiple_of(lax.rem(n - a + tiles, tiles) * v, v), v) for a in range(tiles)]
    row = jnp.concatenate([vir[:, one] for one in at], 1)
    col = jnp.broadcast_to(row, (128, virtuals)).T[:, :1]
    gap = own[v : v + 1, :1] + lows[0][v : v + 1, :1]
    weight = kept[:1, :1]
    right = halves(jnp.concatenate([lows[0][:v]] + [one[...] for one in lows[1:]], 0))
    left = (own_high[...], own_low[...]), (far_high[...], far_low[...])
    pairs = [dot3(one, right, 1) for one in left]
    spans = slice(0, v), slice(v, virtuals)
    for pair, span in zip(pairs, spans):
        amp[span, :] = pair / (col[span, :] + row - gap)
    amp_t[...] = amp[...].T
    total = jnp.float32(0)
    for pair, span in zip(pairs, spans):
        total += jnp.sum(pair * (2.0 * amp[span, :] - amp_t[span, :]))
    value[...] = -weight * total / (virtuals * virtuals)
    high[...], low[...] = halves(amp[...])
    high_t[...], low_t[...] = halves(amp_t[...])
    spots, half = spots_of(tiles), v // 2
    for a in range(tiles):
        for b in range(a, tiles):
            block = dot3((high[at[a], :], low[at[a], :]), (high_t[:, at[b]], low_t[:, at[b]]), 0)
            block += dot3((high_t[at[a], :], low_t[at[a], :]), (high[:, at[b]], low[:, at[b]]), 0)
            block *= weight * scale
            for r in (0, 1):
                for c in (0, 1):
                    k = spots.get((2 * a + r, 2 * b + c))
                    if k is not None:
                        blocks[k] = block[r * half : (r + 1) * half, c * half : (c + 1) * half]


def tail(turned, raw_low, energies, v, scale):
    virtuals, width = energies[-1].shape[0], raw_low[0].shape[1]
    tiles = virtuals // v
    count = len(spots_of(tiles))
    square = [pltpu.VMEM((virtuals, virtuals), kind) for kind in (jnp.float32, jnp.bfloat16)]
    return pl.pallas_call(
        functools.partial(tail_kernel, v, tiles, scale),
        out_shape=[
            jax.ShapeDtypeStruct((count, v // 2, v // 2), jnp.float32),
            jax.ShapeDtypeStruct((1, 1), jnp.float32),
        ],
        in_specs=in_vmem(7 + len(raw_low)),
        out_specs=in_vmem(2),
        scratch_shapes=[square[0]] * 2 + [square[1]] * 4,
        compiler_params=limit(24),
        cost_estimate=cost(6 * virtuals * virtuals * width + 3 * count * v * v * virtuals),
        name="tail",
    )(*energies[:-1], energies[-1][None, :], *turned, *raw_low)


def tail_plain(turned, raw_low, energies, v, scale):
    own, kept, vir = energies
    virtuals = vir.shape[0]
    narrow = virtuals // v
    order = ((lax.axis_index("narrow") - jnp.arange(narrow)) % narrow * v)[:, None] + jnp.arange(v)[None, :]
    order = order.reshape(virtuals)
    weight = kept[0, 0]
    levels = vir[order]
    own_high, own_low, far_high, far_low = [one.astype(jnp.float32) for one in turned]
    left = jnp.concatenate([own_high + own_low, far_high + far_low], 0)
    pair_ints = contract(left, jnp.concatenate([raw_low[0][:v]] + raw_low[1:], 0), 1, 1)
    amplitude = pair_ints / (levels[:, None] + levels[None, :] - own[v, 0] - raw_low[0][v, 0])
    value = jnp.sum(pair_ints * (2.0 * amplitude - amplitude.T)) * -weight / (virtuals * virtuals)
    amplitude = amplitude[order][:, order]
    blocks, half = [], v // 2
    for at in range(0, virtuals, half):
        row = contract(amplitude[at : at + half], amplitude[at:], 1, 1)
        row = row + contract(amplitude[:, at : at + half], amplitude[:, at:], 0, 0)
        blocks += jnp.split(row * (weight * scale), (virtuals - at) // half, 1)
    return jnp.stack(blocks), value.reshape(1, 1)


def halved(blocks, w, bit):
    half = blocks.shape[1] // 2
    side = (w // bit) % 2
    kept = lax.dynamic_slice_in_dim(blocks, side * half, half, 1)
    given = lax.dynamic_slice_in_dim(blocks, (1 - side) * half, half, 1)
    return kept + swapped(given, "wide", bit)


def doubled(blocks, w, bit):
    other = swapped(blocks, "wide", bit)
    low = (w // bit) % 2 == 0
    return jnp.concatenate([jnp.where(low, blocks, other), jnp.where(low, other, blocks)], 1)


def quartered(blocks, w, low):
    rows, spot = blocks.shape[1] // 4, (w // low) % 4
    total = lax.dynamic_slice_in_dim(blocks, spot * rows, rows, 1)
    for flip in (3, 1, 2):
        given = lax.dynamic_slice_in_dim(blocks, (spot ^ flip) * rows, rows, 1)
        total = total + swapped(given, "wide", flip * low)
    return total


def quadrupled(blocks, w, low):
    held = [blocks] + [swapped(blocks, "wide", flip * low) for flip in (1, 2, 3)]
    spot = (w // low) % 4
    return jnp.concatenate(
        [lax.select_n(spot, *[held[at ^ mine] for mine in range(4)]) for at in range(4)], 1
    )


def own_rows(blocks, n, bit):
    wide, narrow = lax.axis_size("wide"), lax.axis_size("narrow")
    spots = [list(row_spots(m, narrow).values()) for m in range(narrow)]

    def of(m):
        picked = [jnp.concatenate([blocks[k : k + 1] for k in row]) for row in spots]
        return lax.select_n(m, *picked)

    total = of(n)
    for s in range(narrow):
        given = of((n + s) % narrow)
        for flip in (0, bit):
            if s or flip:
                steps = [
                    (w * narrow + m, (w ^ flip) * narrow + (m + s) % narrow)
                    for w in range(wide)
                    for m in range(narrow)
                ]
                total = total + lax.ppermute(given, ("wide", "narrow"), steps)
    return total


def row_of(full, m, narrow):
    held = {pair: k for k, pair in enumerate(row_spots(m, narrow))}
    for r in (0, 1):
        for c in range(2 * narrow):
            pair = (2 * m + r, c)
            yield r, c, full[held[pair]] if pair in held else full[held[c, 2 * m + r]].T


def assembled_kernel(narrow, mine, other, out):
    first = lax.rem(lax.axis_index("wide"), 2) == 0
    half = 2 * mine.shape[1]
    whole = jnp.concatenate(
        [jnp.where(first, mine[...], other[...]), jnp.where(first, other[...], mine[...])], 1
    )
    for m in range(narrow):

        @pl.when(lax.axis_index("narrow") == m)
        def _():
            for r, c, block in row_of(whole, m, narrow):
                out[r * half : (r + 1) * half, c * half : (c + 1) * half] = block


def assembled(mine, w, n, narrow):
    other = swapped(mine, "wide", 1)
    half = 2 * mine.shape[1]
    if half % 128 == 0:
        return pl.pallas_call(
            functools.partial(assembled_kernel, narrow),
            out_shape=like(2 * half, 2 * half * narrow, jnp.float32),
            in_specs=in_vmem(2),
            out_specs=in_vmem(1)[0],
            compiler_params=limit(8),
            name="assembled",
        )(mine, other)
    first = w % 2 == 0
    whole = jnp.concatenate([jnp.where(first, mine, other), jnp.where(first, other, mine)], 1)
    rows = []
    for m in range(narrow):
        blocks = [block for *_, block in row_of(whole, m, narrow)]
        spans = blocks[: 2 * narrow], blocks[2 * narrow :]
        rows.append(jnp.concatenate([jnp.concatenate(span, 1) for span in spans], 0))
    return lax.select_n(n, *rows)


def on_device(raw_ints, metric, occ_energy, vir_energy, pair_kept):
    wide, narrow = lax.axis_size("wide"), lax.axis_size("narrow")
    w, n = lax.axis_index("wide"), lax.axis_index("narrow")
    v = raw_ints.shape[1]
    virtuals = v * narrow

    near = 4
    chunks = [(0, v // 2), (v // 2, v // 2)]
    rows = metric.shape[0] // near
    piece = lax.dynamic_slice_in_dim(metric, (w % near) * rows, rows, 0)
    far = [passed_along(piece, "narrow", s) for s in range(1, narrow)]
    own = lax.dynamic_index_in_dim(raw_ints, n, 0, keepdims=False)
    own = jnp.concatenate([own, jnp.broadcast_to(occ_energy, (EXTRA, own.shape[1]))], 0)
    raw_low = [passed_along(own, "wide", 1)]
    arrived, given = [], []
    for s in range(1, narrow):
        block = lax.dynamic_index_in_dim(after(raw_ints, own), (n + s) % narrow, 0, keepdims=False)
        parts = [block[first : first + rows] for first, rows in chunks]
        arrived += [passed_along(one, "narrow", s) for one in reversed(parts)][::-1]
        given += parts
    *fit_near, kept = near_fit(after(own, *given), metric, pair_kept)
    far = [after(one, fit_near[0]) for one in far]
    far_x = [swapped(one, "wide", 2) for one in far]
    far_core = [swapped(one, "wide", 1) for one in far]
    raw_low += [passed_along(one, "wide", 1) for one in arrived[:-1]]
    far_x = [after(one, raw_low[0], arrived[0]) for one in far_x]
    far_last = [swapped(one, "wide", 1) for one in far_x]

    *own_turned, far_high, far_low = turn_own(own, fit_near, far + far_core + far_x + far_last)
    raw_low.append(passed_along(after(arrived[-1], own_turned[0]), "wide", 1))
    turned = [*own_turned, *turn(arrived, fit_near[2:], (far_high, far_low))]

    form = tail if v % 128 == 0 else tail_plain
    energies = own, kept, vir_energy
    blocks, own_value = form(turned, raw_low, energies, v, 0.0625 / (wide * narrow))
    blocks, own_value, w, n = lax.optimization_barrier((blocks, own_value, w, n))
    own_value = own_value.reshape(1)
    upper_value = passed_along(own_value, "wide", -1)

    first, *bits, last = [1 << k for k in range(wide.bit_length() - 1)]
    low, bits = bits[0], bits[2:]
    blocks = halved(blocks, w, first)
    blocks = quartered(blocks, w, low)
    blocks, upper_value = lax.optimization_barrier((blocks, upper_value))
    for bit in bits:
        blocks = halved(blocks, w, bit)
    full = own_rows(blocks, n, last)
    for bit in reversed(bits):
        full = doubled(full, w, bit)
    full = quadrupled(full, w, low)
    return assembled(full, w, n, narrow), own_value + upper_value


def solution(mesh):
    placed = (
        P("wide", "narrow", None),
        P("narrow", None),
        P(("wide", "narrow")),
        P(),
        P(("wide", "narrow")),
    )
    return jax.shard_map(
        on_device,
        mesh=mesh,
        in_specs=placed,
        out_specs=(P("narrow", None), P(("wide", "narrow"))),
        check_vma=False,
    )
```

```python
import functools

import jax
import jax.numpy as jnp
from jax import lax
from jax.experimental import pallas as pl
from jax.experimental.pallas import tpu as pltpu
from jax.sharding import PartitionSpec as P

PASSES = lax.Precision.HIGH
VMEM = pltpu.MemorySpace.VMEM
NEAR_COST = 15_000_000_000


def contract(left, right, left_dim, right_dim):
    return lax.dot_general(
        left,
        right,
        (((left_dim,), (right_dim,)), ((), ())),
        precision=PASSES,
        preferred_element_type=jnp.float32,
    )


def passed_along(shard, axis, by):
    size = lax.axis_size(axis)
    return lax.ppermute(shard, axis, [(i, (i + by) % size) for i in range(size)])


def swapped(shard, axis, bit):
    size = lax.axis_size(axis)
    return lax.ppermute(shard, axis, [(i, i ^ bit) for i in range(size)])


def after(value, *gates):
    return lax.optimization_barrier((value,) + gates)[0]


def in_vmem(count):
    return [pl.BlockSpec(memory_space=VMEM)] * count


def limit(mib):
    return pltpu.CompilerParams(vmem_limit_bytes=mib * 2**20)


def cost(flops):
    return pl.CostEstimate(flops=flops, bytes_accessed=0, transcendentals=0)


def halves(value):
    high = value.astype(jnp.bfloat16)
    low = (value - high.astype(jnp.float32)).astype(jnp.bfloat16)
    return high, low


def dot3(left, right, right_dim):
    (lh, ll), (rh, rl) = left, right
    dims = (((1,), (right_dim,)), ((), ()))
    total = lax.dot_general(ll, rh, dims, preferred_element_type=jnp.float32)
    total += lax.dot_general(lh, rl, dims, preferred_element_type=jnp.float32)
    return total + lax.dot_general(lh, rh, dims, preferred_element_type=jnp.float32)


def stacked(refs):
    return jnp.concatenate([one[...] for one in refs], 0)


def like(rows, width, dtype):
    return jax.ShapeDtypeStruct((rows, width), dtype)


def near_fit_kernel(rows, metric, occ, kept, fit_high, fit_low, high, low, occ_tile, kept_tile):
    parts = halves(metric[...])
    high[...], low[...] = parts
    fit_high[...], fit_low[...] = halves(dot3(halves(rows[...]), parts, 1))
    occ_tile[...] = jnp.broadcast_to(occ[...], occ_tile.shape)
    kept_tile[...] = jnp.broadcast_to(kept[...].astype(jnp.float32), kept_tile.shape)


def near_fit(rows, metric, occ, kept):
    (count, width), near = rows.shape, metric.shape[0]
    return pl.pallas_call(
        near_fit_kernel,
        out_shape=[like(count, near, jnp.bfloat16)] * 2
        + [like(near, width, jnp.bfloat16)] * 2
        + [like(8, 128, jnp.float32)] * 2,
        in_specs=in_vmem(4),
        out_specs=in_vmem(6),
        compiler_params=limit(16),
        cost_estimate=cost(NEAR_COST),
        name="near_fit",
    )(rows, metric, occ[None, :], kept[None, :])


def turn_own_kernel(rows, fit_high, fit_low, near_high, near_low, *refs):
    pieces, (out_high, out_low, high, low) = refs[:-4], refs[-4:]
    parts = halves(stacked(pieces))
    high[...], low[...] = parts
    fit = halves(dot3(halves(rows[...]), parts, 1))
    total = dot3(fit, parts, 0)
    total += dot3((fit_high[...], fit_low[...]), (near_high[...], near_low[...]), 0)
    out_high[...], out_low[...] = halves(total)


def turn_own(rows, near, pieces):
    (count, width), far = rows.shape, sum(piece.shape[0] for piece in pieces)
    return pl.pallas_call(
        turn_own_kernel,
        out_shape=[like(count, width, jnp.bfloat16)] * 2 + [like(far, width, jnp.bfloat16)] * 2,
        in_specs=in_vmem(5 + len(pieces)),
        out_specs=in_vmem(4),
        compiler_params=limit(20),
        cost_estimate=cost(12 * count * far * width),
        name="turn_own",
    )(rows, *near, *pieces)


def turn_kernel(near_high, near_low, far_high, far_low, *refs):
    cuts, (out_high, out_low) = refs[:-2], refs[-2:]
    rows = halves(stacked(cuts))
    total = 0
    for parts in ((near_high[...], near_low[...]), (far_high[...], far_low[...])):
        total += dot3(halves(dot3(rows, parts, 1)), parts, 0)
    out_high[...], out_low[...] = halves(total)


def turn(cuts, near, far):
    count, width = sum(one.shape[0] for one in cuts), cuts[0].shape[1]
    return pl.pallas_call(
        turn_kernel,
        out_shape=[like(count, width, jnp.bfloat16)] * 2,
        in_specs=in_vmem(4 + len(cuts)),
        out_specs=in_vmem(2),
        compiler_params=limit(20),
        cost_estimate=cost(12 * count * width * (near[0].shape[0] + far[0].shape[0])),
        name="turn",
    )(*near, *far, *cuts)


def spots_of(tiles):
    pairs = []
    for a in range(tiles):
        for b in range(a, tiles):
            halves_of = [(2 * a + r, 2 * b + c) for r in (0, 1) for c in (0, 1)]
            pairs += [pair for pair in halves_of if pair[0] <= pair[1]]
    return {pair: k for k, pair in enumerate(pairs)}


def row_spots(n, tiles):
    spots = spots_of(tiles)
    return {pair: k for pair, k in spots.items() if pair[0] // 2 == n or pair[1] // 2 == n}


def tail_kernel(v, tiles, scale, occ, low_occ, kept, vir, own_high, own_low, far_high, far_low, *refs):
    lows, (blocks, value), scratch = refs[:-8], refs[-8:-6], refs[-6:]
    amp, amp_t, high, low, high_t, low_t = scratch
    n = lax.axis_index("narrow")
    virtuals = v * tiles
    at = [pl.ds(pl.multiple_of(lax.rem(n - a + tiles, tiles) * v, v), v) for a in range(tiles)]
    row = jnp.concatenate([vir[:, one] for one in at], 1)
    col = jnp.broadcast_to(row, (128, virtuals)).T[:, :1]
    gap = occ[:1, :1] + low_occ[:1, :1]
    weight = kept[:1, :1]
    right = halves(stacked(lows))
    left = (own_high[...], own_low[...]), (far_high[...], far_low[...])
    pairs = [dot3(one, right, 1) for one in left]
    spans = slice(0, v), slice(v, virtuals)
    for pair, span in zip(pairs, spans):
        amp[span, :] = pair / (col[span, :] + row - gap)
    amp_t[...] = amp[...].T
    total = jnp.float32(0)
    for pair, span in zip(pairs, spans):
        total += jnp.sum(pair * (2.0 * amp[span, :] - amp_t[span, :]))
    value[...] = -weight * total / (virtuals * virtuals)
    high[...], low[...] = halves(amp[...])
    high_t[...], low_t[...] = halves(amp_t[...])
    spots, half = spots_of(tiles), v // 2
    for a in range(tiles):
        for b in range(a, tiles):
            block = dot3((high[at[a], :], low[at[a], :]), (high_t[:, at[b]], low_t[:, at[b]]), 0)
            block += dot3((high_t[at[a], :], low_t[at[a], :]), (high[:, at[b]], low[:, at[b]]), 0)
            block *= weight * scale
            for r in (0, 1):
                for c in (0, 1):
                    k = spots.get((2 * a + r, 2 * b + c))
                    if k is not None:
                        blocks[k] = block[r * half : (r + 1) * half, c * half : (c + 1) * half]


def tail(turned, raw_low, energies, v, scale):
    virtuals, width = energies[-1].shape[0], raw_low[0].shape[1]
    tiles = virtuals // v
    count = len(spots_of(tiles))
    square = [pltpu.VMEM((virtuals, virtuals), kind) for kind in (jnp.float32, jnp.bfloat16)]
    return pl.pallas_call(
        functools.partial(tail_kernel, v, tiles, scale),
        out_shape=[
            jax.ShapeDtypeStruct((count, v // 2, v // 2), jnp.float32),
            jax.ShapeDtypeStruct((1, 1), jnp.float32),
        ],
        in_specs=in_vmem(8 + len(raw_low)),
        out_specs=in_vmem(2),
        scratch_shapes=[square[0]] * 2 + [square[1]] * 4,
        compiler_params=limit(24),
        cost_estimate=cost(6 * virtuals * virtuals * width + 3 * count * v * v * virtuals),
        name="tail",
    )(*energies[:-1], energies[-1][None, :], *turned, *raw_low)


def tail_plain(turned, raw_low, energies, v, scale):
    occ, low_occ, kept, vir = energies
    virtuals = vir.shape[0]
    narrow = virtuals // v
    order = ((lax.axis_index("narrow") - jnp.arange(narrow)) % narrow * v)[:, None] + jnp.arange(v)[None, :]
    order = order.reshape(virtuals)
    weight = kept[0, 0]
    levels = vir[order]
    own_high, own_low, far_high, far_low = [one.astype(jnp.float32) for one in turned]
    left = jnp.concatenate([own_high + own_low, far_high + far_low], 0)
    pair_ints = contract(left, jnp.concatenate(raw_low, 0), 1, 1)
    amplitude = pair_ints / (levels[:, None] + levels[None, :] - occ[0, 0] - low_occ[0, 0])
    value = jnp.sum(pair_ints * (2.0 * amplitude - amplitude.T)) * -weight / (virtuals * virtuals)
    amplitude = amplitude[order][:, order]
    blocks, half = [], v // 2
    for at in range(0, virtuals, half):
        row = contract(amplitude[at : at + half], amplitude[at:], 1, 1)
        row = row + contract(amplitude[:, at : at + half], amplitude[:, at:], 0, 0)
        blocks += jnp.split(row * (weight * scale), (virtuals - at) // half, 1)
    return jnp.stack(blocks), value.reshape(1, 1)


def halved(blocks, w, bit):
    half = blocks.shape[1] // 2
    side = (w // bit) % 2
    kept = lax.dynamic_slice_in_dim(blocks, side * half, half, 1)
    given = lax.dynamic_slice_in_dim(blocks, (1 - side) * half, half, 1)
    return kept + swapped(given, "wide", bit)


def doubled(blocks, w, bit):
    other = swapped(blocks, "wide", bit)
    low = (w // bit) % 2 == 0
    return jnp.concatenate([jnp.where(low, blocks, other), jnp.where(low, other, blocks)], 1)


def quartered(blocks, w, low):
    rows, spot = blocks.shape[1] // 4, (w // low) % 4
    total = lax.dynamic_slice_in_dim(blocks, spot * rows, rows, 1)
    for flip in (3, 1, 2):
        given = lax.dynamic_slice_in_dim(blocks, (spot ^ flip) * rows, rows, 1)
        total = total + swapped(given, "wide", flip * low)
    return total


def quadrupled(blocks, w, low):
    held = [blocks] + [swapped(blocks, "wide", flip * low) for flip in (1, 2, 3)]
    spot = (w // low) % 4
    return jnp.concatenate(
        [lax.select_n(spot, *[held[at ^ mine] for mine in range(4)]) for at in range(4)], 1
    )


def own_rows(blocks, n, bit):
    wide, narrow = lax.axis_size("wide"), lax.axis_size("narrow")
    spots = [list(row_spots(m, narrow).values()) for m in range(narrow)]

    def of(m):
        picked = [jnp.concatenate([blocks[k : k + 1] for k in row]) for row in spots]
        return lax.select_n(m, *picked)

    total = of(n)
    for s in range(narrow):
        given = of((n + s) % narrow)
        for flip in (0, bit):
            if s or flip:
                steps = [
                    (w * narrow + m, (w ^ flip) * narrow + (m + s) % narrow)
                    for w in range(wide)
                    for m in range(narrow)
                ]
                total = total + lax.ppermute(given, ("wide", "narrow"), steps)
    return total


def row_of(full, m, narrow):
    held = {pair: k for k, pair in enumerate(row_spots(m, narrow))}
    for r in (0, 1):
        for c in range(2 * narrow):
            pair = (2 * m + r, c)
            yield r, c, full[held[pair]] if pair in held else full[held[c, 2 * m + r]].T


def assembled_kernel(narrow, mine, other, out):
    first = lax.rem(lax.axis_index("wide"), 2) == 0
    half = 2 * mine.shape[1]
    whole = jnp.concatenate(
        [jnp.where(first, mine[...], other[...]), jnp.where(first, other[...], mine[...])], 1
    )
    for m in range(narrow):

        @pl.when(lax.axis_index("narrow") == m)
        def _():
            for r, c, block in row_of(whole, m, narrow):
                out[r * half : (r + 1) * half, c * half : (c + 1) * half] = block


def assembled(mine, w, n, narrow):
    other = swapped(mine, "wide", 1)
    half = 2 * mine.shape[1]
    if half % 128 == 0:
        return pl.pallas_call(
            functools.partial(assembled_kernel, narrow),
            out_shape=like(2 * half, 2 * half * narrow, jnp.float32),
            in_specs=in_vmem(2),
            out_specs=in_vmem(1)[0],
            compiler_params=limit(8),
            name="assembled",
        )(mine, other)
    first = w % 2 == 0
    whole = jnp.concatenate([jnp.where(first, mine, other), jnp.where(first, other, mine)], 1)
    rows = []
    for m in range(narrow):
        blocks = [block for *_, block in row_of(whole, m, narrow)]
        spans = blocks[: 2 * narrow], blocks[2 * narrow :]
        rows.append(jnp.concatenate([jnp.concatenate(span, 1) for span in spans], 0))
    return lax.select_n(n, *rows)


def on_device(raw_ints, metric, occ_energy, vir_energy, pair_kept):
    wide, narrow = lax.axis_size("wide"), lax.axis_size("narrow")
    w, n = lax.axis_index("wide"), lax.axis_index("narrow")
    v = raw_ints.shape[1]
    virtuals = v * narrow

    near = 4
    chunks = [(0, v // 2), (v // 2, v // 2)]
    rows = metric.shape[0] // near
    piece = lax.dynamic_slice_in_dim(metric, (w % near) * rows, rows, 0)
    far = [passed_along(piece, "narrow", s) for s in range(1, narrow)]
    own = lax.dynamic_index_in_dim(raw_ints, n, 0, keepdims=False)
    raw_low = [passed_along(own, "wide", 1)]
    arrived, given = [], []
    for s in range(1, narrow):
        block = lax.dynamic_index_in_dim(raw_ints, (n + s) % narrow, 0, keepdims=False)
        parts = [block[first : first + rows] for first, rows in chunks]
        arrived += [passed_along(one, "narrow", s) for one in reversed(parts)][::-1]
        given += parts
    *fit_near, occ, kept = near_fit(after(own, *given), metric, occ_energy, pair_kept)
    low_occ = passed_along(occ, "wide", 1)
    far = [after(one, fit_near[0]) for one in far]
    far_x = [swapped(one, "wide", 2) for one in far]
    far_core = [swapped(one, "wide", 1) for one in far]
    raw_low += [passed_along(one, "wide", 1) for one in arrived[:-1]]
    far_x = [after(one, raw_low[0], low_occ, arrived[0]) for one in far_x]
    far_last = [swapped(one, "wide", 1) for one in far_x]

    *own_turned, far_high, far_low = turn_own(own, fit_near, far + far_core + far_x + far_last)
    raw_low.append(passed_along(after(arrived[-1], own_turned[0]), "wide", 1))
    turned = [*own_turned, *turn(arrived, fit_near[2:], (far_high, far_low))]

    form = tail if v % 128 == 0 else tail_plain
    energies = occ, low_occ, kept, vir_energy
    blocks, own_value = form(turned, raw_low, energies, v, 0.0625 / (wide * narrow))
    blocks, own_value, w, n = lax.optimization_barrier((blocks, own_value, w, n))
    own_value = own_value.reshape(1)
    upper_value = passed_along(own_value, "wide", -1)

    first, *bits, last = [1 << k for k in range(wide.bit_length() - 1)]
    low, bits = bits[0], bits[2:]
    blocks = halved(blocks, w, first)
    blocks = quartered(blocks, w, low)
    for bit in bits:
        blocks = halved(blocks, w, bit)
    full = own_rows(blocks, n, last)
    full, upper_value = lax.optimization_barrier((full, upper_value))
    for bit in reversed(bits):
        full = doubled(full, w, bit)
    full = quadrupled(full, w, low)
    return assembled(full, w, n, narrow), own_value + upper_value


def solution(mesh):
    placed = (
        P("wide", "narrow", None),
        P("narrow", None),
        P(("wide", "narrow")),
        P(),
        P(("wide", "narrow")),
    )
    return jax.shard_map(
        on_device,
        mesh=mesh,
        in_specs=placed,
        out_specs=(P("narrow", None), P(("wide", "narrow"))),
        check_vma=False,
    )
```

```python
import functools

import jax
import jax.numpy as jnp
from jax import lax
from jax.experimental import pallas as pl
from jax.experimental.pallas import tpu as pltpu
from jax.sharding import PartitionSpec as P

PASSES = lax.Precision.HIGH
VMEM = pltpu.MemorySpace.VMEM
NEAR_COST = 15_000_000_000
EXTRA = 8


def contract(left, right, left_dim, right_dim):
    return lax.dot_general(
        left,
        right,
        (((left_dim,), (right_dim,)), ((), ())),
        precision=PASSES,
        preferred_element_type=jnp.float32,
    )


def passed_along(shard, axis, by):
    size = lax.axis_size(axis)
    return lax.ppermute(shard, axis, [(i, (i + by) % size) for i in range(size)])


def swapped(shard, axis, bit):
    size = lax.axis_size(axis)
    return lax.ppermute(shard, axis, [(i, i ^ bit) for i in range(size)])


def after(value, *gates):
    return lax.optimization_barrier((value,) + gates)[0]


def in_vmem(count):
    return [pl.BlockSpec(memory_space=VMEM)] * count


def limit(mib):
    return pltpu.CompilerParams(vmem_limit_bytes=mib * 2**20)


def cost(flops):
    return pl.CostEstimate(flops=flops, bytes_accessed=0, transcendentals=0)


def halves(value):
    high = value.astype(jnp.bfloat16)
    low = (value - high.astype(jnp.float32)).astype(jnp.bfloat16)
    return high, low


def dot3(left, right, right_dim):
    (lh, ll), (rh, rl) = left, right
    dims = (((1,), (right_dim,)), ((), ()))
    total = lax.dot_general(ll, rh, dims, preferred_element_type=jnp.float32)
    total += lax.dot_general(lh, rl, dims, preferred_element_type=jnp.float32)
    return total + lax.dot_general(lh, rh, dims, preferred_element_type=jnp.float32)


def stacked(refs):
    return jnp.concatenate([one[...] for one in refs], 0)


def like(rows, width, dtype):
    return jax.ShapeDtypeStruct((rows, width), dtype)


def near_fit_kernel(rows, metric, kept, fit_high, fit_low, high, low, kept_tile):
    parts = halves(metric[...])
    high[...], low[...] = parts
    fit_high[...], fit_low[...] = halves(dot3(halves(rows[: fit_high.shape[0]]), parts, 1))
    kept_tile[...] = jnp.broadcast_to(kept[...].astype(jnp.float32), kept_tile.shape)


def near_fit(rows, metric, kept):
    (count, width), near = rows.shape, metric.shape[0]
    count -= EXTRA
    return pl.pallas_call(
        near_fit_kernel,
        out_shape=[like(count, near, jnp.bfloat16)] * 2
        + [like(near, width, jnp.bfloat16)] * 2
        + [like(8, 128, jnp.float32)],
        in_specs=in_vmem(3),
        out_specs=in_vmem(5),
        compiler_params=limit(16),
        cost_estimate=cost(NEAR_COST),
        name="near_fit",
    )(rows, metric, kept[None, :])


def turn_own_kernel(rows, fit_high, fit_low, near_high, near_low, *refs):
    pieces, (out_high, out_low, high, low) = refs[:-4], refs[-4:]
    parts = halves(stacked(pieces))
    high[...], low[...] = parts
    fit = halves(dot3(halves(rows[: out_high.shape[0]]), parts, 1))
    total = dot3(fit, parts, 0)
    total += dot3((fit_high[...], fit_low[...]), (near_high[...], near_low[...]), 0)
    out_high[...], out_low[...] = halves(total)


def turn_own(rows, near, pieces):
    (count, width), far = rows.shape, sum(piece.shape[0] for piece in pieces)
    count -= EXTRA
    return pl.pallas_call(
        turn_own_kernel,
        out_shape=[like(count, width, jnp.bfloat16)] * 2 + [like(far, width, jnp.bfloat16)] * 2,
        in_specs=in_vmem(5 + len(pieces)),
        out_specs=in_vmem(4),
        compiler_params=limit(20),
        cost_estimate=cost(12 * count * far * width),
        name="turn_own",
    )(rows, *near, *pieces)


def turn_kernel(near_high, near_low, far_high, far_low, *refs):
    cuts, (out_high, out_low) = refs[:-2], refs[-2:]
    rows = halves(stacked(cuts))
    total = 0
    for parts in ((near_high[...], near_low[...]), (far_high[...], far_low[...])):
        total += dot3(halves(dot3(rows, parts, 1)), parts, 0)
    out_high[...], out_low[...] = halves(total)


def turn(cuts, near, far):
    count, width = sum(one.shape[0] for one in cuts), cuts[0].shape[1]
    return pl.pallas_call(
        turn_kernel,
        out_shape=[like(count, width, jnp.bfloat16)] * 2,
        in_specs=in_vmem(4 + len(cuts)),
        out_specs=in_vmem(2),
        compiler_params=limit(20),
        cost_estimate=cost(12 * count * width * (near[0].shape[0] + far[0].shape[0])),
        name="turn",
    )(*near, *far, *cuts)


def spots_of(tiles):
    pairs = []
    for a in range(tiles):
        for b in range(a, tiles):
            halves_of = [(2 * a + r, 2 * b + c) for r in (0, 1) for c in (0, 1)]
            pairs += [pair for pair in halves_of if pair[0] <= pair[1]]
    return {pair: k for k, pair in enumerate(pairs)}


def row_spots(n, tiles):
    spots = spots_of(tiles)
    return {pair: k for pair, k in spots.items() if pair[0] // 2 == n or pair[1] // 2 == n}


def tail_kernel(v, tiles, scale, own, kept, vir, own_high, own_low, far_high, far_low, *refs):
    lows, (blocks, value), scratch = refs[:-8], refs[-8:-6], refs[-6:]
    amp, amp_t, high, low, high_t, low_t = scratch
    n = lax.axis_index("narrow")
    virtuals = v * tiles
    at = [pl.ds(pl.multiple_of(lax.rem(n - a + tiles, tiles) * v, v), v) for a in range(tiles)]
    row = jnp.concatenate([vir[:, one] for one in at], 1)
    col = jnp.broadcast_to(row, (128, virtuals)).T[:, :1]
    gap = own[v : v + 1, :1] + lows[0][v : v + 1, :1]
    weight = kept[:1, :1]
    right = halves(jnp.concatenate([lows[0][:v]] + [one[...] for one in lows[1:]], 0))
    left = (own_high[...], own_low[...]), (far_high[...], far_low[...])
    pairs = [dot3(one, right, 1) for one in left]
    spans = slice(0, v), slice(v, virtuals)
    for pair, span in zip(pairs, spans):
        amp[span, :] = pair / (col[span, :] + row - gap)
    amp_t[...] = amp[...].T
    total = jnp.float32(0)
    for pair, span in zip(pairs, spans):
        total += jnp.sum(pair * (2.0 * amp[span, :] - amp_t[span, :]))
    value[...] = -weight * total / (virtuals * virtuals)
    high[...], low[...] = halves(amp[...])
    high_t[...], low_t[...] = halves(amp_t[...])
    spots, half = spots_of(tiles), v // 2
    for a in range(tiles):
        for b in range(a, tiles):
            block = dot3((high[at[a], :], low[at[a], :]), (high_t[:, at[b]], low_t[:, at[b]]), 0)
            block += dot3((high_t[at[a], :], low_t[at[a], :]), (high[:, at[b]], low[:, at[b]]), 0)
            block *= weight * scale
            for r in (0, 1):
                for c in (0, 1):
                    k = spots.get((2 * a + r, 2 * b + c))
                    if k is not None:
                        blocks[k] = block[r * half : (r + 1) * half, c * half : (c + 1) * half]


def tail(turned, raw_low, energies, v, scale):
    virtuals, width = energies[-1].shape[0], raw_low[0].shape[1]
    tiles = virtuals // v
    count = len(spots_of(tiles))
    square = [pltpu.VMEM((virtuals, virtuals), kind) for kind in (jnp.float32, jnp.bfloat16)]
    return pl.pallas_call(
        functools.partial(tail_kernel, v, tiles, scale),
        out_shape=[
            jax.ShapeDtypeStruct((count, v // 2, v // 2), jnp.float32),
            jax.ShapeDtypeStruct((1, 1), jnp.float32),
        ],
        in_specs=in_vmem(7 + len(raw_low)),
        out_specs=in_vmem(2),
        scratch_shapes=[square[0]] * 2 + [square[1]] * 4,
        compiler_params=limit(24),
        cost_estimate=cost(6 * virtuals * virtuals * width + 3 * count * v * v * virtuals),
        name="tail",
    )(*energies[:-1], energies[-1][None, :], *turned, *raw_low)


def tail_plain(turned, raw_low, energies, v, scale):
    own, kept, vir = energies
    virtuals = vir.shape[0]
    narrow = virtuals // v
    order = ((lax.axis_index("narrow") - jnp.arange(narrow)) % narrow * v)[:, None] + jnp.arange(v)[None, :]
    order = order.reshape(virtuals)
    weight = kept[0, 0]
    levels = vir[order]
    own_high, own_low, far_high, far_low = [one.astype(jnp.float32) for one in turned]
    left = jnp.concatenate([own_high + own_low, far_high + far_low], 0)
    pair_ints = contract(left, jnp.concatenate([raw_low[0][:v]] + raw_low[1:], 0), 1, 1)
    amplitude = pair_ints / (levels[:, None] + levels[None, :] - own[v, 0] - raw_low[0][v, 0])
    value = jnp.sum(pair_ints * (2.0 * amplitude - amplitude.T)) * -weight / (virtuals * virtuals)
    amplitude = amplitude[order][:, order]
    blocks, half = [], v // 2
    for at in range(0, virtuals, half):
        row = contract(amplitude[at : at + half], amplitude[at:], 1, 1)
        row = row + contract(amplitude[:, at : at + half], amplitude[:, at:], 0, 0)
        blocks += jnp.split(row * (weight * scale), (virtuals - at) // half, 1)
    return jnp.stack(blocks), value.reshape(1, 1)


def halved(blocks, w, bit):
    half = blocks.shape[1] // 2
    side = (w // bit) % 2
    kept = lax.dynamic_slice_in_dim(blocks, side * half, half, 1)
    given = lax.dynamic_slice_in_dim(blocks, (1 - side) * half, half, 1)
    return kept + swapped(given, "wide", bit)


def doubled(blocks, w, bit):
    other = swapped(blocks, "wide", bit)
    low = (w // bit) % 2 == 0
    return jnp.concatenate([jnp.where(low, blocks, other), jnp.where(low, other, blocks)], 1)


def quartered(blocks, w, low):
    rows, spot = blocks.shape[1] // 4, (w // low) % 4
    total = lax.dynamic_slice_in_dim(blocks, spot * rows, rows, 1)
    for flip in (3, 1, 2):
        given = lax.dynamic_slice_in_dim(blocks, (spot ^ flip) * rows, rows, 1)
        total = total + swapped(given, "wide", flip * low)
    return total


def quadrupled(blocks, w, low):
    held = [blocks] + [swapped(blocks, "wide", flip * low) for flip in (1, 2, 3)]
    spot = (w // low) % 4
    return jnp.concatenate(
        [lax.select_n(spot, *[held[at ^ mine] for mine in range(4)]) for at in range(4)], 1
    )


def own_rows(blocks, n, bit):
    wide, narrow = lax.axis_size("wide"), lax.axis_size("narrow")
    spots = [list(row_spots(m, narrow).values()) for m in range(narrow)]

    def of(m):
        picked = [jnp.concatenate([blocks[k : k + 1] for k in row]) for row in spots]
        return lax.select_n(m, *picked)

    total = of(n)
    for s in range(narrow):
        given = of((n + s) % narrow)
        for flip in (0, bit):
            if s or flip:
                steps = [
                    (w * narrow + m, (w ^ flip) * narrow + (m + s) % narrow)
                    for w in range(wide)
                    for m in range(narrow)
                ]
                total = total + lax.ppermute(given, ("wide", "narrow"), steps)
    return total


def row_of(full, m, narrow):
    held = {pair: k for k, pair in enumerate(row_spots(m, narrow))}
    for r in (0, 1):
        for c in range(2 * narrow):
            pair = (2 * m + r, c)
            yield r, c, full[held[pair]] if pair in held else full[held[c, 2 * m + r]].T


def assembled_kernel(narrow, mine, other, out):
    first = lax.rem(lax.axis_index("wide"), 2) == 0
    half = 2 * mine.shape[1]
    whole = jnp.concatenate(
        [jnp.where(first, mine[...], other[...]), jnp.where(first, other[...], mine[...])], 1
    )
    for m in range(narrow):

        @pl.when(lax.axis_index("narrow") == m)
        def _():
            for r, c, block in row_of(whole, m, narrow):
                out[r * half : (r + 1) * half, c * half : (c + 1) * half] = block


def assembled(mine, w, n, narrow):
    other = swapped(mine, "wide", 1)
    half = 2 * mine.shape[1]
    if half % 128 == 0:
        return pl.pallas_call(
            functools.partial(assembled_kernel, narrow),
            out_shape=like(2 * half, 2 * half * narrow, jnp.float32),
            in_specs=in_vmem(2),
            out_specs=in_vmem(1)[0],
            compiler_params=limit(8),
            name="assembled",
        )(mine, other)
    first = w % 2 == 0
    whole = jnp.concatenate([jnp.where(first, mine, other), jnp.where(first, other, mine)], 1)
    rows = []
    for m in range(narrow):
        blocks = [block for *_, block in row_of(whole, m, narrow)]
        spans = blocks[: 2 * narrow], blocks[2 * narrow :]
        rows.append(jnp.concatenate([jnp.concatenate(span, 1) for span in spans], 0))
    return lax.select_n(n, *rows)


def on_device(raw_ints, metric, occ_energy, vir_energy, pair_kept):
    wide, narrow = lax.axis_size("wide"), lax.axis_size("narrow")
    w, n = lax.axis_index("wide"), lax.axis_index("narrow")
    v = raw_ints.shape[1]
    virtuals = v * narrow

    near = 4
    chunks = [(0, v // 2), (v // 2, v // 2)]
    rows = metric.shape[0] // near
    piece = lax.dynamic_slice_in_dim(metric, (w % near) * rows, rows, 0)
    far = [passed_along(piece, "narrow", s) for s in range(1, narrow)]
    own = lax.dynamic_index_in_dim(raw_ints, n, 0, keepdims=False)
    own = jnp.concatenate([own, jnp.broadcast_to(occ_energy, (EXTRA, own.shape[1]))], 0)
    raw_low = [passed_along(own, "wide", 1)]
    arrived, given = [], []
    for s in range(1, narrow):
        block = lax.dynamic_index_in_dim(after(raw_ints, own), (n + s) % narrow, 0, keepdims=False)
        parts = [block[first : first + rows] for first, rows in chunks]
        arrived += [passed_along(one, "narrow", s) for one in reversed(parts)][::-1]
        given += parts
    *fit_near, kept = near_fit(after(own, *given), metric, pair_kept)
    far = [after(one, fit_near[0]) for one in far]
    far_x = [swapped(one, "wide", 2) for one in far]
    far_core = [swapped(one, "wide", 1) for one in far]
    raw_low += [passed_along(one, "wide", 1) for one in arrived[:-1]]
    far_x = [after(one, raw_low[0], arrived[0]) for one in far_x]
    far_last = [swapped(one, "wide", 1) for one in far_x]

    *own_turned, far_high, far_low = turn_own(own, fit_near, far + far_core + far_x + far_last)
    raw_low.append(passed_along(after(arrived[-1], raw_low[1]), "wide", 1))
    turned = [*own_turned, *turn(arrived, fit_near[2:], (far_high, far_low))]

    form = tail if v % 128 == 0 else tail_plain
    energies = own, kept, vir_energy
    blocks, own_value = form(turned, raw_low, energies, v, 0.0625 / (wide * narrow))
    blocks, own_value, w, n = lax.optimization_barrier((blocks, own_value, w, n))
    own_value = own_value.reshape(1)
    upper_value = passed_along(own_value, "wide", -1)

    first, *bits, last = [1 << k for k in range(wide.bit_length() - 1)]
    low, bits = bits[0], bits[2:]
    blocks = halved(blocks, w, first)
    blocks = quartered(blocks, w, low)
    for bit in bits:
        blocks = halved(blocks, w, bit)
    full = own_rows(blocks, n, last)
    full, upper_value = lax.optimization_barrier((full, upper_value))
    for bit in reversed(bits):
        full = doubled(full, w, bit)
    full = quadrupled(full, w, low)
    return assembled(full, w, n, narrow), own_value + upper_value


def solution(mesh):
    placed = (
        P("wide", "narrow", None),
        P("narrow", None),
        P(("wide", "narrow")),
        P(),
        P(("wide", "narrow")),
    )
    return jax.shard_map(
        on_device,
        mesh=mesh,
        in_specs=placed,
        out_specs=(P("narrow", None), P(("wide", "narrow"))),
        check_vma=False,
    )
```

```python
import functools

import jax
import jax.numpy as jnp
from jax import lax
from jax.experimental import pallas as pl
from jax.experimental.pallas import tpu as pltpu
from jax.sharding import PartitionSpec as P

PASSES = lax.Precision.HIGH
VMEM = pltpu.MemorySpace.VMEM
NEAR_COST = 15_000_000_000


def contract(left, right, left_dim, right_dim):
    return lax.dot_general(
        left,
        right,
        (((left_dim,), (right_dim,)), ((), ())),
        precision=PASSES,
        preferred_element_type=jnp.float32,
    )


def passed_along(shard, axis, by):
    size = lax.axis_size(axis)
    return lax.ppermute(shard, axis, [(i, (i + by) % size) for i in range(size)])


def swapped(shard, axis, bit):
    size = lax.axis_size(axis)
    return lax.ppermute(shard, axis, [(i, i ^ bit) for i in range(size)])


def after(value, *gates):
    return lax.optimization_barrier((value,) + gates)[0]


def in_vmem(count):
    return [pl.BlockSpec(memory_space=VMEM)] * count


def limit(mib):
    return pltpu.CompilerParams(vmem_limit_bytes=mib * 2**20)


def cost(flops):
    return pl.CostEstimate(flops=flops, bytes_accessed=0, transcendentals=0)


def halves(value):
    high = value.astype(jnp.bfloat16)
    low = (value - high.astype(jnp.float32)).astype(jnp.bfloat16)
    return high, low


def dot3(left, right, right_dim):
    (lh, ll), (rh, rl) = left, right
    dims = (((1,), (right_dim,)), ((), ()))
    total = lax.dot_general(ll, rh, dims, preferred_element_type=jnp.float32)
    total += lax.dot_general(lh, rl, dims, preferred_element_type=jnp.float32)
    return total + lax.dot_general(lh, rh, dims, preferred_element_type=jnp.float32)


def stacked(refs):
    return jnp.concatenate([one[...] for one in refs], 0)


def like(rows, width, dtype):
    return jax.ShapeDtypeStruct((rows, width), dtype)


def near_fit_kernel(rows, metric, occ, kept, fit_high, fit_low, high, low, occ_tile, kept_tile):
    parts = halves(metric[...])
    high[...], low[...] = parts
    fit_high[...], fit_low[...] = halves(dot3(halves(rows[...]), parts, 1))
    occ_tile[...] = jnp.broadcast_to(occ[...], occ_tile.shape)
    kept_tile[...] = jnp.broadcast_to(kept[...].astype(jnp.float32), kept_tile.shape)


def near_fit(rows, metric, occ, kept):
    (count, width), near = rows.shape, metric.shape[0]
    return pl.pallas_call(
        near_fit_kernel,
        out_shape=[like(count, near, jnp.bfloat16)] * 2
        + [like(near, width, jnp.bfloat16)] * 2
        + [like(8, 128, jnp.float32)] * 2,
        in_specs=in_vmem(4),
        out_specs=in_vmem(6),
        compiler_params=limit(16),
        cost_estimate=cost(NEAR_COST),
        name="near_fit",
    )(rows, metric, occ[None, :], kept[None, :])


def turn_own_kernel(rows, fit_high, fit_low, near_high, near_low, *refs):
    pieces, (out_high, out_low, high, low) = refs[:-4], refs[-4:]
    parts = halves(stacked(pieces))
    high[...], low[...] = parts
    fit = halves(dot3(halves(rows[...]), parts, 1))
    total = dot3(fit, parts, 0)
    total += dot3((fit_high[...], fit_low[...]), (near_high[...], near_low[...]), 0)
    out_high[...], out_low[...] = halves(total)


def turn_own(rows, near, pieces):
    (count, width), far = rows.shape, sum(piece.shape[0] for piece in pieces)
    return pl.pallas_call(
        turn_own_kernel,
        out_shape=[like(count, width, jnp.bfloat16)] * 2 + [like(far, width, jnp.bfloat16)] * 2,
        in_specs=in_vmem(5 + len(pieces)),
        out_specs=in_vmem(4),
        compiler_params=limit(20),
        cost_estimate=cost(12 * count * far * width),
        name="turn_own",
    )(rows, *near, *pieces)


def turn_kernel(near_high, near_low, far_high, far_low, *refs):
    cuts, (out_high, out_low) = refs[:-2], refs[-2:]
    rows = halves(stacked(cuts))
    total = 0
    for parts in ((near_high[...], near_low[...]), (far_high[...], far_low[...])):
        total += dot3(halves(dot3(rows, parts, 1)), parts, 0)
    out_high[...], out_low[...] = halves(total)


def turn(cuts, near, far):
    count, width = sum(one.shape[0] for one in cuts), cuts[0].shape[1]
    return pl.pallas_call(
        turn_kernel,
        out_shape=[like(count, width, jnp.bfloat16)] * 2,
        in_specs=in_vmem(4 + len(cuts)),
        out_specs=in_vmem(2),
        compiler_params=limit(20),
        cost_estimate=cost(12 * count * width * (near[0].shape[0] + far[0].shape[0])),
        name="turn",
    )(*near, *far, *cuts)


def spots_of(tiles):
    pairs = []
    for a in range(tiles):
        for b in range(a, tiles):
            halves_of = [(2 * a + r, 2 * b + c) for r in (0, 1) for c in (0, 1)]
            pairs += [pair for pair in halves_of if pair[0] <= pair[1]]
    return {pair: k for k, pair in enumerate(pairs)}


def row_spots(n, tiles):
    spots = spots_of(tiles)
    return {pair: k for pair, k in spots.items() if pair[0] // 2 == n or pair[1] // 2 == n}


def tail_kernel(v, tiles, scale, occ, low_occ, kept, vir, own_high, own_low, far_high, far_low, *refs):
    lows, (blocks, value), scratch = refs[:-8], refs[-8:-6], refs[-6:]
    amp, amp_t, high, low, high_t, low_t = scratch
    n = lax.axis_index("narrow")
    virtuals = v * tiles
    at = [pl.ds(pl.multiple_of(lax.rem(n - a + tiles, tiles) * v, v), v) for a in range(tiles)]
    row = jnp.concatenate([vir[:, one] for one in at], 1)
    col = jnp.broadcast_to(row, (128, virtuals)).T[:, :1]
    gap = occ[:1, :1] + low_occ[:1, :1]
    weight = kept[:1, :1]
    right = halves(stacked(lows))
    left = (own_high[...], own_low[...]), (far_high[...], far_low[...])
    pairs = [dot3(one, right, 1) for one in left]
    spans = slice(0, v), slice(v, virtuals)
    for pair, span in zip(pairs, spans):
        amp[span, :] = pair / (col[span, :] + row - gap)
    amp_t[...] = amp[...].T
    total = jnp.float32(0)
    for pair, span in zip(pairs, spans):
        total += jnp.sum(pair * (2.0 * amp[span, :] - amp_t[span, :]))
    value[...] = -weight * total / (virtuals * virtuals)
    high[...], low[...] = halves(amp[...])
    high_t[...], low_t[...] = halves(amp_t[...])
    spots, half = spots_of(tiles), v // 2
    for a in range(tiles):
        for b in range(a, tiles):
            block = dot3((high[at[a], :], low[at[a], :]), (high_t[:, at[b]], low_t[:, at[b]]), 0)
            block += dot3((high_t[at[a], :], low_t[at[a], :]), (high[:, at[b]], low[:, at[b]]), 0)
            block *= weight * scale
            for r in (0, 1):
                for c in (0, 1):
                    k = spots.get((2 * a + r, 2 * b + c))
                    if k is not None:
                        blocks[k] = block[r * half : (r + 1) * half, c * half : (c + 1) * half]


def tail(turned, raw_low, energies, v, scale):
    virtuals, width = energies[-1].shape[0], raw_low[0].shape[1]
    tiles = virtuals // v
    count = len(spots_of(tiles))
    square = [pltpu.VMEM((virtuals, virtuals), kind) for kind in (jnp.float32, jnp.bfloat16)]
    return pl.pallas_call(
        functools.partial(tail_kernel, v, tiles, scale),
        out_shape=[
            jax.ShapeDtypeStruct((count, v // 2, v // 2), jnp.float32),
            jax.ShapeDtypeStruct((1, 1), jnp.float32),
        ],
        in_specs=in_vmem(8 + len(raw_low)),
        out_specs=in_vmem(2),
        scratch_shapes=[square[0]] * 2 + [square[1]] * 4,
        compiler_params=limit(24),
        cost_estimate=cost(6 * virtuals * virtuals * width + 3 * count * v * v * virtuals),
        name="tail",
    )(*energies[:-1], energies[-1][None, :], *turned, *raw_low)


def tail_plain(turned, raw_low, energies, v, scale):
    occ, low_occ, kept, vir = energies
    virtuals = vir.shape[0]
    narrow = virtuals // v
    order = ((lax.axis_index("narrow") - jnp.arange(narrow)) % narrow * v)[:, None] + jnp.arange(v)[None, :]
    order = order.reshape(virtuals)
    weight = kept[0, 0]
    levels = vir[order]
    own_high, own_low, far_high, far_low = [one.astype(jnp.float32) for one in turned]
    left = jnp.concatenate([own_high + own_low, far_high + far_low], 0)
    pair_ints = contract(left, jnp.concatenate(raw_low, 0), 1, 1)
    amplitude = pair_ints / (levels[:, None] + levels[None, :] - occ[0, 0] - low_occ[0, 0])
    value = jnp.sum(pair_ints * (2.0 * amplitude - amplitude.T)) * -weight / (virtuals * virtuals)
    amplitude = amplitude[order][:, order]
    blocks, half = [], v // 2
    for at in range(0, virtuals, half):
        row = contract(amplitude[at : at + half], amplitude[at:], 1, 1)
        row = row + contract(amplitude[:, at : at + half], amplitude[:, at:], 0, 0)
        blocks += jnp.split(row * (weight * scale), (virtuals - at) // half, 1)
    return jnp.stack(blocks), value.reshape(1, 1)


def halved(blocks, w, bit):
    half = blocks.shape[1] // 2
    side = (w // bit) % 2
    kept = lax.dynamic_slice_in_dim(blocks, side * half, half, 1)
    given = lax.dynamic_slice_in_dim(blocks, (1 - side) * half, half, 1)
    return kept + swapped(given, "wide", bit)


def doubled(blocks, w, bit):
    other = swapped(blocks, "wide", bit)
    low = (w // bit) % 2 == 0
    return jnp.concatenate([jnp.where(low, blocks, other), jnp.where(low, other, blocks)], 1)


def quartered(blocks, w, low):
    rows, spot = blocks.shape[1] // 4, (w // low) % 4
    total = lax.dynamic_slice_in_dim(blocks, spot * rows, rows, 1)
    for flip in (3, 1, 2):
        given = lax.dynamic_slice_in_dim(blocks, (spot ^ flip) * rows, rows, 1)
        total = total + swapped(given, "wide", flip * low)
    return total


def quadrupled(blocks, w, low):
    held = [blocks] + [swapped(blocks, "wide", flip * low) for flip in (1, 2, 3)]
    spot = (w // low) % 4
    return jnp.concatenate(
        [lax.select_n(spot, *[held[at ^ mine] for mine in range(4)]) for at in range(4)], 1
    )


def own_rows(blocks, n, bit):
    wide, narrow = lax.axis_size("wide"), lax.axis_size("narrow")
    spots = [list(row_spots(m, narrow).values()) for m in range(narrow)]

    def of(m):
        picked = [jnp.concatenate([blocks[k : k + 1] for k in row]) for row in spots]
        return lax.select_n(m, *picked)

    total = of(n)
    for s in range(narrow):
        given = of((n + s) % narrow)
        for flip in (0, bit):
            if s or flip:
                steps = [
                    (w * narrow + m, (w ^ flip) * narrow + (m + s) % narrow)
                    for w in range(wide)
                    for m in range(narrow)
                ]
                total = total + lax.ppermute(given, ("wide", "narrow"), steps)
    return total


def row_of(full, m, narrow):
    held = {pair: k for k, pair in enumerate(row_spots(m, narrow))}
    for r in (0, 1):
        for c in range(2 * narrow):
            pair = (2 * m + r, c)
            yield r, c, full[held[pair]] if pair in held else full[held[c, 2 * m + r]].T


def assembled_kernel(narrow, mine, other, out):
    first = lax.rem(lax.axis_index("wide"), 2) == 0
    half = 2 * mine.shape[1]
    whole = jnp.concatenate(
        [jnp.where(first, mine[...], other[...]), jnp.where(first, other[...], mine[...])], 1
    )
    for m in range(narrow):

        @pl.when(lax.axis_index("narrow") == m)
        def _():
            for r, c, block in row_of(whole, m, narrow):
                out[r * half : (r + 1) * half, c * half : (c + 1) * half] = block


def assembled(mine, w, n, narrow):
    other = swapped(mine, "wide", 1)
    half = 2 * mine.shape[1]
    if half % 128 == 0:
        return pl.pallas_call(
            functools.partial(assembled_kernel, narrow),
            out_shape=like(2 * half, 2 * half * narrow, jnp.float32),
            in_specs=in_vmem(2),
            out_specs=in_vmem(1)[0],
            compiler_params=limit(8),
            name="assembled",
        )(mine, other)
    first = w % 2 == 0
    whole = jnp.concatenate([jnp.where(first, mine, other), jnp.where(first, other, mine)], 1)
    rows = []
    for m in range(narrow):
        blocks = [block for *_, block in row_of(whole, m, narrow)]
        spans = blocks[: 2 * narrow], blocks[2 * narrow :]
        rows.append(jnp.concatenate([jnp.concatenate(span, 1) for span in spans], 0))
    return lax.select_n(n, *rows)


def on_device(raw_ints, metric, occ_energy, vir_energy, pair_kept):
    wide, narrow = lax.axis_size("wide"), lax.axis_size("narrow")
    w, n = lax.axis_index("wide"), lax.axis_index("narrow")
    v = raw_ints.shape[1]
    virtuals = v * narrow

    near = 4
    chunks = [(0, v // 2), (v // 2, v // 4), (3 * v // 4, v // 4)]
    rows = metric.shape[0] // near
    piece = lax.dynamic_slice_in_dim(metric, (w % near) * rows, rows, 0)
    far = [passed_along(piece, "narrow", s) for s in range(1, narrow)]
    own = lax.dynamic_index_in_dim(raw_ints, n, 0, keepdims=False)
    raw_low = [passed_along(own, "wide", 1)]
    arrived, given = [], []
    for s in range(1, narrow):
        block = lax.dynamic_index_in_dim(raw_ints, (n + s) % narrow, 0, keepdims=False)
        parts = [block[first : first + rows] for first, rows in chunks]
        arrived += [passed_along(one, "narrow", s) for one in reversed(parts)][::-1]
        given += parts
    *fit_near, occ, kept = near_fit(after(own, *given), metric, occ_energy, pair_kept)
    low_occ = passed_along(occ, "wide", 1)
    far = [after(one, fit_near[0]) for one in far]
    far_x = [swapped(one, "wide", 2) for one in far]
    far_core = [swapped(one, "wide", 1) for one in far]
    raw_low += [passed_along(one, "wide", 1) for one in arrived[:-1]]
    far_x = [after(one, raw_low[0], low_occ, arrived[0], arrived[1]) for one in far_x]
    far_last = [swapped(one, "wide", 1) for one in far_x]

    *own_turned, far_high, far_low = turn_own(own, fit_near, far + far_core + far_x + far_last)
    raw_low.append(passed_along(after(arrived[-1], own_turned[0]), "wide", 1))
    turned = [*own_turned, *turn(arrived, fit_near[2:], (far_high, far_low))]

    form = tail if v % 128 == 0 else tail_plain
    energies = occ, low_occ, kept, vir_energy
    blocks, own_value = form(turned, raw_low, energies, v, 0.0625 / (wide * narrow))
    blocks, own_value, w, n = lax.optimization_barrier((blocks, own_value, w, n))
    own_value = own_value.reshape(1)
    upper_value = passed_along(own_value, "wide", -1)

    first, *bits, last = [1 << k for k in range(wide.bit_length() - 1)]
    low, bits = bits[0], bits[2:]
    blocks = halved(blocks, w, first)
    blocks = quartered(blocks, w, low)
    for bit in bits:
        blocks = halved(blocks, w, bit)
    full = own_rows(blocks, n, last)
    full, upper_value = lax.optimization_barrier((full, upper_value))
    for bit in reversed(bits):
        full = doubled(full, w, bit)
    full = quadrupled(full, w, low)
    return assembled(full, w, n, narrow), own_value + upper_value


def solution(mesh):
    placed = (
        P("wide", "narrow", None),
        P("narrow", None),
        P(("wide", "narrow")),
        P(),
        P(("wide", "narrow")),
    )
    return jax.shard_map(
        on_device,
        mesh=mesh,
        in_specs=placed,
        out_specs=(P("narrow", None), P(("wide", "narrow"))),
        check_vma=False,
    )
```

```python
import functools

import jax
import jax.numpy as jnp
from jax import lax
from jax.experimental import pallas as pl
from jax.experimental.pallas import tpu as pltpu
from jax.sharding import PartitionSpec as P

PASSES = lax.Precision.HIGH
VMEM = pltpu.MemorySpace.VMEM
NEAR_COST = 15_000_000_000


def contract(left, right, left_dim, right_dim):
    return lax.dot_general(
        left,
        right,
        (((left_dim,), (right_dim,)), ((), ())),
        precision=PASSES,
        preferred_element_type=jnp.float32,
    )


def passed_along(shard, axis, by):
    size = lax.axis_size(axis)
    return lax.ppermute(shard, axis, [(i, (i + by) % size) for i in range(size)])


def swapped(shard, axis, bit):
    size = lax.axis_size(axis)
    return lax.ppermute(shard, axis, [(i, i ^ bit) for i in range(size)])


def after(value, *gates):
    return lax.optimization_barrier((value,) + gates)[0]


def in_vmem(count):
    return [pl.BlockSpec(memory_space=VMEM)] * count


def limit(mib):
    return pltpu.CompilerParams(vmem_limit_bytes=mib * 2**20)


def cost(flops):
    return pl.CostEstimate(flops=flops, bytes_accessed=0, transcendentals=0)


def halves(value):
    high = value.astype(jnp.bfloat16)
    low = (value - high.astype(jnp.float32)).astype(jnp.bfloat16)
    return high, low


def dot3(left, right, right_dim):
    (lh, ll), (rh, rl) = left, right
    dims = (((1,), (right_dim,)), ((), ()))
    total = lax.dot_general(ll, rh, dims, preferred_element_type=jnp.float32)
    total += lax.dot_general(lh, rl, dims, preferred_element_type=jnp.float32)
    return total + lax.dot_general(lh, rh, dims, preferred_element_type=jnp.float32)


def stacked(refs):
    return jnp.concatenate([one[...] for one in refs], 0)


def like(rows, width, dtype):
    return jax.ShapeDtypeStruct((rows, width), dtype)


def near_fit_kernel(rows, metric, occ, kept, fit_high, fit_low, high, low, occ_tile, kept_tile):
    parts = halves(metric[...])
    high[...], low[...] = parts
    fit_high[...], fit_low[...] = halves(dot3(halves(rows[...]), parts, 1))
    occ_tile[...] = jnp.broadcast_to(occ[...], occ_tile.shape)
    kept_tile[...] = jnp.broadcast_to(kept[...].astype(jnp.float32), kept_tile.shape)


def near_fit(rows, metric, occ, kept):
    (count, width), near = rows.shape, metric.shape[0]
    return pl.pallas_call(
        near_fit_kernel,
        out_shape=[like(count, near, jnp.bfloat16)] * 2
        + [like(near, width, jnp.bfloat16)] * 2
        + [like(8, 128, jnp.float32)] * 2,
        in_specs=in_vmem(4),
        out_specs=in_vmem(6),
        compiler_params=limit(16),
        cost_estimate=cost(NEAR_COST),
        name="near_fit",
    )(rows, metric, occ[None, :], kept[None, :])


def turn_own_kernel(rows, fit_high, fit_low, near_high, near_low, *refs):
    pieces, (out_high, out_low, high, low) = refs[:-4], refs[-4:]
    parts = halves(stacked(pieces))
    high[...], low[...] = parts
    fit = halves(dot3(halves(rows[...]), parts, 1))
    total = dot3(fit, parts, 0)
    total += dot3((fit_high[...], fit_low[...]), (near_high[...], near_low[...]), 0)
    out_high[...], out_low[...] = halves(total)


def turn_own(rows, near, pieces):
    (count, width), far = rows.shape, sum(piece.shape[0] for piece in pieces)
    return pl.pallas_call(
        turn_own_kernel,
        out_shape=[like(count, width, jnp.bfloat16)] * 2 + [like(far, width, jnp.bfloat16)] * 2,
        in_specs=in_vmem(5 + len(pieces)),
        out_specs=in_vmem(4),
        compiler_params=limit(20),
        cost_estimate=cost(12 * count * far * width),
        name="turn_own",
    )(rows, *near, *pieces)


def turn_kernel(near_high, near_low, far_high, far_low, *refs):
    cuts, (out_high, out_low) = refs[:-2], refs[-2:]
    rows = halves(stacked(cuts))
    total = 0
    for parts in ((near_high[...], near_low[...]), (far_high[...], far_low[...])):
        total += dot3(halves(dot3(rows, parts, 1)), parts, 0)
    out_high[...], out_low[...] = halves(total)


def turn(cuts, near, far):
    count, width = sum(one.shape[0] for one in cuts), cuts[0].shape[1]
    return pl.pallas_call(
        turn_kernel,
        out_shape=[like(count, width, jnp.bfloat16)] * 2,
        in_specs=in_vmem(4 + len(cuts)),
        out_specs=in_vmem(2),
        compiler_params=limit(20),
        cost_estimate=cost(12 * count * width * (near[0].shape[0] + far[0].shape[0])),
        name="turn",
    )(*near, *far, *cuts)


def spots_of(tiles):
    pairs = []
    for a in range(tiles):
        for b in range(a, tiles):
            halves_of = [(2 * a + r, 2 * b + c) for r in (0, 1) for c in (0, 1)]
            pairs += [pair for pair in halves_of if pair[0] <= pair[1]]
    return {pair: k for k, pair in enumerate(pairs)}


def row_spots(n, tiles):
    spots = spots_of(tiles)
    return {pair: k for pair, k in spots.items() if pair[0] // 2 == n or pair[1] // 2 == n}


def tail_kernel(v, tiles, scale, occ, low_occ, kept, vir, own_high, own_low, far_high, far_low, *refs):
    lows, (blocks, value), scratch = refs[:-8], refs[-8:-6], refs[-6:]
    amp, amp_t, high, low, high_t, low_t = scratch
    n = lax.axis_index("narrow")
    virtuals = v * tiles
    at = [pl.ds(pl.multiple_of(lax.rem(n - a + tiles, tiles) * v, v), v) for a in range(tiles)]
    row = jnp.concatenate([vir[:, one] for one in at], 1)
    col = jnp.broadcast_to(row, (128, virtuals)).T[:, :1]
    gap = occ[:1, :1] + low_occ[:1, :1]
    weight = kept[:1, :1]
    right = halves(stacked(lows))
    left = (own_high[...], own_low[...]), (far_high[...], far_low[...])
    pairs = [dot3(one, right, 1) for one in left]
    spans = slice(0, v), slice(v, virtuals)
    for pair, span in zip(pairs, spans):
        amp[span, :] = pair / (col[span, :] + row - gap)
    amp_t[...] = amp[...].T
    total = jnp.float32(0)
    for pair, span in zip(pairs, spans):
        total += jnp.sum(pair * (2.0 * amp[span, :] - amp_t[span, :]))
    value[...] = -weight * total / (virtuals * virtuals)
    high[...], low[...] = halves(amp[...])
    high_t[...], low_t[...] = halves(amp_t[...])
    spots, half = spots_of(tiles), v // 2
    for a in range(tiles):
        for b in range(a, tiles):
            block = dot3((high[at[a], :], low[at[a], :]), (high_t[:, at[b]], low_t[:, at[b]]), 0)
            block += dot3((high_t[at[a], :], low_t[at[a], :]), (high[:, at[b]], low[:, at[b]]), 0)
            block *= weight * scale
            for r in (0, 1):
                for c in (0, 1):
                    k = spots.get((2 * a + r, 2 * b + c))
                    if k is not None:
                        blocks[k] = block[r * half : (r + 1) * half, c * half : (c + 1) * half]


def tail(turned, raw_low, energies, v, scale):
    virtuals, width = energies[-1].shape[0], raw_low[0].shape[1]
    tiles = virtuals // v
    count = len(spots_of(tiles))
    square = [pltpu.VMEM((virtuals, virtuals), kind) for kind in (jnp.float32, jnp.bfloat16)]
    return pl.pallas_call(
        functools.partial(tail_kernel, v, tiles, scale),
        out_shape=[
            jax.ShapeDtypeStruct((count, v // 2, v // 2), jnp.float32),
            jax.ShapeDtypeStruct((1, 1), jnp.float32),
        ],
        in_specs=in_vmem(8 + len(raw_low)),
        out_specs=in_vmem(2),
        scratch_shapes=[square[0]] * 2 + [square[1]] * 4,
        compiler_params=limit(24),
        cost_estimate=cost(6 * virtuals * virtuals * width + 3 * count * v * v * virtuals),
        name="tail",
    )(*energies[:-1], energies[-1][None, :], *turned, *raw_low)


def tail_plain(turned, raw_low, energies, v, scale):
    occ, low_occ, kept, vir = energies
    virtuals = vir.shape[0]
    narrow = virtuals // v
    order = ((lax.axis_index("narrow") - jnp.arange(narrow)) % narrow * v)[:, None] + jnp.arange(v)[None, :]
    order = order.reshape(virtuals)
    weight = kept[0, 0]
    levels = vir[order]
    own_high, own_low, far_high, far_low = [one.astype(jnp.float32) for one in turned]
    left = jnp.concatenate([own_high + own_low, far_high + far_low], 0)
    pair_ints = contract(left, jnp.concatenate(raw_low, 0), 1, 1)
    amplitude = pair_ints / (levels[:, None] + levels[None, :] - occ[0, 0] - low_occ[0, 0])
    value = jnp.sum(pair_ints * (2.0 * amplitude - amplitude.T)) * -weight / (virtuals * virtuals)
    amplitude = amplitude[order][:, order]
    blocks, half = [], v // 2
    for at in range(0, virtuals, half):
        row = contract(amplitude[at : at + half], amplitude[at:], 1, 1)
        row = row + contract(amplitude[:, at : at + half], amplitude[:, at:], 0, 0)
        blocks += jnp.split(row * (weight * scale), (virtuals - at) // half, 1)
    return jnp.stack(blocks), value.reshape(1, 1)


def halved(blocks, w, bit):
    half = blocks.shape[1] // 2
    side = (w // bit) % 2
    kept = lax.dynamic_slice_in_dim(blocks, side * half, half, 1)
    given = lax.dynamic_slice_in_dim(blocks, (1 - side) * half, half, 1)
    return kept + swapped(given, "wide", bit)


def doubled(blocks, w, bit):
    other = swapped(blocks, "wide", bit)
    low = (w // bit) % 2 == 0
    return jnp.concatenate([jnp.where(low, blocks, other), jnp.where(low, other, blocks)], 1)


def quartered(blocks, w, low):
    rows, spot = blocks.shape[1] // 4, (w // low) % 4
    total = lax.dynamic_slice_in_dim(blocks, spot * rows, rows, 1)
    for flip in (3, 1, 2):
        given = lax.dynamic_slice_in_dim(blocks, (spot ^ flip) * rows, rows, 1)
        total = total + swapped(given, "wide", flip * low)
    return total


def quadrupled(blocks, w, low):
    held = [blocks] + [swapped(blocks, "wide", flip * low) for flip in (1, 2, 3)]
    spot = (w // low) % 4
    return jnp.concatenate(
        [lax.select_n(spot, *[held[at ^ mine] for mine in range(4)]) for at in range(4)], 1
    )


def own_rows(blocks, n, bit):
    wide, narrow = lax.axis_size("wide"), lax.axis_size("narrow")
    spots = [list(row_spots(m, narrow).values()) for m in range(narrow)]

    def of(m):
        picked = [jnp.concatenate([blocks[k : k + 1] for k in row]) for row in spots]
        return lax.select_n(m, *picked)

    total = of(n)
    for s in range(narrow):
        given = of((n + s) % narrow)
        for flip in (0, bit):
            if s or flip:
                steps = [
                    (w * narrow + m, (w ^ flip) * narrow + (m + s) % narrow)
                    for w in range(wide)
                    for m in range(narrow)
                ]
                total = total + lax.ppermute(given, ("wide", "narrow"), steps)
    return total


def row_of(full, m, narrow):
    held = {pair: k for k, pair in enumerate(row_spots(m, narrow))}
    for r in (0, 1):
        for c in range(2 * narrow):
            pair = (2 * m + r, c)
            yield r, c, full[held[pair]] if pair in held else full[held[c, 2 * m + r]].T


def assembled_kernel(narrow, mine, other, out):
    first = lax.rem(lax.axis_index("wide"), 2) == 0
    half = 2 * mine.shape[1]
    whole = jnp.concatenate(
        [jnp.where(first, mine[...], other[...]), jnp.where(first, other[...], mine[...])], 1
    )
    for m in range(narrow):

        @pl.when(lax.axis_index("narrow") == m)
        def _():
            for r, c, block in row_of(whole, m, narrow):
                out[r * half : (r + 1) * half, c * half : (c + 1) * half] = block


def assembled(mine, w, n, narrow):
    other = swapped(mine, "wide", 1)
    half = 2 * mine.shape[1]
    if half % 128 == 0:
        return pl.pallas_call(
            functools.partial(assembled_kernel, narrow),
            out_shape=like(2 * half, 2 * half * narrow, jnp.float32),
            in_specs=in_vmem(2),
            out_specs=in_vmem(1)[0],
            compiler_params=limit(8),
            name="assembled",
        )(mine, other)
    first = w % 2 == 0
    whole = jnp.concatenate([jnp.where(first, mine, other), jnp.where(first, other, mine)], 1)
    rows = []
    for m in range(narrow):
        blocks = [block for *_, block in row_of(whole, m, narrow)]
        spans = blocks[: 2 * narrow], blocks[2 * narrow :]
        rows.append(jnp.concatenate([jnp.concatenate(span, 1) for span in spans], 0))
    return lax.select_n(n, *rows)


def on_device(raw_ints, metric, occ_energy, vir_energy, pair_kept):
    wide, narrow = lax.axis_size("wide"), lax.axis_size("narrow")
    w, n = lax.axis_index("wide"), lax.axis_index("narrow")
    v = raw_ints.shape[1]
    virtuals = v * narrow

    near = 4
    chunks = [(0, v // 2), (v // 2, v // 2)]
    rows = metric.shape[0] // near
    piece = lax.dynamic_slice_in_dim(metric, (w % near) * rows, rows, 0)
    far = [passed_along(piece, "narrow", s) for s in range(1, narrow)]
    own = lax.dynamic_index_in_dim(raw_ints, n, 0, keepdims=False)
    raw_low = [passed_along(own[: v // 2], "wide", 1)]
    arrived, given = [], []
    for s in range(1, narrow):
        block = lax.dynamic_index_in_dim(raw_ints, (n + s) % narrow, 0, keepdims=False)
        parts = [block[first : first + rows] for first, rows in chunks]
        arrived += [passed_along(one, "narrow", s) for one in reversed(parts)][::-1]
        given += parts
    *fit_near, occ, kept = near_fit(after(own, *given), metric, occ_energy, pair_kept)
    low_occ = passed_along(occ, "wide", 1)
    far = [after(one, fit_near[0]) for one in far]
    far_x = [swapped(one, "wide", 2) for one in far]
    far_core = [swapped(one, "wide", 1) for one in far]
    raw_low.append(passed_along(after(own[v // 2 :], *far), "wide", 1))
    raw_low += [passed_along(one, "wide", 1) for one in arrived[:-1]]
    far_x = [after(one, raw_low[0], arrived[0]) for one in far_x]
    far_last = [swapped(one, "wide", 1) for one in far_x]

    *own_turned, far_high, far_low = turn_own(after(own, raw_low[1], low_occ), fit_near, far + far_core + far_x + far_last)
    raw_low.append(passed_along(after(arrived[-1], own_turned[0]), "wide", 1))
    turned = [*own_turned, *turn(arrived, fit_near[2:], (far_high, far_low))]

    form = tail if v % 128 == 0 else tail_plain
    energies = occ, low_occ, kept, vir_energy
    blocks, own_value = form(turned, raw_low, energies, v, 0.0625 / (wide * narrow))
    blocks, own_value, w, n = lax.optimization_barrier((blocks, own_value, w, n))
    own_value = own_value.reshape(1)
    upper_value = passed_along(own_value, "wide", -1)

    first, *bits, last = [1 << k for k in range(wide.bit_length() - 1)]
    low, bits = bits[0], bits[2:]
    blocks = halved(blocks, w, first)
    blocks = quartered(blocks, w, low)
    for bit in bits:
        blocks = halved(blocks, w, bit)
    full = own_rows(blocks, n, last)
    full, upper_value = lax.optimization_barrier((full, upper_value))
    for bit in reversed(bits):
        full = doubled(full, w, bit)
    full = quadrupled(full, w, low)
    return assembled(full, w, n, narrow), own_value + upper_value


def solution(mesh):
    placed = (
        P("wide", "narrow", None),
        P("narrow", None),
        P(("wide", "narrow")),
        P(),
        P(("wide", "narrow")),
    )
    return jax.shard_map(
        on_device,
        mesh=mesh,
        in_specs=placed,
        out_specs=(P("narrow", None), P(("wide", "narrow"))),
        check_vma=False,
    )
```

```python
import functools

import jax
import jax.numpy as jnp
from jax import lax
from jax.experimental import pallas as pl
from jax.experimental.pallas import tpu as pltpu
from jax.sharding import PartitionSpec as P

PASSES = lax.Precision.HIGH
VMEM = pltpu.MemorySpace.VMEM
NEAR_COST = 15_000_000_000


def contract(left, right, left_dim, right_dim):
    return lax.dot_general(
        left,
        right,
        (((left_dim,), (right_dim,)), ((), ())),
        precision=PASSES,
        preferred_element_type=jnp.float32,
    )


def passed_along(shard, axis, by):
    size = lax.axis_size(axis)
    return lax.ppermute(shard, axis, [(i, (i + by) % size) for i in range(size)])


def swapped(shard, axis, bit):
    size = lax.axis_size(axis)
    return lax.ppermute(shard, axis, [(i, i ^ bit) for i in range(size)])


def after(value, *gates):
    return lax.optimization_barrier((value,) + gates)[0]


def in_vmem(count):
    return [pl.BlockSpec(memory_space=VMEM)] * count


def limit(mib):
    return pltpu.CompilerParams(vmem_limit_bytes=mib * 2**20)


def cost(flops):
    return pl.CostEstimate(flops=flops, bytes_accessed=0, transcendentals=0)


def halves(value):
    high = value.astype(jnp.bfloat16)
    low = (value - high.astype(jnp.float32)).astype(jnp.bfloat16)
    return high, low


def dot3(left, right, right_dim):
    (lh, ll), (rh, rl) = left, right
    dims = (((1,), (right_dim,)), ((), ()))
    total = lax.dot_general(ll, rh, dims, preferred_element_type=jnp.float32)
    total += lax.dot_general(lh, rl, dims, preferred_element_type=jnp.float32)
    return total + lax.dot_general(lh, rh, dims, preferred_element_type=jnp.float32)


def stacked(refs):
    return jnp.concatenate([one[...] for one in refs], 0)


def like(rows, width, dtype):
    return jax.ShapeDtypeStruct((rows, width), dtype)


def near_fit_kernel(rows, metric, occ, kept, _, fit_high, fit_low, high, low, occ_tile, kept_tile):
    parts = halves(metric[...])
    high[...], low[...] = parts
    fit_high[...], fit_low[...] = halves(dot3(halves(rows[...]), parts, 1))
    occ_tile[...] = jnp.broadcast_to(occ[...], occ_tile.shape)
    kept_tile[...] = jnp.broadcast_to(kept[...].astype(jnp.float32), kept_tile.shape)


def near_fit(rows, metric, occ, kept, piece):
    (count, width), near = rows.shape, metric.shape[0]
    return pl.pallas_call(
        near_fit_kernel,
        out_shape=[like(count, near, jnp.bfloat16)] * 2
        + [like(near, width, jnp.bfloat16)] * 2
        + [like(8, 128, jnp.float32)] * 2,
        in_specs=in_vmem(5),
        out_specs=in_vmem(6),
        compiler_params=limit(16),
        cost_estimate=cost(NEAR_COST),
        name="near_fit",
    )(rows, metric, occ[None, :], kept[None, :], piece)


def turn_own_kernel(rows, fit_high, fit_low, near_high, near_low, *refs):
    pieces, (out_high, out_low, high, low) = refs[:-4], refs[-4:]
    parts = halves(stacked(pieces))
    high[...], low[...] = parts
    fit = halves(dot3(halves(rows[...]), parts, 1))
    total = dot3(fit, parts, 0)
    total += dot3((fit_high[...], fit_low[...]), (near_high[...], near_low[...]), 0)
    out_high[...], out_low[...] = halves(total)


def turn_own(rows, near, pieces):
    (count, width), far = rows.shape, sum(piece.shape[0] for piece in pieces)
    return pl.pallas_call(
        turn_own_kernel,
        out_shape=[like(count, width, jnp.bfloat16)] * 2 + [like(far, width, jnp.bfloat16)] * 2,
        in_specs=in_vmem(5 + len(pieces)),
        out_specs=in_vmem(4),
        compiler_params=limit(20),
        cost_estimate=cost(12 * count * far * width),
        name="turn_own",
    )(rows, *near, *pieces)


def turn_kernel(near_high, near_low, far_high, far_low, *refs):
    cuts, (out_high, out_low) = refs[:-2], refs[-2:]
    rows = halves(stacked(cuts))
    total = 0
    for parts in ((near_high[...], near_low[...]), (far_high[...], far_low[...])):
        total += dot3(halves(dot3(rows, parts, 1)), parts, 0)
    out_high[...], out_low[...] = halves(total)


def turn(cuts, near, far):
    count, width = sum(one.shape[0] for one in cuts), cuts[0].shape[1]
    return pl.pallas_call(
        turn_kernel,
        out_shape=[like(count, width, jnp.bfloat16)] * 2,
        in_specs=in_vmem(4 + len(cuts)),
        out_specs=in_vmem(2),
        compiler_params=limit(20),
        cost_estimate=cost(12 * count * width * (near[0].shape[0] + far[0].shape[0])),
        name="turn",
    )(*near, *far, *cuts)


def spots_of(tiles):
    pairs = []
    for a in range(tiles):
        for b in range(a, tiles):
            halves_of = [(2 * a + r, 2 * b + c) for r in (0, 1) for c in (0, 1)]
            pairs += [pair for pair in halves_of if pair[0] <= pair[1]]
    return {pair: k for k, pair in enumerate(pairs)}


def row_spots(n, tiles):
    spots = spots_of(tiles)
    return {pair: k for pair, k in spots.items() if pair[0] // 2 == n or pair[1] // 2 == n}


def tail_kernel(v, tiles, scale, occ, low_occ, kept, vir, own_high, own_low, far_high, far_low, *refs):
    lows, (blocks, value), scratch = refs[:-8], refs[-8:-6], refs[-6:]
    amp, amp_t, high, low, high_t, low_t = scratch
    n = lax.axis_index("narrow")
    virtuals = v * tiles
    at = [pl.ds(pl.multiple_of(lax.rem(n - a + tiles, tiles) * v, v), v) for a in range(tiles)]
    row = jnp.concatenate([vir[:, one] for one in at], 1)
    col = jnp.broadcast_to(row, (128, virtuals)).T[:, :1]
    gap = occ[:1, :1] + low_occ[:1, :1]
    weight = kept[:1, :1]
    right = halves(stacked(lows))
    left = (own_high[...], own_low[...]), (far_high[...], far_low[...])
    pairs = [dot3(one, right, 1) for one in left]
    spans = slice(0, v), slice(v, virtuals)
    for pair, span in zip(pairs, spans):
        amp[span, :] = pair / (col[span, :] + row - gap)
    amp_t[...] = amp[...].T
    total = jnp.float32(0)
    for pair, span in zip(pairs, spans):
        total += jnp.sum(pair * (2.0 * amp[span, :] - amp_t[span, :]))
    value[...] = -weight * total / (virtuals * virtuals)
    high[...], low[...] = halves(amp[...])
    high_t[...], low_t[...] = halves(amp_t[...])
    spots, half = spots_of(tiles), v // 2
    for a in range(tiles):
        for b in range(a, tiles):
            block = dot3((high[at[a], :], low[at[a], :]), (high_t[:, at[b]], low_t[:, at[b]]), 0)
            block += dot3((high_t[at[a], :], low_t[at[a], :]), (high[:, at[b]], low[:, at[b]]), 0)
            block *= weight * scale
            for r in (0, 1):
                for c in (0, 1):
                    k = spots.get((2 * a + r, 2 * b + c))
                    if k is not None:
                        blocks[k] = block[r * half : (r + 1) * half, c * half : (c + 1) * half]


def tail(turned, raw_low, energies, v, scale):
    virtuals, width = energies[-1].shape[0], raw_low[0].shape[1]
    tiles = virtuals // v
    count = len(spots_of(tiles))
    square = [pltpu.VMEM((virtuals, virtuals), kind) for kind in (jnp.float32, jnp.bfloat16)]
    return pl.pallas_call(
        functools.partial(tail_kernel, v, tiles, scale),
        out_shape=[
            jax.ShapeDtypeStruct((count, v // 2, v // 2), jnp.float32),
            jax.ShapeDtypeStruct((1, 1), jnp.float32),
        ],
        in_specs=in_vmem(8 + len(raw_low)),
        out_specs=in_vmem(2),
        scratch_shapes=[square[0]] * 2 + [square[1]] * 4,
        compiler_params=limit(24),
        cost_estimate=cost(6 * virtuals * virtuals * width + 3 * count * v * v * virtuals),
        name="tail",
    )(*energies[:-1], energies[-1][None, :], *turned, *raw_low)


def tail_plain(turned, raw_low, energies, v, scale):
    occ, low_occ, kept, vir = energies
    virtuals = vir.shape[0]
    narrow = virtuals // v
    order = ((lax.axis_index("narrow") - jnp.arange(narrow)) % narrow * v)[:, None] + jnp.arange(v)[None, :]
    order = order.reshape(virtuals)
    weight = kept[0, 0]
    levels = vir[order]
    own_high, own_low, far_high, far_low = [one.astype(jnp.float32) for one in turned]
    left = jnp.concatenate([own_high + own_low, far_high + far_low], 0)
    pair_ints = contract(left, jnp.concatenate(raw_low, 0), 1, 1)
    amplitude = pair_ints / (levels[:, None] + levels[None, :] - occ[0, 0] - low_occ[0, 0])
    value = jnp.sum(pair_ints * (2.0 * amplitude - amplitude.T)) * -weight / (virtuals * virtuals)
    amplitude = amplitude[order][:, order]
    blocks, half = [], v // 2
    for at in range(0, virtuals, half):
        row = contract(amplitude[at : at + half], amplitude[at:], 1, 1)
        row = row + contract(amplitude[:, at : at + half], amplitude[:, at:], 0, 0)
        blocks += jnp.split(row * (weight * scale), (virtuals - at) // half, 1)
    return jnp.stack(blocks), value.reshape(1, 1)


def halved(blocks, w, bit):
    half = blocks.shape[1] // 2
    side = (w // bit) % 2
    kept = lax.dynamic_slice_in_dim(blocks, side * half, half, 1)
    given = lax.dynamic_slice_in_dim(blocks, (1 - side) * half, half, 1)
    return kept + swapped(given, "wide", bit)


def doubled(blocks, w, bit):
    other = swapped(blocks, "wide", bit)
    low = (w // bit) % 2 == 0
    return jnp.concatenate([jnp.where(low, blocks, other), jnp.where(low, other, blocks)], 1)


def quartered(blocks, w, low):
    rows, spot = blocks.shape[1] // 4, (w // low) % 4
    total = lax.dynamic_slice_in_dim(blocks, spot * rows, rows, 1)
    for flip in (3, 1, 2):
        given = lax.dynamic_slice_in_dim(blocks, (spot ^ flip) * rows, rows, 1)
        total = total + swapped(given, "wide", flip * low)
    return total


def quadrupled(blocks, w, low):
    held = [blocks] + [swapped(blocks, "wide", flip * low) for flip in (1, 2, 3)]
    spot = (w // low) % 4
    return jnp.concatenate(
        [lax.select_n(spot, *[held[at ^ mine] for mine in range(4)]) for at in range(4)], 1
    )


def own_rows(blocks, n, bit):
    wide, narrow = lax.axis_size("wide"), lax.axis_size("narrow")
    spots = [list(row_spots(m, narrow).values()) for m in range(narrow)]

    def of(m):
        picked = [jnp.concatenate([blocks[k : k + 1] for k in row]) for row in spots]
        return lax.select_n(m, *picked)

    total = of(n)
    for s in range(narrow):
        given = of((n + s) % narrow)
        for flip in (0, bit):
            if s or flip:
                steps = [
                    (w * narrow + m, (w ^ flip) * narrow + (m + s) % narrow)
                    for w in range(wide)
                    for m in range(narrow)
                ]
                total = total + lax.ppermute(given, ("wide", "narrow"), steps)
    return total


def row_of(full, m, narrow):
    held = {pair: k for k, pair in enumerate(row_spots(m, narrow))}
    for r in (0, 1):
        for c in range(2 * narrow):
            pair = (2 * m + r, c)
            yield r, c, full[held[pair]] if pair in held else full[held[c, 2 * m + r]].T


def assembled_kernel(narrow, mine, other, out):
    first = lax.rem(lax.axis_index("wide"), 2) == 0
    half = 2 * mine.shape[1]
    whole = jnp.concatenate(
        [jnp.where(first, mine[...], other[...]), jnp.where(first, other[...], mine[...])], 1
    )
    for m in range(narrow):

        @pl.when(lax.axis_index("narrow") == m)
        def _():
            for r, c, block in row_of(whole, m, narrow):
                out[r * half : (r + 1) * half, c * half : (c + 1) * half] = block


def assembled(mine, w, n, narrow):
    other = swapped(mine, "wide", 1)
    half = 2 * mine.shape[1]
    if half % 128 == 0:
        return pl.pallas_call(
            functools.partial(assembled_kernel, narrow),
            out_shape=like(2 * half, 2 * half * narrow, jnp.float32),
            in_specs=in_vmem(2),
            out_specs=in_vmem(1)[0],
            compiler_params=limit(8),
            name="assembled",
        )(mine, other)
    first = w % 2 == 0
    whole = jnp.concatenate([jnp.where(first, mine, other), jnp.where(first, other, mine)], 1)
    rows = []
    for m in range(narrow):
        blocks = [block for *_, block in row_of(whole, m, narrow)]
        spans = blocks[: 2 * narrow], blocks[2 * narrow :]
        rows.append(jnp.concatenate([jnp.concatenate(span, 1) for span in spans], 0))
    return lax.select_n(n, *rows)


def on_device(raw_ints, metric, occ_energy, vir_energy, pair_kept):
    wide, narrow = lax.axis_size("wide"), lax.axis_size("narrow")
    w, n = lax.axis_index("wide"), lax.axis_index("narrow")
    v = raw_ints.shape[1]
    virtuals = v * narrow

    near = 4
    chunks = [(0, v // 2), (v // 2, v // 2)]
    rows = metric.shape[0] // near
    piece = lax.dynamic_slice_in_dim(metric, (w % near) * rows, rows, 0)
    far = [passed_along(piece, "narrow", s) for s in range(1, narrow)]
    own = lax.dynamic_index_in_dim(raw_ints, n, 0, keepdims=False)
    raw_low = [passed_along(own, "wide", 1)]
    arrived, given = [], []
    for s in range(1, narrow):
        block = lax.dynamic_index_in_dim(raw_ints, (n + s) % narrow, 0, keepdims=False)
        parts = [block[first : first + rows] for first, rows in chunks]
        arrived += [passed_along(one, "narrow", s) for one in reversed(parts)][::-1]
        given += parts
    *fit_near, occ, kept = near_fit(after(own, *given), metric, occ_energy, pair_kept, piece)
    low_occ = passed_along(occ, "wide", 1)
    far = [after(one, fit_near[0]) for one in far]
    far_x = [swapped(one, "wide", 2) for one in far]
    far_core = [swapped(one, "wide", 1) for one in far]
    raw_low += [passed_along(one, "wide", 1) for one in arrived[:-1]]
    far_x = [after(one, raw_low[0], low_occ, arrived[0]) for one in far_x]
    far_last = [swapped(one, "wide", 1) for one in far_x]

    *own_turned, far_high, far_low = turn_own(own, fit_near, far + far_core + far_x + far_last)
    raw_low.append(passed_along(after(arrived[-1], own_turned[0]), "wide", 1))
    turned = [*own_turned, *turn(arrived, fit_near[2:], (far_high, far_low))]

    form = tail if v % 128 == 0 else tail_plain
    energies = occ, low_occ, kept, vir_energy
    blocks, own_value = form(turned, raw_low, energies, v, 0.0625 / (wide * narrow))
    blocks, own_value, w, n = lax.optimization_barrier((blocks, own_value, w, n))
    own_value = own_value.reshape(1)
    upper_value = passed_along(own_value, "wide", -1)

    first, *bits, last = [1 << k for k in range(wide.bit_length() - 1)]
    low, bits = bits[0], bits[2:]
    blocks = halved(blocks, w, first)
    blocks = quartered(blocks, w, low)
    for bit in bits:
        blocks = halved(blocks, w, bit)
    full = own_rows(blocks, n, last)
    full, upper_value = lax.optimization_barrier((full, upper_value))
    for bit in reversed(bits):
        full = doubled(full, w, bit)
    full = quadrupled(full, w, low)
    return assembled(full, w, n, narrow), own_value + upper_value


def solution(mesh):
    placed = (
        P("wide", "narrow", None),
        P("narrow", None),
        P(("wide", "narrow")),
        P(),
        P(("wide", "narrow")),
    )
    return jax.shard_map(
        on_device,
        mesh=mesh,
        in_specs=placed,
        out_specs=(P("narrow", None), P(("wide", "narrow"))),
        check_vma=False,
    )
```

```python
import functools

import jax
import jax.numpy as jnp
from jax import lax
from jax.experimental import pallas as pl
from jax.experimental.pallas import tpu as pltpu
from jax.sharding import PartitionSpec as P

PASSES = lax.Precision.HIGH
VMEM = pltpu.MemorySpace.VMEM
NEAR_COST = 15_000_000_000


def contract(left, right, left_dim, right_dim):
    return lax.dot_general(
        left,
        right,
        (((left_dim,), (right_dim,)), ((), ())),
        precision=PASSES,
        preferred_element_type=jnp.float32,
    )


def passed_along(shard, axis, by):
    size = lax.axis_size(axis)
    return lax.ppermute(shard, axis, [(i, (i + by) % size) for i in range(size)])


def swapped(shard, axis, bit):
    size = lax.axis_size(axis)
    return lax.ppermute(shard, axis, [(i, i ^ bit) for i in range(size)])


def after(value, *gates):
    return lax.optimization_barrier((value,) + gates)[0]


def in_vmem(count):
    return [pl.BlockSpec(memory_space=VMEM)] * count


def limit(mib):
    return pltpu.CompilerParams(vmem_limit_bytes=mib * 2**20)


def cost(flops):
    return pl.CostEstimate(flops=flops, bytes_accessed=0, transcendentals=0)


def halves(value):
    high = value.astype(jnp.bfloat16)
    low = (value - high.astype(jnp.float32)).astype(jnp.bfloat16)
    return high, low


def dot3(left, right, right_dim):
    (lh, ll), (rh, rl) = left, right
    dims = (((1,), (right_dim,)), ((), ()))
    total = lax.dot_general(ll, rh, dims, preferred_element_type=jnp.float32)
    total += lax.dot_general(lh, rl, dims, preferred_element_type=jnp.float32)
    return total + lax.dot_general(lh, rh, dims, preferred_element_type=jnp.float32)


def stacked(refs):
    return jnp.concatenate([one[...] for one in refs], 0)


def like(rows, width, dtype):
    return jax.ShapeDtypeStruct((rows, width), dtype)


def near_fit_kernel(rows, metric, occ, kept, _, fit_high, fit_low, high, low, occ_tile, kept_tile):
    parts = halves(metric[...])
    high[...], low[...] = parts
    fit_high[...], fit_low[...] = halves(dot3(halves(rows[...]), parts, 1))
    occ_tile[...] = jnp.broadcast_to(occ[...], occ_tile.shape)
    kept_tile[...] = jnp.broadcast_to(kept[...].astype(jnp.float32), kept_tile.shape)


def near_fit(rows, metric, occ, kept, piece):
    (count, width), near = rows.shape, metric.shape[0]
    return pl.pallas_call(
        near_fit_kernel,
        out_shape=[like(count, near, jnp.bfloat16)] * 2
        + [like(near, width, jnp.bfloat16)] * 2
        + [like(8, 128, jnp.float32)] * 2,
        in_specs=in_vmem(5),
        out_specs=in_vmem(6),
        compiler_params=limit(16),
        cost_estimate=cost(NEAR_COST),
        name="near_fit",
    )(rows, metric, occ[None, :], kept[None, :], piece)


def turn_own_kernel(rows, fit_high, fit_low, near_high, near_low, *refs):
    pieces, (out_high, out_low, high, low) = refs[:-4], refs[-4:]
    parts = halves(stacked(pieces))
    high[...], low[...] = parts
    fit = halves(dot3(halves(rows[...]), parts, 1))
    total = dot3(fit, parts, 0)
    total += dot3((fit_high[...], fit_low[...]), (near_high[...], near_low[...]), 0)
    out_high[...], out_low[...] = halves(total)


def turn_own(rows, near, pieces):
    (count, width), far = rows.shape, sum(piece.shape[0] for piece in pieces)
    return pl.pallas_call(
        turn_own_kernel,
        out_shape=[like(count, width, jnp.bfloat16)] * 2 + [like(far, width, jnp.bfloat16)] * 2,
        in_specs=in_vmem(5 + len(pieces)),
        out_specs=in_vmem(4),
        compiler_params=limit(20),
        cost_estimate=cost(12 * count * far * width),
        name="turn_own",
    )(rows, *near, *pieces)


def turn_kernel(near_high, near_low, far_high, far_low, *refs):
    cuts, (out_high, out_low) = refs[:-2], refs[-2:]
    rows = halves(stacked(cuts))
    total = 0
    for parts in ((near_high[...], near_low[...]), (far_high[...], far_low[...])):
        total += dot3(halves(dot3(rows, parts, 1)), parts, 0)
    out_high[...], out_low[...] = halves(total)


def turn(cuts, near, far):
    count, width = sum(one.shape[0] for one in cuts), cuts[0].shape[1]
    return pl.pallas_call(
        turn_kernel,
        out_shape=[like(count, width, jnp.bfloat16)] * 2,
        in_specs=in_vmem(4 + len(cuts)),
        out_specs=in_vmem(2),
        compiler_params=limit(20),
        cost_estimate=cost(12 * count * width * (near[0].shape[0] + far[0].shape[0])),
        name="turn",
    )(*near, *far, *cuts)


def spots_of(tiles):
    pairs = []
    for a in range(tiles):
        for b in range(a, tiles):
            halves_of = [(2 * a + r, 2 * b + c) for r in (0, 1) for c in (0, 1)]
            pairs += [pair for pair in halves_of if pair[0] <= pair[1]]
    return {pair: k for k, pair in enumerate(pairs)}


def row_spots(n, tiles):
    spots = spots_of(tiles)
    return {pair: k for pair, k in spots.items() if pair[0] // 2 == n or pair[1] // 2 == n}


def tail_kernel(v, tiles, scale, occ, low_occ, kept, vir, own_high, own_low, far_high, far_low, *refs):
    lows, (blocks, value), scratch = refs[:-8], refs[-8:-6], refs[-6:]
    amp, amp_t, high, low, high_t, low_t = scratch
    n = lax.axis_index("narrow")
    virtuals = v * tiles
    at = [pl.ds(pl.multiple_of(lax.rem(n - a + tiles, tiles) * v, v), v) for a in range(tiles)]
    row = jnp.concatenate([vir[:, one] for one in at], 1)
    col = jnp.broadcast_to(row, (128, virtuals)).T[:, :1]
    gap = occ[:1, :1] + low_occ[:1, :1]
    weight = kept[:1, :1]
    right = halves(stacked(lows))
    left = (own_high[...], own_low[...]), (far_high[...], far_low[...])
    pairs = [dot3(one, right, 1) for one in left]
    spans = slice(0, v), slice(v, virtuals)
    for pair, span in zip(pairs, spans):
        amp[span, :] = pair / (col[span, :] + row - gap)
    amp_t[...] = amp[...].T
    total = jnp.float32(0)
    for pair, span in zip(pairs, spans):
        total += jnp.sum(pair * (2.0 * amp[span, :] - amp_t[span, :]))
    value[...] = -weight * total / (virtuals * virtuals)
    high[...], low[...] = halves(amp[...])
    high_t[...], low_t[...] = halves(amp_t[...])
    spots, half = spots_of(tiles), v // 2
    for a in range(tiles):
        for b in range(a, tiles):
            block = dot3((high[at[a], :], low[at[a], :]), (high_t[:, at[b]], low_t[:, at[b]]), 0)
            block += dot3((high_t[at[a], :], low_t[at[a], :]), (high[:, at[b]], low[:, at[b]]), 0)
            block *= weight * scale
            for r in (0, 1):
                for c in (0, 1):
                    k = spots.get((2 * a + r, 2 * b + c))
                    if k is not None:
                        blocks[k] = block[r * half : (r + 1) * half, c * half : (c + 1) * half]


def tail(turned, raw_low, energies, v, scale):
    virtuals, width = energies[-1].shape[0], raw_low[0].shape[1]
    tiles = virtuals // v
    count = len(spots_of(tiles))
    square = [pltpu.VMEM((virtuals, virtuals), kind) for kind in (jnp.float32, jnp.bfloat16)]
    return pl.pallas_call(
        functools.partial(tail_kernel, v, tiles, scale),
        out_shape=[
            jax.ShapeDtypeStruct((count, v // 2, v // 2), jnp.float32),
            jax.ShapeDtypeStruct((1, 1), jnp.float32),
        ],
        in_specs=in_vmem(8 + len(raw_low)),
        out_specs=in_vmem(2),
        scratch_shapes=[square[0]] * 2 + [square[1]] * 4,
        compiler_params=limit(24),
        cost_estimate=cost(6 * virtuals * virtuals * width + 3 * count * v * v * virtuals),
        name="tail",
    )(*energies[:-1], energies[-1][None, :], *turned, *raw_low)


def tail_plain(turned, raw_low, energies, v, scale):
    occ, low_occ, kept, vir = energies
    virtuals = vir.shape[0]
    narrow = virtuals // v
    order = ((lax.axis_index("narrow") - jnp.arange(narrow)) % narrow * v)[:, None] + jnp.arange(v)[None, :]
    order = order.reshape(virtuals)
    weight = kept[0, 0]
    levels = vir[order]
    own_high, own_low, far_high, far_low = [one.astype(jnp.float32) for one in turned]
    left = jnp.concatenate([own_high + own_low, far_high + far_low], 0)
    pair_ints = contract(left, jnp.concatenate(raw_low, 0), 1, 1)
    amplitude = pair_ints / (levels[:, None] + levels[None, :] - occ[0, 0] - low_occ[0, 0])
    value = jnp.sum(pair_ints * (2.0 * amplitude - amplitude.T)) * -weight / (virtuals * virtuals)
    amplitude = amplitude[order][:, order]
    blocks, half = [], v // 2
    for at in range(0, virtuals, half):
        row = contract(amplitude[at : at + half], amplitude[at:], 1, 1)
        row = row + contract(amplitude[:, at : at + half], amplitude[:, at:], 0, 0)
        blocks += jnp.split(row * (weight * scale), (virtuals - at) // half, 1)
    return jnp.stack(blocks), value.reshape(1, 1)


def halved(blocks, w, bit):
    half = blocks.shape[1] // 2
    side = (w // bit) % 2
    kept = lax.dynamic_slice_in_dim(blocks, side * half, half, 1)
    given = lax.dynamic_slice_in_dim(blocks, (1 - side) * half, half, 1)
    return kept + swapped(given, "wide", bit)


def doubled(blocks, w, bit):
    other = swapped(blocks, "wide", bit)
    low = (w // bit) % 2 == 0
    return jnp.concatenate([jnp.where(low, blocks, other), jnp.where(low, other, blocks)], 1)


def quartered(blocks, w, low):
    rows, spot = blocks.shape[1] // 4, (w // low) % 4
    total = lax.dynamic_slice_in_dim(blocks, spot * rows, rows, 1)
    for flip in (3, 1, 2):
        given = lax.dynamic_slice_in_dim(blocks, (spot ^ flip) * rows, rows, 1)
        total = total + swapped(given, "wide", flip * low)
    return total


def quadrupled(blocks, w, low):
    held = [blocks] + [swapped(blocks, "wide", flip * low) for flip in (1, 2, 3)]
    spot = (w // low) % 4
    return jnp.concatenate(
        [lax.select_n(spot, *[held[at ^ mine] for mine in range(4)]) for at in range(4)], 1
    )


def own_rows(blocks, n, bit):
    wide, narrow = lax.axis_size("wide"), lax.axis_size("narrow")
    spots = [list(row_spots(m, narrow).values()) for m in range(narrow)]

    def of(m):
        picked = [jnp.concatenate([blocks[k : k + 1] for k in row]) for row in spots]
        return lax.select_n(m, *picked)

    total = of(n)
    for s in range(narrow):
        given = of((n + s) % narrow)
        for flip in (0, bit):
            if s or flip:
                steps = [
                    (w * narrow + m, (w ^ flip) * narrow + (m + s) % narrow)
                    for w in range(wide)
                    for m in range(narrow)
                ]
                total = total + lax.ppermute(given, ("wide", "narrow"), steps)
    return total


def row_of(full, m, narrow):
    held = {pair: k for k, pair in enumerate(row_spots(m, narrow))}
    for r in (0, 1):
        for c in range(2 * narrow):
            pair = (2 * m + r, c)
            yield r, c, full[held[pair]] if pair in held else full[held[c, 2 * m + r]].T


def assembled_kernel(narrow, mine, other, out):
    first = lax.rem(lax.axis_index("wide"), 2) == 0
    half = 2 * mine.shape[1]
    whole = jnp.concatenate(
        [jnp.where(first, mine[...], other[...]), jnp.where(first, other[...], mine[...])], 1
    )
    for m in range(narrow):

        @pl.when(lax.axis_index("narrow") == m)
        def _():
            for r, c, block in row_of(whole, m, narrow):
                out[r * half : (r + 1) * half, c * half : (c + 1) * half] = block


def assembled(mine, w, n, narrow):
    other = swapped(mine, "wide", 1)
    half = 2 * mine.shape[1]
    if half % 128 == 0:
        return pl.pallas_call(
            functools.partial(assembled_kernel, narrow),
            out_shape=like(2 * half, 2 * half * narrow, jnp.float32),
            in_specs=in_vmem(2),
            out_specs=in_vmem(1)[0],
            compiler_params=limit(8),
            name="assembled",
        )(mine, other)
    first = w % 2 == 0
    whole = jnp.concatenate([jnp.where(first, mine, other), jnp.where(first, other, mine)], 1)
    rows = []
    for m in range(narrow):
        blocks = [block for *_, block in row_of(whole, m, narrow)]
        spans = blocks[: 2 * narrow], blocks[2 * narrow :]
        rows.append(jnp.concatenate([jnp.concatenate(span, 1) for span in spans], 0))
    return lax.select_n(n, *rows)


def on_device(raw_ints, metric, occ_energy, vir_energy, pair_kept):
    wide, narrow = lax.axis_size("wide"), lax.axis_size("narrow")
    w, n = lax.axis_index("wide"), lax.axis_index("narrow")
    v = raw_ints.shape[1]
    virtuals = v * narrow

    near = 4
    chunks = [(0, v // 2), (v // 2, v // 2)]
    rows = metric.shape[0] // near
    piece = lax.dynamic_slice_in_dim(metric, (w % near) * rows, rows, 0)
    far = [passed_along(piece, "narrow", s) for s in range(1, narrow)]
    own = lax.dynamic_index_in_dim(raw_ints, n, 0, keepdims=False)
    raw_low = [passed_along(own, "wide", 1)]
    arrived, given = [], []
    for s in range(1, narrow):
        block = lax.dynamic_index_in_dim(raw_ints, (n + s) % narrow, 0, keepdims=False)
        parts = [block[first : first + rows] for first, rows in chunks]
        arrived += [passed_along(one, "narrow", s) for one in reversed(parts)][::-1]
        given += parts
    *fit_near, occ, kept = near_fit(after(own, *given), metric, occ_energy, pair_kept, piece)
    low_occ = passed_along(occ, "wide", 1)
    far = [after(one, fit_near[0]) for one in far]
    far_x = [swapped(one, "wide", 2) for one in far]
    far_core = [swapped(one, "wide", 1) for one in far]
    raw_low += [passed_along(one, "wide", 1) for one in arrived[:-1]]
    far_x = [after(one, raw_low[0], low_occ, arrived[0]) for one in far_x]
    far_last = [swapped(one, "wide", 1) for one in far_x]

    *own_turned, far_high, far_low = turn_own(own, fit_near, far + far_core + far_x + far_last)
    raw_low.append(passed_along(after(arrived[-1], *far_last), "wide", 1))
    turned = [*own_turned, *turn(arrived, fit_near[2:], (far_high, far_low))]

    form = tail if v % 128 == 0 else tail_plain
    energies = occ, low_occ, kept, vir_energy
    blocks, own_value = form(turned, raw_low, energies, v, 0.0625 / (wide * narrow))
    blocks, own_value, w, n = lax.optimization_barrier((blocks, own_value, w, n))
    own_value = own_value.reshape(1)
    upper_value = passed_along(own_value, "wide", -1)

    first, *bits, last = [1 << k for k in range(wide.bit_length() - 1)]
    low, bits = bits[0], bits[2:]
    blocks = halved(blocks, w, first)
    blocks = quartered(blocks, w, low)
    for bit in bits:
        blocks = halved(blocks, w, bit)
    full = own_rows(blocks, n, last)
    full, upper_value = lax.optimization_barrier((full, upper_value))
    for bit in reversed(bits):
        full = doubled(full, w, bit)
    full = quadrupled(full, w, low)
    return assembled(full, w, n, narrow), own_value + upper_value


def solution(mesh):
    placed = (
        P("wide", "narrow", None),
        P("narrow", None),
        P(("wide", "narrow")),
        P(),
        P(("wide", "narrow")),
    )
    return jax.shard_map(
        on_device,
        mesh=mesh,
        in_specs=placed,
        out_specs=(P("narrow", None), P(("wide", "narrow"))),
        check_vma=False,
    )
```

```python
import functools

import jax
import jax.numpy as jnp
from jax import lax
from jax.experimental import pallas as pl
from jax.experimental.pallas import tpu as pltpu
from jax.sharding import PartitionSpec as P

PASSES = lax.Precision.HIGH
VMEM = pltpu.MemorySpace.VMEM
NEAR_COST = 15_000_000_000


def contract(left, right, left_dim, right_dim):
    return lax.dot_general(
        left,
        right,
        (((left_dim,), (right_dim,)), ((), ())),
        precision=PASSES,
        preferred_element_type=jnp.float32,
    )


def passed_along(shard, axis, by):
    size = lax.axis_size(axis)
    return lax.ppermute(shard, axis, [(i, (i + by) % size) for i in range(size)])


def swapped(shard, axis, bit):
    size = lax.axis_size(axis)
    return lax.ppermute(shard, axis, [(i, i ^ bit) for i in range(size)])


def after(value, *gates):
    return lax.optimization_barrier((value,) + gates)[0]


def in_vmem(count):
    return [pl.BlockSpec(memory_space=VMEM)] * count


def limit(mib):
    return pltpu.CompilerParams(vmem_limit_bytes=mib * 2**20)


def cost(flops):
    return pl.CostEstimate(flops=flops, bytes_accessed=0, transcendentals=0)


def halves(value):
    high = value.astype(jnp.bfloat16)
    low = (value - high.astype(jnp.float32)).astype(jnp.bfloat16)
    return high, low


def dot3(left, right, right_dim):
    (lh, ll), (rh, rl) = left, right
    dims = (((1,), (right_dim,)), ((), ()))
    total = lax.dot_general(ll, rh, dims, preferred_element_type=jnp.float32)
    total += lax.dot_general(lh, rl, dims, preferred_element_type=jnp.float32)
    return total + lax.dot_general(lh, rh, dims, preferred_element_type=jnp.float32)


def stacked(refs):
    return jnp.concatenate([one[...] for one in refs], 0)


def like(rows, width, dtype):
    return jax.ShapeDtypeStruct((rows, width), dtype)


def near_fit_kernel(rows, metric, occ, kept, _, fit_high, fit_low, high, low, occ_tile, kept_tile):
    parts = halves(metric[...])
    high[...], low[...] = parts
    fit_high[...], fit_low[...] = halves(dot3(halves(rows[...]), parts, 1))
    occ_tile[...] = jnp.broadcast_to(occ[...], occ_tile.shape)
    kept_tile[...] = jnp.broadcast_to(kept[...].astype(jnp.float32), kept_tile.shape)


def near_fit(rows, metric, occ, kept, piece):
    (count, width), near = rows.shape, metric.shape[0]
    return pl.pallas_call(
        near_fit_kernel,
        out_shape=[like(count, near, jnp.bfloat16)] * 2
        + [like(near, width, jnp.bfloat16)] * 2
        + [like(8, 128, jnp.float32)] * 2,
        in_specs=in_vmem(5),
        out_specs=in_vmem(6),
        compiler_params=limit(16),
        cost_estimate=cost(NEAR_COST),
        name="near_fit",
    )(rows, metric, occ[None, :], kept[None, :], piece)


def turn_own_kernel(rows, fit_high, fit_low, near_high, near_low, *refs):
    pieces, (out_high, out_low, high, low) = refs[:-4], refs[-4:]
    parts = halves(stacked(pieces))
    high[...], low[...] = parts
    fit = halves(dot3(halves(rows[...]), parts, 1))
    total = dot3(fit, parts, 0)
    total += dot3((fit_high[...], fit_low[...]), (near_high[...], near_low[...]), 0)
    out_high[...], out_low[...] = halves(total)


def turn_own(rows, near, pieces):
    (count, width), far = rows.shape, sum(piece.shape[0] for piece in pieces)
    return pl.pallas_call(
        turn_own_kernel,
        out_shape=[like(count, width, jnp.bfloat16)] * 2 + [like(far, width, jnp.bfloat16)] * 2,
        in_specs=in_vmem(5 + len(pieces)),
        out_specs=in_vmem(4),
        compiler_params=limit(20),
        cost_estimate=cost(12 * count * far * width),
        name="turn_own",
    )(rows, *near, *pieces)


def turn_kernel(near_high, near_low, far_high, far_low, *refs):
    cuts, (out_high, out_low) = refs[:-2], refs[-2:]
    rows = halves(stacked(cuts))
    total = 0
    for parts in ((near_high[...], near_low[...]), (far_high[...], far_low[...])):
        total += dot3(halves(dot3(rows, parts, 1)), parts, 0)
    out_high[...], out_low[...] = halves(total)


def turn(cuts, near, far):
    count, width = sum(one.shape[0] for one in cuts), cuts[0].shape[1]
    return pl.pallas_call(
        turn_kernel,
        out_shape=[like(count, width, jnp.bfloat16)] * 2,
        in_specs=in_vmem(4 + len(cuts)),
        out_specs=in_vmem(2),
        compiler_params=limit(20),
        cost_estimate=cost(12 * count * width * (near[0].shape[0] + far[0].shape[0])),
        name="turn",
    )(*near, *far, *cuts)


def spots_of(tiles):
    pairs = []
    for a in range(tiles):
        for b in range(a, tiles):
            halves_of = [(2 * a + r, 2 * b + c) for r in (0, 1) for c in (0, 1)]
            pairs += [pair for pair in halves_of if pair[0] <= pair[1]]
    return {pair: k for k, pair in enumerate(pairs)}


def row_spots(n, tiles):
    spots = spots_of(tiles)
    return {pair: k for pair, k in spots.items() if pair[0] // 2 == n or pair[1] // 2 == n}


def tail_kernel(v, tiles, scale, occ, low_occ, kept, vir, own_high, own_low, far_high, far_low, *refs):
    lows, (blocks, value), scratch = refs[:-8], refs[-8:-6], refs[-6:]
    amp, amp_t, high, low, high_t, low_t = scratch
    n = lax.axis_index("narrow")
    virtuals = v * tiles
    at = [pl.ds(pl.multiple_of(lax.rem(n - a + tiles, tiles) * v, v), v) for a in range(tiles)]
    row = jnp.concatenate([vir[:, one] for one in at], 1)
    col = jnp.broadcast_to(row, (128, virtuals)).T[:, :1]
    gap = occ[:1, :1] + low_occ[:1, :1]
    weight = kept[:1, :1]
    right = halves(stacked(lows))
    left = (own_high[...], own_low[...]), (far_high[...], far_low[...])
    pairs = [dot3(one, right, 1) for one in left]
    spans = slice(0, v), slice(v, virtuals)
    for pair, span in zip(pairs, spans):
        amp[span, :] = pair / (col[span, :] + row - gap)
    amp_t[...] = amp[...].T
    total = jnp.float32(0)
    for pair, span in zip(pairs, spans):
        total += jnp.sum(pair * (2.0 * amp[span, :] - amp_t[span, :]))
    value[...] = -weight * total / (virtuals * virtuals)
    high[...], low[...] = halves(amp[...])
    high_t[...], low_t[...] = halves(amp_t[...])
    spots, half = spots_of(tiles), v // 2
    for a in range(tiles):
        for b in range(a, tiles):
            block = dot3((high[at[a], :], low[at[a], :]), (high_t[:, at[b]], low_t[:, at[b]]), 0)
            block += dot3((high_t[at[a], :], low_t[at[a], :]), (high[:, at[b]], low[:, at[b]]), 0)
            block *= weight * scale
            for r in (0, 1):
                for c in (0, 1):
                    k = spots.get((2 * a + r, 2 * b + c))
                    if k is not None:
                        blocks[k] = block[r * half : (r + 1) * half, c * half : (c + 1) * half]


def tail(turned, raw_low, energies, v, scale):
    virtuals, width = energies[-1].shape[0], raw_low[0].shape[1]
    tiles = virtuals // v
    count = len(spots_of(tiles))
    square = [pltpu.VMEM((virtuals, virtuals), kind) for kind in (jnp.float32, jnp.bfloat16)]
    return pl.pallas_call(
        functools.partial(tail_kernel, v, tiles, scale),
        out_shape=[
            jax.ShapeDtypeStruct((count, v // 2, v // 2), jnp.float32),
            jax.ShapeDtypeStruct((1, 1), jnp.float32),
        ],
        in_specs=in_vmem(8 + len(raw_low)),
        out_specs=in_vmem(2),
        scratch_shapes=[square[0]] * 2 + [square[1]] * 4,
        compiler_params=limit(24),
        cost_estimate=cost(6 * virtuals * virtuals * width + 3 * count * v * v * virtuals),
        name="tail",
    )(*energies[:-1], energies[-1][None, :], *turned, *raw_low)


def tail_plain(turned, raw_low, energies, v, scale):
    occ, low_occ, kept, vir = energies
    virtuals = vir.shape[0]
    narrow = virtuals // v
    order = ((lax.axis_index("narrow") - jnp.arange(narrow)) % narrow * v)[:, None] + jnp.arange(v)[None, :]
    order = order.reshape(virtuals)
    weight = kept[0, 0]
    levels = vir[order]
    own_high, own_low, far_high, far_low = [one.astype(jnp.float32) for one in turned]
    left = jnp.concatenate([own_high + own_low, far_high + far_low], 0)
    pair_ints = contract(left, jnp.concatenate(raw_low, 0), 1, 1)
    amplitude = pair_ints / (levels[:, None] + levels[None, :] - occ[0, 0] - low_occ[0, 0])
    value = jnp.sum(pair_ints * (2.0 * amplitude - amplitude.T)) * -weight / (virtuals * virtuals)
    amplitude = amplitude[order][:, order]
    blocks, half = [], v // 2
    for at in range(0, virtuals, half):
        row = contract(amplitude[at : at + half], amplitude[at:], 1, 1)
        row = row + contract(amplitude[:, at : at + half], amplitude[:, at:], 0, 0)
        blocks += jnp.split(row * (weight * scale), (virtuals - at) // half, 1)
    return jnp.stack(blocks), value.reshape(1, 1)


def halved(blocks, w, bit):
    half = blocks.shape[1] // 2
    side = (w // bit) % 2
    kept = lax.dynamic_slice_in_dim(blocks, side * half, half, 1)
    given = lax.dynamic_slice_in_dim(blocks, (1 - side) * half, half, 1)
    return kept + swapped(given, "wide", bit)


def doubled(blocks, w, bit):
    other = swapped(blocks, "wide", bit)
    low = (w // bit) % 2 == 0
    return jnp.concatenate([jnp.where(low, blocks, other), jnp.where(low, other, blocks)], 1)


def quartered(blocks, w, low):
    rows, spot = blocks.shape[1] // 4, (w // low) % 4
    total = lax.dynamic_slice_in_dim(blocks, spot * rows, rows, 1)
    for flip in (1, 2, 3):
        given = lax.dynamic_slice_in_dim(blocks, (spot ^ flip) * rows, rows, 1)
        total = total + swapped(given, "wide", flip * low)
    return total


def quadrupled(blocks, w, low):
    held = [blocks] + [swapped(blocks, "wide", flip * low) for flip in (1, 2, 3)]
    spot = (w // low) % 4
    return jnp.concatenate(
        [lax.select_n(spot, *[held[at ^ mine] for mine in range(4)]) for at in range(4)], 1
    )


def own_rows(blocks, n, bit):
    wide, narrow = lax.axis_size("wide"), lax.axis_size("narrow")
    spots = [list(row_spots(m, narrow).values()) for m in range(narrow)]

    def of(m):
        picked = [jnp.concatenate([blocks[k : k + 1] for k in row]) for row in spots]
        return lax.select_n(m, *picked)

    total = of(n)
    for s in range(narrow):
        given = of((n + s) % narrow)
        for flip in (0, bit):
            if s or flip:
                steps = [
                    (w * narrow + m, (w ^ flip) * narrow + (m + s) % narrow)
                    for w in range(wide)
                    for m in range(narrow)
                ]
                total = total + lax.ppermute(given, ("wide", "narrow"), steps)
    return total


def row_of(full, m, narrow):
    held = {pair: k for k, pair in enumerate(row_spots(m, narrow))}
    for r in (0, 1):
        for c in range(2 * narrow):
            pair = (2 * m + r, c)
            yield r, c, full[held[pair]] if pair in held else full[held[c, 2 * m + r]].T


def assembled_kernel(narrow, mine, other, out):
    first = lax.rem(lax.axis_index("wide"), 2) == 0
    half = 2 * mine.shape[1]
    whole = jnp.concatenate(
        [jnp.where(first, mine[...], other[...]), jnp.where(first, other[...], mine[...])], 1
    )
    for m in range(narrow):

        @pl.when(lax.axis_index("narrow") == m)
        def _():
            for r, c, block in row_of(whole, m, narrow):
                out[r * half : (r + 1) * half, c * half : (c + 1) * half] = block


def assembled(mine, w, n, narrow):
    other = swapped(mine, "wide", 1)
    half = 2 * mine.shape[1]
    if half % 128 == 0:
        return pl.pallas_call(
            functools.partial(assembled_kernel, narrow),
            out_shape=like(2 * half, 2 * half * narrow, jnp.float32),
            in_specs=in_vmem(2),
            out_specs=in_vmem(1)[0],
            compiler_params=limit(8),
            name="assembled",
        )(mine, other)
    first = w % 2 == 0
    whole = jnp.concatenate([jnp.where(first, mine, other), jnp.where(first, other, mine)], 1)
    rows = []
    for m in range(narrow):
        blocks = [block for *_, block in row_of(whole, m, narrow)]
        spans = blocks[: 2 * narrow], blocks[2 * narrow :]
        rows.append(jnp.concatenate([jnp.concatenate(span, 1) for span in spans], 0))
    return lax.select_n(n, *rows)


def on_device(raw_ints, metric, occ_energy, vir_energy, pair_kept):
    wide, narrow = lax.axis_size("wide"), lax.axis_size("narrow")
    w, n = lax.axis_index("wide"), lax.axis_index("narrow")
    v = raw_ints.shape[1]
    virtuals = v * narrow

    near = 4
    chunks = [(0, v // 2), (v // 2, v // 2)]
    rows = metric.shape[0] // near
    piece = lax.dynamic_slice_in_dim(metric, (w % near) * rows, rows, 0)
    far = [passed_along(piece, "narrow", s) for s in range(1, narrow)]
    own = lax.dynamic_index_in_dim(raw_ints, n, 0, keepdims=False)
    raw_low = [passed_along(own, "wide", 1)]
    arrived, given = [], []
    for s in range(1, narrow):
        block = lax.dynamic_index_in_dim(raw_ints, (n + s) % narrow, 0, keepdims=False)
        parts = [block[first : first + rows] for first, rows in chunks]
        arrived += [passed_along(one, "narrow", s) for one in reversed(parts)][::-1]
        given += parts
    *fit_near, occ, kept = near_fit(after(own, *given), metric, occ_energy, pair_kept, piece)
    low_occ = passed_along(occ, "wide", 1)
    far = [after(one, fit_near[0]) for one in far]
    far_x = [swapped(one, "wide", 2) for one in far]
    far_core = [swapped(one, "wide", 1) for one in far]
    raw_low += [passed_along(one, "wide", 1) for one in arrived[:-1]]
    far_x = [after(one, raw_low[0], low_occ, arrived[0]) for one in far_x]
    far_last = [swapped(one, "wide", 1) for one in far_x]

    *own_turned, far_high, far_low = turn_own(own, fit_near, far + far_core + far_x + far_last)
    raw_low.append(passed_along(after(arrived[-1], own_turned[0]), "wide", 1))
    turned = [*own_turned, *turn(arrived, fit_near[2:], (far_high, far_low))]

    form = tail if v % 128 == 0 else tail_plain
    energies = occ, low_occ, kept, vir_energy
    blocks, own_value = form(turned, raw_low, energies, v, 0.0625 / (wide * narrow))
    blocks, own_value, w, n = lax.optimization_barrier((blocks, own_value, w, n))
    own_value = own_value.reshape(1)
    upper_value = passed_along(own_value, "wide", -1)

    first, *bits, last = [1 << k for k in range(wide.bit_length() - 1)]
    low, bits = bits[0], bits[2:]
    blocks = halved(blocks, w, first)
    blocks = quartered(blocks, w, low)
    for bit in bits:
        blocks = halved(blocks, w, bit)
    full = own_rows(blocks, n, last)
    full, upper_value = lax.optimization_barrier((full, upper_value))
    for bit in reversed(bits):
        full = doubled(full, w, bit)
    full = quadrupled(full, w, low)
    return assembled(full, w, n, narrow), own_value + upper_value


def solution(mesh):
    placed = (
        P("wide", "narrow", None),
        P("narrow", None),
        P(("wide", "narrow")),
        P(),
        P(("wide", "narrow")),
    )
    return jax.shard_map(
        on_device,
        mesh=mesh,
        in_specs=placed,
        out_specs=(P("narrow", None), P(("wide", "narrow"))),
        check_vma=False,
    )
```
